32 devices in a mesh: row: 4 (over y, x), col: 8 (over z, core).
Axes of the slice: x: 2, y: 2, z: 4, core: 2. Of those that a mesh axis runs over, the one named last changes fastest.
Arguments:
- galaxy: float32 [128, 256, 256], P('row', 'col'), may hold values from 0.03 to 32, as said below
- randoms: float32 [128, 256, 256], P('row', 'col'), may hold values from 0.5 to 4
- coverage: int32 [128, 256, 256], P('row', 'col'), may hold values from 0 to 1
- patch: int32 [128, 256, 256], P('row', 'col'), may hold values from 0 to 127
Outputs:
- contrast: float32 [128, 256, 256], P('row', 'col')
- patch_sums: float32 [4, 128], replicated
The draws below stay inside these ranges and needn't reach their ends.
Inputs may be any that keep to these rules, and one draw needn't show every extreme that they name: `galaxy`: positive densities.
All inputs are finite; a program needn't handle non-finite values.
Results may differ from the reference program's by a relative error of at most 0.00016.
Values sent between devices are 32-bit elements; how exact they have to be, the bound alone decides.
A program may use at most 64 MiB of HBM per device.

```python
import math
import jax
import jax.numpy as jnp

NZ = 256
RADIUS = 16
NPATCH = 128
NX = 128
NY = 256


def line_factor(key, count):
    logs = jax.random.uniform(key, (count,), jnp.float32, jnp.log(0.4), jnp.log(2.5))
    return jnp.exp(logs)


def draw_galaxy(key, part):
    keys = jax.random.split(jax.random.fold_in(key, 11), 4)
    base_logs = jax.random.uniform(keys[0], (NX, NY, NZ), jnp.float32, jnp.log(0.5), jnp.log(2.0))
    base = jnp.exp(base_logs)
    along_x = line_factor(keys[1], NX)[:, None, None]
    along_y = line_factor(keys[2], NY)[None, :, None]
    along_z = line_factor(keys[3], NZ)[None, None, :]
    return (base * along_x * along_y * along_z).astype(jnp.float32)


def draw_coverage(key, part):
    keys = jax.random.split(key, 4)
    centre_x = jax.random.randint(keys[0], (), NX // 4, 3 * NX // 4 + 1)
    centre_y = jax.random.randint(keys[1], (), NY // 4, 3 * NY // 4 + 1)
    radius = jax.random.randint(keys[2], (), 200, 350)
    xpos = jnp.arange(NX, dtype=jnp.int32)[:, None, None]
    ypos = jnp.arange(NY, dtype=jnp.int32)[None, :, None]
    upos = (xpos - centre_x) * 1024 // NX
    vpos = (ypos - centre_y) * 1024 // NY
    outside = upos * upos + vpos * vpos >= radius * radius
    holes = jax.random.randint(keys[3], (NX, NY, NZ), 0, 8) > 0
    return (outside & holes).astype(jnp.int32)


def draw_patch(key, part):
    keys = jax.random.split(key, 4)
    shift_x = jax.random.randint(keys[0], (), 0, NX)
    shift_y = jax.random.randint(keys[1], (), 0, NY)
    xpos = (jnp.arange(NX, dtype=jnp.int32) + shift_x) % NX
    ypos = (jnp.arange(NY, dtype=jnp.int32) + shift_y) % NY
    tile = xpos[:, None] // (NX // 8) * (NPATCH // 8) + ypos[None, :] // (NY // 16) * (NPATCH // 128)
    tile = jnp.broadcast_to(tile[:, :, None], (NX, NY, NZ))
    spread = jax.random.randint(keys[2], (NX, NY, NZ), 0, NPATCH)
    relabel = jax.random.randint(keys[3], (NX, NY, NZ), 0, 8) == 0
    return jnp.where(relabel, spread, tile).astype(jnp.int32)


def level_of(key, extent, pieces, smallest, top_value):
    def one(axis_at, shards_of):
        steps = jax.random.uniform(jax.random.fold_in(jax.random.fold_in(key, 6), axis_at), (shards_of,), jnp.float32, smallest / len(pieces), top_value / len(pieces))
        return jnp.repeat(jnp.exp(steps), extent[axis_at] // shards_of).reshape((-1,) + (1,) * (len(extent) - axis_at - 1))

    factor_of = one(*pieces[0])
    for cut in pieces[1:]:
        factor_of = factor_of * one(*cut)
    return factor_of


def setup_inputs(seed: int = 0) -> dict:
    key_of = jax.random.split(jax.random.key(seed), 5)
    galaxy = draw_galaxy(jax.random.fold_in(key_of[4], 71), 0)
    randoms = jnp.clip(jnp.exp(math.log(4.0) - 2.0794415 * jax.random.uniform(key_of[1], (NX, NY, NZ), jnp.float32) ** level_of(key_of[1], (NX, NY, NZ), ((0, 4), (1, 8)), -0.2, 0.2)), 0.5, 4.0)
    coverage = draw_coverage(jax.random.fold_in(key_of[4], 71), 0)
    patch = draw_patch(jax.random.fold_in(key_of[4], 71), 0)
    return {"galaxy": galaxy, "randoms": randoms, "coverage": coverage, "patch": patch}


def kernel_taps():
    offs = jnp.arange(-RADIUS, RADIUS + 1).astype(jnp.float32)
    sigma = RADIUS / 2.0
    vals = jnp.exp(-offs * offs / (2.0 * sigma * sigma))
    return vals / jnp.sum(vals)


def smooth_axis(field, taps, axis):
    width = [(0, 0)] * field.ndim
    width[axis] = (RADIUS, RADIUS)
    padded = jnp.pad(field, width)
    count = field.shape[axis]
    total = jnp.zeros_like(field)
    for j in range(2 * RADIUS + 1):
        total = total + taps[j] * lax_slice(padded, j, count, axis)
    return total


def lax_slice(padded, start, count, axis):
    return jax.lax.slice_in_dim(padded, start, start + count, axis=axis)


def reference(galaxy, randoms, coverage, patch):
    taps = kernel_taps()

    def smooth(field):
        return smooth_axis(smooth_axis(smooth_axis(field, taps, 2), taps, 0), taps, 1)

    gal_s = smooth(galaxy)
    ran_s = smooth(randoms)
    weightm = coverage.astype(jnp.float32)
    alpha = jnp.sum(weightm * galaxy) / jnp.sum(weightm * randoms)
    nbar = alpha * ran_s
    weight = 1.0 / (1.0 + 2.0 * nbar)
    contrast = weightm * weight * (gal_s / nbar - 1.0)
    flat_m = weightm.reshape(-1)
    flat_c = contrast.reshape(-1)
    powers = jnp.stack([flat_m, flat_m * flat_c, flat_m * flat_c * flat_c, flat_m * flat_c * flat_c * flat_c], axis=1)
    sums = jax.ops.segment_sum(powers, patch.reshape(-1), num_segments=NPATCH)
    scale = NPATCH / (NX * NY * NZ)
    return contrast, (sums.T * scale).astype(jnp.float32)
```

```python
import functools

import jax
import jax.numpy as jnp
import ml_dtypes
import numpy as np
from jax import lax
from jax.experimental import pallas as pl
from jax.experimental.pallas import tpu as pltpu
from jax.sharding import PartitionSpec as P

RADIUS = 16
NPATCH = 128
LANES = 128
GROUP = 4
F32 = jnp.float32
BF16 = jnp.bfloat16
MESH = pl.DeviceIdType.MESH


def taps_np():
    offs = np.arange(-RADIUS, RADIUS + 1).astype(np.float32)
    sigma = RADIUS / 2.0
    vals = np.exp(-offs * offs / np.float32(2.0 * sigma * sigma)).astype(np.float32)
    return (vals / vals.sum(dtype=np.float32)).astype(np.float32)


def split_np(mat):
    high = mat.astype(ml_dtypes.bfloat16)
    low = (mat - high.astype(np.float32)).astype(ml_dtypes.bfloat16)
    return high, low


def band(outs, ins, shift):
    taps = taps_np()
    mat = np.zeros((outs, ins), np.float32)
    for o in range(outs):
        for j in range(-RADIUS, RADIUS + 1):
            i = o + j + shift
            if 0 <= i < ins:
                mat[o, i] = taps[j + RADIUS]
    return mat


def split(val):
    high = val.astype(BF16)
    low = (val - high.astype(F32)).astype(BF16)
    return high, low


def dot(a, b):
    return jnp.dot(a, b, preferred_element_type=F32)


def gather_sum(axis, size, buf, send, recv):
    me = lax.axis_index(axis)
    copies = []
    for k in range(1, size):
        copy = pltpu.make_async_remote_copy(
            src_ref=buf.at[me],
            dst_ref=buf.at[me],
            send_sem=send.at[k - 1],
            recv_sem=recv.at[k - 1],
            device_id={axis: lax.rem(me + k, size)},
            device_id_type=MESH,
        )
        copy.start()
        copies.append(copy)
    return copies


def add_up(copies, buf, size):
    for copy in copies:
        copy.wait()
    total = buf[0]
    for k in range(1, size):
        total = total + buf[k]
    return total


def kernel(
    rows, cols, scale,
    *refs,
):
    hbm, (contrast, sums), vmem = refs[:11], refs[11:13], refs[13:24]
    (
        xb, yb, acc, trow, tcol, srow, scol, rb, oh, rh, sin,
        sx, rx, sy, ry, srel, rrel, s1, r1, s2, r2, s3, r3, s4, r4,
    ) = refs[24:]
    gal, ran, cov, pat, thi, tlo, kxhi, kxlo, kyhi, kylo, rep = vmem
    X, Y, Z = gal.shape
    W = RADIUS
    tiles = Y // 8
    me_r = lax.axis_index("row")
    me_c = lax.axis_index("col")

    PX = 8
    slabs = X // PX
    def fetch(k, slab=None):
        at = slice(None) if slab is None else pl.ds(slab * PX, PX)
        return pltpu.make_async_copy(
            hbm[k].at[at], vmem[k].at[at], sin.at[k, 0 if slab is None else slab]
        )

    fetch(4).start()
    fetch(5).start()
    for i in range(slabs):
        fetch(0, i).start()
        fetch(1, i).start()
    for k in (2, 3, 8, 9, 6, 7, 10):
        fetch(k).start()

    barrier = pltpu.get_barrier_semaphore()
    for k in range(1, rows):
        pl.semaphore_signal(barrier, inc=1, device_id={"row": lax.rem(me_r + k, rows)}, device_id_type=MESH)
    for k in range(1, cols):
        pl.semaphore_signal(barrier, inc=1, device_id={"col": lax.rem(me_c + k, cols)}, device_id_type=MESH)
    fetch(4).wait()
    fetch(5).wait()

    relayed = rows == 4
    detour = tiles // 2 if relayed else 0

    def xsrc(h, up, t):
        return xb.at[h, :, pl.ds(X if up else W, W), pl.ds(t * 8, 8)]

    def xdst(h, up, t):
        return xb.at[h, :, pl.ds(0 if up else X + W, W), pl.ds(t * 8, 8)]

    def xsend(src, dst, ssem, rsem, hop):
        return pltpu.make_async_remote_copy(
            src_ref=src, dst_ref=dst, send_sem=ssem, recv_sem=rsem,
            device_id={"row": lax.rem(me_r + (hop + rows), rows)}, device_id_type=MESH,
        )

    def xcopy(h, up, t):
        u = int(up)
        return xsend(xsrc(h, up, t), xdst(h, up, t), sx.at[h, u, t], rx.at[h, u, t], 1 if up else -1)

    def xfirst(h, up, t):
        return xsend(xsrc(h, up, t), rb.at[h, t], sx.at[h, int(up), t], rrel.at[h, t], 2 if up else -2)

    def xsecond(h, up, t):
        return xsend(rb.at[h, t], xdst(h, up, t), srel.at[h, t], rx.at[h, int(up), t], -1 if up else 1)

    def xeach(h, t, act):
        for up in (False, True):
            has = me_r < rows - 1 if up else me_r > 0
            if t < detour:
                turn = me_r == (1 if up else 2)

                @pl.when(turn)
                def _():
                    act(xfirst(h, up, t))

                has = jnp.logical_and(has, jnp.logical_not(turn))

            @pl.when(has)
            def _():
                act(xcopy(h, up, t))

    def relay(h, t, act):
        if t < detour:
            for up in (False, True):
                @pl.when(me_r == (3 if up else 0))
                def _():
                    act(up)

    def relay_on(h, t):
        def go(up):
            xfirst(h, up, t).wait_recv()
            xsecond(h, up, t).start()

        relay(h, t, go)

    def xarrived(h, t):
        @pl.when(me_r > 0)
        def _():
            xcopy(h, True, t).wait_recv()

        @pl.when(me_r < rows - 1)
        def _():
            xcopy(h, False, t).wait_recv()

    def ycopy(h, up):
        own, far = ((Y, 0) if up else (W, Y + W))
        return pltpu.make_async_remote_copy(
            src_ref=yb.at[h, :, :, pl.ds(own, W)],
            dst_ref=yb.at[h, :, :, pl.ds(far, W)],
            send_sem=sy.at[h, int(up)],
            recv_sem=ry.at[h, int(up)],
            device_id={"col": lax.rem(me_c + (1 if up else cols - 1), cols)},
            device_id_type=MESH,
        )

    def yeach(h, up, act):
        @pl.when(me_c < cols - 1 if up else me_c > 0)
        def _():
            act(ycopy(h, up))

    def yarrived(h):
        @pl.when(me_c > 0)
        def _():
            ycopy(h, True).wait_recv()

        @pl.when(me_c < cols - 1)
        def _():
            ycopy(h, False).wait_recv()

    def xstart(h, t):
        xeach(h, t, lambda copy: copy.start())

    for h in range(2):
        @pl.when(me_r == 0)
        def _():
            xb[h, :, 0:W] = jnp.zeros((2, W, Y, LANES), F32)

        @pl.when(me_r == rows - 1)
        def _():
            xb[h, :, X + W:] = jnp.zeros((2, W, Y, LANES), F32)

        @pl.when(me_c == 0)
        def _():
            yb[h, :, :, 0:W] = jnp.zeros((2, X, W, LANES), F32)

        @pl.when(me_c == cols - 1)
        def _():
            yb[h, :, :, Y + W:] = jnp.zeros((2, X, W, LANES), F32)

    for i in range(slabs):
        fetch(0, i).wait()
        fetch(1, i).wait()
        for f, ref in enumerate((gal, ran)):
            high, low = split(ref[pl.ds(i * PX, PX)].reshape(PX * Y, Z))
            val = dot(high, thi[...]) + dot(high, tlo[...]) + dot(low, thi[...])
            xb[0, f, pl.ds(W + i * PX, PX)] = val[:, :LANES].reshape(PX, Y, LANES)
            yb[1, f, pl.ds(i * PX, PX), pl.ds(W, Y)] = val[:, LANES:].reshape(PX, Y, LANES)

    pl.semaphore_wait(barrier, rows + cols - 2)
    for t in range(tiles):
        xstart(0, t)
    for up in (False, True):
        yeach(1, up, lambda copy: copy.start())

    for k in (2, 3):
        fetch(k).wait()

    def tstep(i, carry):
        m = cov[i].astype(F32)
        g = (m * gal[i]).reshape(Y // 8, 8, Z).sum(axis=0)
        r = (m * ran[i]).reshape(Y // 8, 8, Z).sum(axis=0)
        return carry[0] + g, carry[1] + r

    zero = jnp.zeros((8, Z), F32)
    tg, tr = lax.fori_loop(0, X, tstep, (zero, zero))
    for f, t in enumerate((tg, tr)):
        trow[me_r, f] = sum(t[:, k * LANES:(k + 1) * LANES] for k in range(Z // LANES))
    row_totals = gather_sum("row", rows, trow, s1, r1)

    acc[...] = jnp.zeros_like(acc)
    groups = X // 2 * tiles // GROUP

    def members(h, n):
        for k in range(GROUP):
            i = n * GROUP + k
            yield (i // tiles, i % tiles) if h == 0 else (i % (X // 2), i // (X // 2))

    def cells(ref, h, n):
        parts = []
        for lx, t in members(h, n):
            at = pl.ds(pl.multiple_of(t * 8, 8), 8), pl.ds(h * LANES, LANES)
            parts += [ref[(2 * lx, *at)], ref[(2 * lx + 1, *at)]]
        return jnp.concatenate(parts, axis=1)

    def onehots(h, first, last):
        def step(n, unused):
            p = jnp.where(cells(cov, h, n) > 0, cells(pat, h, n), -1)
            phi, plo = p >> 5, p & 31

            def rows_of(a, b):
                return jnp.concatenate([a, b], axis=0).astype(BF16)

            def one(v, k):
                return jnp.where(v == k, 1.0, 0.0)

            for k in range(4):
                hit = one(phi, k)
                oh[h, n, pl.ds(16 * k, 16)] = rows_of(hit, hit)
            for k in range(16):
                rh[h, n, pl.ds(16 * k, 16)] = rows_of(one(plo, 2 * k), one(plo, 2 * k + 1))
            return unused

        lax.fori_loop(first, last, step, 0)

    def histogram(h, first, last):
        def step(n, unused):
            c = cells(contrast, h, n)
            hot = oh[h, n]
            terms = [hot]
            power = c
            for q in range(3):
                high, low = split(power)
                both = jnp.concatenate([high.astype(F32), low.astype(F32)], axis=0).astype(BF16)
                terms.append(jnp.concatenate([both] * 4, axis=0) * hot)
                power = power * c
            acc[...] += lax.dot_general(
                rh[h, n], jnp.concatenate(terms, axis=0), (((1,), (1,)), ((), ())),
                preferred_element_type=F32,
            )
            return unused

        lax.fori_loop(first, last, step, 0)

    def ypass(h, i):
        both = jnp.concatenate(
            [yb[h, f, pl.ds(i * 4, 4)].reshape(4 * (Y + 2 * W), LANES) for f in range(2)], axis=1
        )
        high, low = split(both)
        kh = kyhi[...]
        return dot(kh, high) + dot(kylo[...], high) + dot(kh, low)

    def xpass(h, t):
        ys = pl.ds(t * 8, 8)
        both = jnp.concatenate(
            [xb[h, f, :, ys].reshape((X + 2 * W) * 8, LANES) for f in range(2)], axis=1
        )
        high, low = split(both)
        kh = kxhi[...]
        return dot(kh, high) + dot(kxlo[...], high) + dot(kh, low)

    def contrast_of(val, m, alpha):
        nbar = alpha * val[:, LANES:]
        weight = 1.0 / (1.0 + 2.0 * nbar)
        return m * weight * (val[:, :LANES] / nbar - 1.0)

    half = groups // 2
    onehots(0, 0, half)
    for k in (8, 9):
        fetch(k).wait()
    yarrived(1)

    def yown(i, unused):
        val = ypass(1, i)
        for f in range(2):
            xb[1, f, pl.ds(W + i * 4, 4)] = val[:, f * LANES:(f + 1) * LANES].reshape(4, Y, LANES)
        return unused

    lax.fori_loop(0, X // 4, yown, 0, unroll=2)
    for t in range(detour):
        relay_on(0, t)
    tcol[me_c] = add_up(row_totals, trow, rows)
    col_totals = gather_sum("col", cols, tcol, s2, r2)
    for t in range(tiles):
        xstart(1, t)
    onehots(0, half, groups)
    onehots(1, 0, groups)
    for t in range(detour):
        relay_on(1, t)
    tot = add_up(col_totals, tcol, cols)
    alpha = jnp.sum(tot[0], keepdims=True) / jnp.sum(tot[1], keepdims=True)
    for k in (6, 7, 10):
        fetch(k).wait()

    for t in range(tiles):
        xarrived(0, t)
        val = xpass(0, t)
        for f in range(2):
            yb[0, f, :, pl.ds(W + t * 8, 8)] = val[:, f * LANES:(f + 1) * LANES].reshape(X, 8, LANES)
        if t == W // 8 - 1:
            yeach(0, False, lambda copy: copy.start())
    yeach(0, True, lambda copy: copy.start())

    def last_of(h, t):
        lanes = pl.ds(h * LANES, LANES)
        xarrived(h, t)
        val = xpass(h, t)
        m = cov[:, pl.ds(t * 8, 8), lanes].astype(F32).reshape(X * 8, LANES)
        contrast[:, pl.ds(t * 8, 8), lanes] = contrast_of(val, m, alpha).reshape(X, 8, LANES)
        histogram(h, groups * t // tiles, groups * (t + 1) // tiles)

    def cstep(i, unused):
        val = ypass(0, i)
        x4, lanes = pl.ds(i * 4, 4), pl.ds(0, LANES)
        m = cov[x4, :, lanes].astype(F32).reshape(4 * Y, LANES)
        contrast[x4, :, lanes] = contrast_of(val, m, alpha).reshape(4, Y, LANES)
        return unused

    for t in range(tiles):
        if t == tiles // 2:
            yarrived(0)
            lax.fori_loop(0, X // 4, cstep, 0, unroll=2)
            histogram(0, 0, groups)
        last_of(1, t)

    a = acc[...]
    same = lax.broadcasted_iota(jnp.int32, a.shape, 0) % 8 == lax.broadcasted_iota(jnp.int32, a.shape, 1) % 8
    a = jnp.where(same, a, 0.0).reshape(32, 8, 256).sum(axis=1).T
    terms = []
    for q in range(4):
        for k in range(4):
            at = q * 64 + k * 16
            term = a[at:at + 8] if q == 0 else a[at:at + 8] + a[at + 8:at + 16]
            terms.append(jnp.sum(term, axis=0, keepdims=True))
    spread = jnp.dot(
        jnp.concatenate(terms, axis=0), rep[...],
        precision=lax.Precision.HIGHEST, preferred_element_type=F32,
    )
    own = lax.broadcasted_iota(jnp.int32, spread.shape, 1) // 32 == lax.broadcasted_iota(jnp.int32, spread.shape, 0) % 4
    spread = jnp.where(own, spread, 0.0)
    for q in range(4):
        srow[me_r, q:q + 1] = jnp.sum(spread[4 * q:4 * q + 4], axis=0, keepdims=True)
    srow[me_r, 4:8] = jnp.zeros((4, NPATCH), F32)
    scol[me_c] = add_up(gather_sum("row", rows, srow, s3, r3), srow, rows)
    whole = add_up(gather_sum("col", cols, scol, s4, r4), scol, cols)
    sums[...] = whole[0:4] * scale

    for h in range(2):
        for t in range(tiles):
            xeach(h, t, lambda copy: copy.wait_send())
            relay(h, t, lambda up: xsecond(h, up, t).wait_send())
        for up in (False, True):
            yeach(h, up, lambda copy: copy.wait_send())


def local(galaxy, randoms, coverage, patch):
    rows, cols = lax.axis_size("row"), lax.axis_size("col")
    X, Y, Z = galaxy.shape
    W = RADIUS
    tiles = Y // 8
    groups = X // 2 * tiles // GROUP
    scale = NPATCH / (X * rows * Y * cols * Z)
    tz = split_np(band(Z, Z, 0).T)
    kx = split_np(np.kron(band(X, X + 2 * W, W), np.eye(8, dtype=np.float32)))
    ky = split_np(np.kron(np.eye(4, dtype=np.float32), band(Y, Y + 2 * W, W)))
    rep = (np.arange(NPATCH)[None, :] % 32 == np.arange(32)[:, None]).astype(np.float32)
    consts = [jnp.asarray(v) for v in (*tz, *kx, *ky, rep)]
    args = (galaxy, randoms, coverage, patch, *consts)
    vmem = pl.BlockSpec(memory_space=pltpu.VMEM)
    dma = pltpu.SemaphoreType.DMA
    contrast, sums = pl.pallas_call(
        functools.partial(kernel, rows, cols, scale),
        out_shape=(
            pltpu.VMEM((X, Y, Z), F32),
            pltpu.VMEM((4, NPATCH), F32),
        ),
        in_specs=[pl.BlockSpec(memory_space=pl.ANY)] * 11,
        out_specs=(vmem, vmem),
        scratch_shapes=[pltpu.VMEM(v.shape, v.dtype) for v in args] + [
            pltpu.VMEM((2, 2, X + 2 * W, Y, LANES), F32),
            pltpu.VMEM((2, 2, X, Y + 2 * W, LANES), F32),
            pltpu.VMEM((256, 256), F32),
            pltpu.VMEM((rows, 2, 8, LANES), F32),
            pltpu.VMEM((cols, 2, 8, LANES), F32),
            pltpu.VMEM((rows, 8, NPATCH), F32),
            pltpu.VMEM((cols, 8, NPATCH), F32),
            pltpu.VMEM((2, tiles // 2, 2, W, 8, LANES), F32),
            pltpu.VMEM((2, groups, 64, 2 * LANES * GROUP), BF16),
            pltpu.VMEM((2, groups, 256, 2 * LANES * GROUP), BF16),
            dma((11, X // 8)),
            dma((2, 2, tiles)), dma((2, 2, tiles)), dma((2, 2)), dma((2, 2)),
            dma((2, tiles // 2)), dma((2, tiles // 2)),
            dma((rows - 1,)), dma((rows - 1,)), dma((cols - 1,)), dma((cols - 1,)),
            dma((rows - 1,)), dma((rows - 1,)), dma((cols - 1,)), dma((cols - 1,)),
        ],
        compiler_params=pltpu.CompilerParams(
            collective_id=0, has_side_effects=True, vmem_limit_bytes=56 * 1024 * 1024
        ),
    )(*args)
    return contrast, sums


def solution(mesh):
    spec = P("row", "col", None)
    return jax.shard_map(
        local, mesh=mesh, in_specs=(spec,) * 4, out_specs=(spec, P()), check_vma=False
    )
```

```python
import functools

import jax
import jax.numpy as jnp
import ml_dtypes
import numpy as np
from jax import lax
from jax.experimental import pallas as pl
from jax.experimental.pallas import tpu as pltpu
from jax.sharding import PartitionSpec as P

RADIUS = 16
NPATCH = 128
LANES = 128
GROUP = 16
F32 = jnp.float32
BF16 = jnp.bfloat16
MESH = pl.DeviceIdType.MESH


def taps_np():
    offs = np.arange(-RADIUS, RADIUS + 1).astype(np.float32)
    sigma = RADIUS / 2.0
    vals = np.exp(-offs * offs / np.float32(2.0 * sigma * sigma)).astype(np.float32)
    return (vals / vals.sum(dtype=np.float32)).astype(np.float32)


def split_np(mat):
    high = mat.astype(ml_dtypes.bfloat16)
    low = (mat - high.astype(np.float32)).astype(ml_dtypes.bfloat16)
    return high, low


def band(outs, ins, shift):
    taps = taps_np()
    mat = np.zeros((outs, ins), np.float32)
    for o in range(outs):
        for j in range(-RADIUS, RADIUS + 1):
            i = o + j + shift
            if 0 <= i < ins:
                mat[o, i] = taps[j + RADIUS]
    return mat


def split(val):
    high = val.astype(BF16)
    low = (val - high.astype(F32)).astype(BF16)
    return high, low


def dot(a, b):
    return jnp.dot(a, b, preferred_element_type=F32)


def gather_sum(axis, size, buf, send, recv):
    me = lax.axis_index(axis)
    copies = []
    for k in range(1, size):
        copy = pltpu.make_async_remote_copy(
            src_ref=buf.at[me],
            dst_ref=buf.at[me],
            send_sem=send.at[k - 1],
            recv_sem=recv.at[k - 1],
            device_id={axis: lax.rem(me + k, size)},
            device_id_type=MESH,
        )
        copy.start()
        copies.append(copy)
    return copies


def add_up(copies, buf, size):
    for copy in copies:
        copy.wait()
    total = buf[0]
    for k in range(1, size):
        total = total + buf[k]
    return total


def kernel(
    rows, cols, scale,
    *refs,
):
    hbm, (contrast, sums), vmem = refs[:11], refs[11:13], refs[13:24]
    (
        xb, yb, acc, trow, tcol, srow, scol, rb, oh, rh, sin,
        sx, rx, sy, ry, srel, rrel, s1, r1, s2, r2, s3, r3, s4, r4,
    ) = refs[24:]
    gal, ran, cov, pat, thi, tlo, kxhi, kxlo, kyhi, kylo, rep = vmem
    X, Y, Z = gal.shape
    W = RADIUS
    tiles = Y // 8
    me_r = lax.axis_index("row")
    me_c = lax.axis_index("col")

    PX = 8
    slabs = X // PX
    def fetch(k, slab=None):
        at = slice(None) if slab is None else pl.ds(slab * PX, PX)
        return pltpu.make_async_copy(
            hbm[k].at[at], vmem[k].at[at], sin.at[k, 0 if slab is None else slab]
        )

    fetch(4).start()
    fetch(5).start()
    for i in range(slabs):
        fetch(0, i).start()
        fetch(1, i).start()
    for k in (2, 3, 8, 9, 6, 7, 10):
        fetch(k).start()

    barrier = pltpu.get_barrier_semaphore()
    for k in range(1, rows):
        pl.semaphore_signal(barrier, inc=1, device_id={"row": lax.rem(me_r + k, rows)}, device_id_type=MESH)
    for k in range(1, cols):
        pl.semaphore_signal(barrier, inc=1, device_id={"col": lax.rem(me_c + k, cols)}, device_id_type=MESH)
    fetch(4).wait()
    fetch(5).wait()

    relayed = rows == 4
    detour = tiles // 2 if relayed else 0

    def xsrc(h, up, t):
        return xb.at[h, :, pl.ds(X if up else W, W), pl.ds(t * 8, 8)]

    def xdst(h, up, t):
        return xb.at[h, :, pl.ds(0 if up else X + W, W), pl.ds(t * 8, 8)]

    def xsend(src, dst, ssem, rsem, hop):
        return pltpu.make_async_remote_copy(
            src_ref=src, dst_ref=dst, send_sem=ssem, recv_sem=rsem,
            device_id={"row": lax.rem(me_r + (hop + rows), rows)}, device_id_type=MESH,
        )

    def xcopy(h, up, t):
        u = int(up)
        return xsend(xsrc(h, up, t), xdst(h, up, t), sx.at[h, u, t], rx.at[h, u, t], 1 if up else -1)

    def xfirst(h, up, t):
        return xsend(xsrc(h, up, t), rb.at[h, t], sx.at[h, int(up), t], rrel.at[h, t], 2 if up else -2)

    def xsecond(h, up, t):
        return xsend(rb.at[h, t], xdst(h, up, t), srel.at[h, t], rx.at[h, int(up), t], -1 if up else 1)

    def xeach(h, t, act):
        for up in (False, True):
            has = me_r < rows - 1 if up else me_r > 0
            if t < detour:
                turn = me_r == (1 if up else 2)

                @pl.when(turn)
                def _():
                    act(xfirst(h, up, t))

                has = jnp.logical_and(has, jnp.logical_not(turn))

            @pl.when(has)
            def _():
                act(xcopy(h, up, t))

    def relay(h, t, act):
        if t < detour:
            for up in (False, True):
                @pl.when(me_r == (3 if up else 0))
                def _():
                    act(up)

    def relay_on(h, t):
        def go(up):
            xfirst(h, up, t).wait_recv()
            xsecond(h, up, t).start()

        relay(h, t, go)

    def xarrived(h, t):
        @pl.when(me_r > 0)
        def _():
            xcopy(h, True, t).wait_recv()

        @pl.when(me_r < rows - 1)
        def _():
            xcopy(h, False, t).wait_recv()

    def ycopy(h, up):
        own, far = ((Y, 0) if up else (W, Y + W))
        return pltpu.make_async_remote_copy(
            src_ref=yb.at[h, :, :, pl.ds(own, W)],
            dst_ref=yb.at[h, :, :, pl.ds(far, W)],
            send_sem=sy.at[h, int(up)],
            recv_sem=ry.at[h, int(up)],
            device_id={"col": lax.rem(me_c + (1 if up else cols - 1), cols)},
            device_id_type=MESH,
        )

    def yeach(h, up, act):
        @pl.when(me_c < cols - 1 if up else me_c > 0)
        def _():
            act(ycopy(h, up))

    def yarrived(h):
        @pl.when(me_c > 0)
        def _():
            ycopy(h, True).wait_recv()

        @pl.when(me_c < cols - 1)
        def _():
            ycopy(h, False).wait_recv()

    def xstart(h, t):
        xeach(h, t, lambda copy: copy.start())

    for h in range(2):
        @pl.when(me_r == 0)
        def _():
            xb[h, :, 0:W] = jnp.zeros((2, W, Y, LANES), F32)

        @pl.when(me_r == rows - 1)
        def _():
            xb[h, :, X + W:] = jnp.zeros((2, W, Y, LANES), F32)

        @pl.when(me_c == 0)
        def _():
            yb[h, :, :, 0:W] = jnp.zeros((2, X, W, LANES), F32)

        @pl.when(me_c == cols - 1)
        def _():
            yb[h, :, :, Y + W:] = jnp.zeros((2, X, W, LANES), F32)

    for i in range(slabs):
        fetch(0, i).wait()
        fetch(1, i).wait()
        for f, ref in enumerate((gal, ran)):
            high, low = split(ref[pl.ds(i * PX, PX)].reshape(PX * Y, Z))
            val = dot(high, thi[...]) + dot(high, tlo[...]) + dot(low, thi[...])
            xb[0, f, pl.ds(W + i * PX, PX)] = val[:, :LANES].reshape(PX, Y, LANES)
            yb[1, f, pl.ds(i * PX, PX), pl.ds(W, Y)] = val[:, LANES:].reshape(PX, Y, LANES)

    pl.semaphore_wait(barrier, rows + cols - 2)
    for t in range(tiles):
        xstart(0, t)
    for up in (False, True):
        yeach(1, up, lambda copy: copy.start())

    for k in (2, 3):
        fetch(k).wait()

    def tstep(i, carry):
        m = cov[i].astype(F32)
        g = (m * gal[i]).reshape(Y // 8, 8, Z).sum(axis=0)
        r = (m * ran[i]).reshape(Y // 8, 8, Z).sum(axis=0)
        return carry[0] + g, carry[1] + r

    zero = jnp.zeros((8, Z), F32)
    tg, tr = lax.fori_loop(0, X, tstep, (zero, zero))
    for f, t in enumerate((tg, tr)):
        trow[me_r, f] = sum(t[:, k * LANES:(k + 1) * LANES] for k in range(Z // LANES))
    row_totals = gather_sum("row", rows, trow, s1, r1)

    acc[...] = jnp.zeros_like(acc)
    groups = X // 2 * tiles // GROUP

    def members(h, n):
        for k in range(GROUP):
            i = n * GROUP + k
            yield (i // tiles, i % tiles) if h == 0 else (i % (X // 2), i // (X // 2))

    def cells(ref, h, n):
        parts = []
        for lx, t in members(h, n):
            at = pl.ds(pl.multiple_of(t * 8, 8), 8), pl.ds(h * LANES, LANES)
            parts += [ref[(2 * lx, *at)], ref[(2 * lx + 1, *at)]]
        return jnp.concatenate(parts, axis=1)

    def onehots(h):
        def step(n, unused):
            p = jnp.where(cells(cov, h, n) > 0, cells(pat, h, n), -1)
            phi, plo = p >> 5, p & 31

            def rows_of(a, b):
                return jnp.concatenate([a, b], axis=0).astype(BF16)

            def one(v, k):
                return jnp.where(v == k, 1.0, 0.0)

            for k in range(4):
                hit = one(phi, k)
                oh[h, n, pl.ds(16 * k, 16)] = rows_of(hit, hit)
            for k in range(16):
                rh[h, n, pl.ds(16 * k, 16)] = rows_of(one(plo, 2 * k), one(plo, 2 * k + 1))
            return unused

        lax.fori_loop(0, groups, step, 0)

    def histogram(h, first, last):
        def step(n, unused):
            c = cells(contrast, h, n)
            hot = oh[h, n]
            terms = [hot]
            power = c
            for q in range(3):
                high, low = split(power)
                both = jnp.concatenate([high.astype(F32), low.astype(F32)], axis=0).astype(BF16)
                terms.append(jnp.concatenate([both] * 4, axis=0) * hot)
                power = power * c
            acc[...] += lax.dot_general(
                rh[h, n], jnp.concatenate(terms, axis=0), (((1,), (1,)), ((), ())),
                preferred_element_type=F32,
            )
            return unused

        lax.fori_loop(first, last, step, 0, unroll=min(2, last - first))

    def ypass(h, i):
        both = jnp.concatenate(
            [yb[h, f, pl.ds(i * 4, 4)].reshape(4 * (Y + 2 * W), LANES) for f in range(2)], axis=1
        )
        high, low = split(both)
        kh = kyhi[...]
        return dot(kh, high) + dot(kylo[...], high) + dot(kh, low)

    def xpass(h, t):
        ys = pl.ds(t * 8, 8)
        both = jnp.concatenate(
            [xb[h, f, :, ys].reshape((X + 2 * W) * 8, LANES) for f in range(2)], axis=1
        )
        high, low = split(both)
        kh = kxhi[...]
        return dot(kh, high) + dot(kxlo[...], high) + dot(kh, low)

    def contrast_of(val, m, alpha):
        nbar = alpha * val[:, LANES:]
        weight = 1.0 / (1.0 + 2.0 * nbar)
        return m * weight * (val[:, :LANES] / nbar - 1.0)

    onehots(0)
    onehots(1)
    for k in (8, 9):
        fetch(k).wait()
    yarrived(1)

    def yown(i, unused):
        val = ypass(1, i)
        for f in range(2):
            xb[1, f, pl.ds(W + i * 4, 4)] = val[:, f * LANES:(f + 1) * LANES].reshape(4, Y, LANES)
        return unused

    lax.fori_loop(0, X // 4, yown, 0, unroll=2)
    for t in range(detour):
        relay_on(0, t)
    xstart(1, 0)
    tcol[me_c] = add_up(row_totals, trow, rows)
    col_totals = gather_sum("col", cols, tcol, s2, r2)
    for t in range(1, tiles):
        relay_on(1, t - 1)
        xstart(1, t)
    tot = add_up(col_totals, tcol, cols)
    alpha = jnp.sum(tot[0], keepdims=True) / jnp.sum(tot[1], keepdims=True)
    for k in (6, 7, 10):
        fetch(k).wait()

    for t in range(tiles):
        xarrived(0, t)
        val = xpass(0, t)
        for f in range(2):
            yb[0, f, :, pl.ds(W + t * 8, 8)] = val[:, f * LANES:(f + 1) * LANES].reshape(X, 8, LANES)
        if t == W // 8 - 1:
            yeach(0, False, lambda copy: copy.start())
    yeach(0, True, lambda copy: copy.start())

    def last_of(h, t):
        lanes = pl.ds(h * LANES, LANES)
        xarrived(h, t)
        val = xpass(h, t)
        m = cov[:, pl.ds(t * 8, 8), lanes].astype(F32).reshape(X * 8, LANES)
        contrast[:, pl.ds(t * 8, 8), lanes] = contrast_of(val, m, alpha).reshape(X, 8, LANES)
        histogram(h, groups * t // tiles, groups * (t + 1) // tiles)

    def cstep(i, unused):
        val = ypass(0, i)
        x4, lanes = pl.ds(i * 4, 4), pl.ds(0, LANES)
        m = cov[x4, :, lanes].astype(F32).reshape(4 * Y, LANES)
        contrast[x4, :, lanes] = contrast_of(val, m, alpha).reshape(4, Y, LANES)
        return unused

    for t in range(tiles):
        if t == tiles // 2:
            yarrived(0)
            lax.fori_loop(0, X // 4, cstep, 0, unroll=2)
            histogram(0, 0, groups)
        last_of(1, t)

    a = acc[...]
    same = lax.broadcasted_iota(jnp.int32, a.shape, 0) % 8 == lax.broadcasted_iota(jnp.int32, a.shape, 1) % 8
    a = jnp.where(same, a, 0.0).reshape(32, 8, 256).sum(axis=1).T
    terms = []
    for q in range(4):
        for k in range(4):
            at = q * 64 + k * 16
            term = a[at:at + 8] if q == 0 else a[at:at + 8] + a[at + 8:at + 16]
            terms.append(jnp.sum(term, axis=0, keepdims=True))
    spread = jnp.dot(
        jnp.concatenate(terms, axis=0), rep[...],
        precision=lax.Precision.HIGHEST, preferred_element_type=F32,
    )
    own = lax.broadcasted_iota(jnp.int32, spread.shape, 1) // 32 == lax.broadcasted_iota(jnp.int32, spread.shape, 0) % 4
    spread = jnp.where(own, spread, 0.0)
    for q in range(4):
        srow[me_r, q:q + 1] = jnp.sum(spread[4 * q:4 * q + 4], axis=0, keepdims=True)
    srow[me_r, 4:8] = jnp.zeros((4, NPATCH), F32)
    scol[me_c] = add_up(gather_sum("row", rows, srow, s3, r3), srow, rows)
    whole = add_up(gather_sum("col", cols, scol, s4, r4), scol, cols)
    sums[...] = whole[0:4] * scale

    for h in range(2):
        for t in range(tiles):
            xeach(h, t, lambda copy: copy.wait_send())
            relay(h, t, lambda up: xsecond(h, up, t).wait_send())
        for up in (False, True):
            yeach(h, up, lambda copy: copy.wait_send())


def local(galaxy, randoms, coverage, patch):
    rows, cols = lax.axis_size("row"), lax.axis_size("col")
    X, Y, Z = galaxy.shape
    W = RADIUS
    tiles = Y // 8
    groups = X // 2 * tiles // GROUP
    scale = NPATCH / (X * rows * Y * cols * Z)
    tz = split_np(band(Z, Z, 0).T)
    kx = split_np(np.kron(band(X, X + 2 * W, W), np.eye(8, dtype=np.float32)))
    ky = split_np(np.kron(np.eye(4, dtype=np.float32), band(Y, Y + 2 * W, W)))
    rep = (np.arange(NPATCH)[None, :] % 32 == np.arange(32)[:, None]).astype(np.float32)
    consts = [jnp.asarray(v) for v in (*tz, *kx, *ky, rep)]
    args = (galaxy, randoms, coverage, patch, *consts)
    vmem = pl.BlockSpec(memory_space=pltpu.VMEM)
    dma = pltpu.SemaphoreType.DMA
    contrast, sums = pl.pallas_call(
        functools.partial(kernel, rows, cols, scale),
        out_shape=(
            pltpu.VMEM((X, Y, Z), F32),
            pltpu.VMEM((4, NPATCH), F32),
        ),
        in_specs=[pl.BlockSpec(memory_space=pl.ANY)] * 11,
        out_specs=(vmem, vmem),
        scratch_shapes=[pltpu.VMEM(v.shape, v.dtype) for v in args] + [
            pltpu.VMEM((2, 2, X + 2 * W, Y, LANES), F32),
            pltpu.VMEM((2, 2, X, Y + 2 * W, LANES), F32),
            pltpu.VMEM((256, 256), F32),
            pltpu.VMEM((rows, 2, 8, LANES), F32),
            pltpu.VMEM((cols, 2, 8, LANES), F32),
            pltpu.VMEM((rows, 8, NPATCH), F32),
            pltpu.VMEM((cols, 8, NPATCH), F32),
            pltpu.VMEM((2, tiles // 2, 2, W, 8, LANES), F32),
            pltpu.VMEM((2, groups, 64, 2 * LANES * GROUP), BF16),
            pltpu.VMEM((2, groups, 256, 2 * LANES * GROUP), BF16),
            dma((11, X // 8)),
            dma((2, 2, tiles)), dma((2, 2, tiles)), dma((2, 2)), dma((2, 2)),
            dma((2, tiles // 2)), dma((2, tiles // 2)),
            dma((rows - 1,)), dma((rows - 1,)), dma((cols - 1,)), dma((cols - 1,)),
            dma((rows - 1,)), dma((rows - 1,)), dma((cols - 1,)), dma((cols - 1,)),
        ],
        compiler_params=pltpu.CompilerParams(
            collective_id=0, has_side_effects=True, vmem_limit_bytes=56 * 1024 * 1024
        ),
    )(*args)
    return contrast, sums


def solution(mesh):
    spec = P("row", "col", None)
    return jax.shard_map(
        local, mesh=mesh, in_specs=(spec,) * 4, out_specs=(spec, P()), check_vma=False
    )
```

```python
import functools

import jax
import jax.numpy as jnp
import ml_dtypes
import numpy as np
from jax import lax
from jax.experimental import pallas as pl
from jax.experimental.pallas import tpu as pltpu
from jax.sharding import PartitionSpec as P

RADIUS = 16
NPATCH = 128
LANES = 128
GROUP = 16
DIRECT = 32
F32 = jnp.float32
BF16 = jnp.bfloat16
MESH = pl.DeviceIdType.MESH


def taps_np():
    offs = np.arange(-RADIUS, RADIUS + 1).astype(np.float32)
    sigma = RADIUS / 2.0
    vals = np.exp(-offs * offs / np.float32(2.0 * sigma * sigma)).astype(np.float32)
    return (vals / vals.sum(dtype=np.float32)).astype(np.float32)


def split_np(mat):
    high = mat.astype(ml_dtypes.bfloat16)
    low = (mat - high.astype(np.float32)).astype(ml_dtypes.bfloat16)
    return high, low


def band(outs, ins, shift):
    taps = taps_np()
    mat = np.zeros((outs, ins), np.float32)
    for o in range(outs):
        for j in range(-RADIUS, RADIUS + 1):
            i = o + j + shift
            if 0 <= i < ins:
                mat[o, i] = taps[j + RADIUS]
    return mat


def split(val):
    high = val.astype(BF16)
    low = (val - high.astype(F32)).astype(BF16)
    return high, low


def dot(a, b):
    return jnp.dot(a, b, preferred_element_type=F32)


def gather_sum(axis, size, buf, send, recv):
    me = lax.axis_index(axis)
    copies = []
    for k in range(1, size):
        copy = pltpu.make_async_remote_copy(
            src_ref=buf.at[me],
            dst_ref=buf.at[me],
            send_sem=send.at[k - 1],
            recv_sem=recv.at[k - 1],
            device_id={axis: lax.rem(me + k, size)},
            device_id_type=MESH,
        )
        copy.start()
        copies.append(copy)
    return copies


def add_up(copies, buf, size):
    for copy in copies:
        copy.wait()
    total = buf[0]
    for k in range(1, size):
        total = total + buf[k]
    return total


def shifts(rows, cols):
    pairs = [(r, c) for r in range(rows) for c in range(cols) if (r, c) != (0, 0)]
    return sorted(pairs, key=lambda rc: -(min(rc[0], 1) + min(rc[1], cols - rc[1])))


def kernel(
    rows, cols, scale,
    *refs,
):
    hbm, (contrast, sums), vmem = refs[:11], refs[11:13], refs[13:24]
    (
        xb, yb, acc, trow, tcol, sall, scol, rb, oh, rh, sin,
        sx, rx, sy, ry, srel, rrel, s1, r1, s2, r2, s3, r3, s4, r4,
    ) = refs[24:]
    gal, ran, cov, pat, thi, tlo, kxhi, kxlo, kyhi, kylo, rep = vmem
    X, Y, Z = gal.shape
    W = RADIUS
    tiles = Y // 8
    me_r = lax.axis_index("row")
    me_c = lax.axis_index("col")

    PX = 8
    slabs = X // PX
    def fetch(k, slab=None):
        at = slice(None) if slab is None else pl.ds(slab * PX, PX)
        return pltpu.make_async_copy(
            hbm[k].at[at], vmem[k].at[at], sin.at[k, 0 if slab is None else slab]
        )

    fetch(4).start()
    fetch(5).start()
    for i in range(slabs):
        fetch(0, i).start()
        fetch(1, i).start()
    for k in (2, 3, 8, 9, 6, 7, 10):
        fetch(k).start()

    barrier = pltpu.get_barrier_semaphore()
    for k in range(1, rows):
        pl.semaphore_signal(barrier, inc=1, device_id={"row": lax.rem(me_r + k, rows)}, device_id_type=MESH)
    for k in range(1, cols):
        pl.semaphore_signal(barrier, inc=1, device_id={"col": lax.rem(me_c + k, cols)}, device_id_type=MESH)
    fetch(4).wait()
    fetch(5).wait()

    relayed = rows == 4
    detour = tiles // 2 if relayed else 0

    def xsrc(h, up, t):
        return xb.at[h, :, pl.ds(X if up else W, W), pl.ds(t * 8, 8)]

    def xdst(h, up, t):
        return xb.at[h, :, pl.ds(0 if up else X + W, W), pl.ds(t * 8, 8)]

    def xsend(src, dst, ssem, rsem, hop):
        return pltpu.make_async_remote_copy(
            src_ref=src, dst_ref=dst, send_sem=ssem, recv_sem=rsem,
            device_id={"row": lax.rem(me_r + (hop + rows), rows)}, device_id_type=MESH,
        )

    def xcopy(h, up, t):
        u = int(up)
        return xsend(xsrc(h, up, t), xdst(h, up, t), sx.at[h, u, t], rx.at[h, u, t], 1 if up else -1)

    def xfirst(h, up, t):
        return xsend(xsrc(h, up, t), rb.at[h, t], sx.at[h, int(up), t], rrel.at[h, t], 2 if up else -2)

    def xsecond(h, up, t):
        return xsend(rb.at[h, t], xdst(h, up, t), srel.at[h, t], rx.at[h, int(up), t], -1 if up else 1)

    def xeach(h, t, act):
        for up in (False, True):
            has = me_r < rows - 1 if up else me_r > 0
            if t < detour:
                turn = me_r == (1 if up else 2)

                @pl.when(turn)
                def _():
                    act(xfirst(h, up, t))

                has = jnp.logical_and(has, jnp.logical_not(turn))

            @pl.when(has)
            def _():
                act(xcopy(h, up, t))

    def relay(h, t, act):
        if t < detour:
            for up in (False, True):
                @pl.when(me_r == (3 if up else 0))
                def _():
                    act(up)

    def relay_on(h, t):
        def go(up):
            xfirst(h, up, t).wait_recv()
            xsecond(h, up, t).start()

        relay(h, t, go)

    def xarrived(h, t):
        @pl.when(me_r > 0)
        def _():
            xcopy(h, True, t).wait_recv()

        @pl.when(me_r < rows - 1)
        def _():
            xcopy(h, False, t).wait_recv()

    def ycopy(h, up, part):
        own, far = ((Y, 0) if up else (W, Y + W))
        return pltpu.make_async_remote_copy(
            src_ref=yb.at[h, :, :, pl.ds(own + 8 * part, 8)],
            dst_ref=yb.at[h, :, :, pl.ds(far + 8 * part, 8)],
            send_sem=sy.at[h, int(up), part],
            recv_sem=ry.at[h, int(up), part],
            device_id={"col": lax.rem(me_c + (1 if up else cols - 1), cols)},
            device_id_type=MESH,
        )

    def yeach(h, up, part, act):
        @pl.when(me_c < cols - 1 if up else me_c > 0)
        def _():
            act(ycopy(h, up, part))

    def ystart(h, t):
        for up in (False, True):
            part = t - (tiles - W // 8 if up else 0)
            if 0 <= part < W // 8:
                yeach(h, up, part, lambda copy: copy.start())

    def yarrived(h):
        for part in range(W // 8):
            @pl.when(me_c > 0)
            def _():
                ycopy(h, True, part).wait_recv()

            @pl.when(me_c < cols - 1)
            def _():
                ycopy(h, False, part).wait_recv()

    def xstart(h, t):
        xeach(h, t, lambda copy: copy.start())

    for h in range(2):
        @pl.when(me_r == 0)
        def _():
            xb[h, :, 0:W] = jnp.zeros((2, W, Y, LANES), F32)

        @pl.when(me_r == rows - 1)
        def _():
            xb[h, :, X + W:] = jnp.zeros((2, W, Y, LANES), F32)

        @pl.when(me_c == 0)
        def _():
            yb[h, :, :, 0:W] = jnp.zeros((2, X, W, LANES), F32)

        @pl.when(me_c == cols - 1)
        def _():
            yb[h, :, :, Y + W:] = jnp.zeros((2, X, W, LANES), F32)

    for i in range(slabs):
        fetch(0, i).wait()
        fetch(1, i).wait()
        for f, ref in enumerate((gal, ran)):
            high, low = split(ref[pl.ds(i * PX, PX)].reshape(PX * Y, Z))
            val = dot(high, thi[...]) + dot(high, tlo[...]) + dot(low, thi[...])
            xb[0, f, pl.ds(W + i * PX, PX)] = val[:, :LANES].reshape(PX, Y, LANES)
            yb[1, f, pl.ds(i * PX, PX), pl.ds(W, Y)] = val[:, LANES:].reshape(PX, Y, LANES)

    pl.semaphore_wait(barrier, rows + cols - 2)
    xstart(0, 0)
    xstart(0, 1)
    for t in range(tiles):
        ystart(1, t)

    for k in (2, 3):
        fetch(k).wait()

    def tstep(i, carry):
        m = cov[i].astype(F32)
        g = (m * gal[i]).reshape(Y // 8, 8, Z).sum(axis=0)
        r = (m * ran[i]).reshape(Y // 8, 8, Z).sum(axis=0)
        return carry[0] + g, carry[1] + r

    zero = jnp.zeros((8, Z), F32)
    tg, tr = lax.fori_loop(0, X, tstep, (zero, zero))
    for f, t in enumerate((tg, tr)):
        trow[me_r, f] = sum(t[:, k * LANES:(k + 1) * LANES] for k in range(Z // LANES))
    row_totals = gather_sum("row", rows, trow, s1, r1)

    acc[...] = jnp.zeros_like(acc)
    groups = X // 2 * tiles // GROUP

    def members(h, n):
        for k in range(GROUP):
            i = n * GROUP + k
            yield (i // tiles, i % tiles) if h == 0 else (i % (X // 2), i // (X // 2))

    def cells(ref, h, n):
        parts = []
        for lx, t in members(h, n):
            at = pl.ds(pl.multiple_of(t * 8, 8), 8), pl.ds(h * LANES, LANES)
            parts += [ref[(2 * lx, *at)], ref[(2 * lx + 1, *at)]]
        return jnp.concatenate(parts, axis=1)

    def onehots(h):
        def step(n, unused):
            p = jnp.where(cells(cov, h, n) > 0, cells(pat, h, n), -1)
            phi, plo = p >> 5, p & 31

            def rows_of(a, b):
                return jnp.concatenate([a, b], axis=0).astype(BF16)

            def one(v, k):
                return jnp.where(v == k, 1.0, 0.0)

            for k in range(4):
                hit = one(phi, k)
                oh[h, n, pl.ds(16 * k, 16)] = rows_of(hit, hit)
            for k in range(16):
                rh[h, n, pl.ds(16 * k, 16)] = rows_of(one(plo, 2 * k), one(plo, 2 * k + 1))
            return unused

        lax.fori_loop(0, groups, step, 0)

    def histogram(h, first, last):
        def step(n, unused):
            c = cells(contrast, h, n)
            hot = oh[h, n]
            terms = [hot]
            power = c
            for q in range(3):
                high, low = split(power)
                both = jnp.concatenate([high.astype(F32), low.astype(F32)], axis=0).astype(BF16)
                terms.append(jnp.concatenate([both] * 4, axis=0) * hot)
                power = power * c
            acc[...] += lax.dot_general(
                rh[h, n], jnp.concatenate(terms, axis=0), (((1,), (1,)), ((), ())),
                preferred_element_type=F32,
            )
            return unused

        lax.fori_loop(first, last, step, 0, unroll=min(2, last - first))

    def ypass(h, i):
        both = jnp.concatenate(
            [yb[h, f, pl.ds(i * 4, 4)].reshape(4 * (Y + 2 * W), LANES) for f in range(2)], axis=1
        )
        high, low = split(both)
        kh = kyhi[...]
        return dot(kh, high) + dot(kylo[...], high) + dot(kh, low)

    def xpass(h, t):
        ys = pl.ds(t * 8, 8)
        both = jnp.concatenate(
            [xb[h, f, :, ys].reshape((X + 2 * W) * 8, LANES) for f in range(2)], axis=1
        )
        high, low = split(both)
        kh = kxhi[...]
        return dot(kh, high) + dot(kxlo[...], high) + dot(kh, low)

    def contrast_of(val, m, alpha):
        nbar = alpha * val[:, LANES:]
        weight = 1.0 / (1.0 + 2.0 * nbar)
        return m * weight * (val[:, :LANES] / nbar - 1.0)

    def yown(i, unused):
        val = ypass(1, i)
        for f in range(2):
            xb[1, f, pl.ds(W + i * 4, 4)] = val[:, f * LANES:(f + 1) * LANES].reshape(4, Y, LANES)
        return unused

    def first_of(t):
        xarrived(0, t)
        val = xpass(0, t)
        for f in range(2):
            yb[0, f, :, pl.ds(W + t * 8, 8)] = val[:, f * LANES:(f + 1) * LANES].reshape(X, 8, LANES)
        ystart(0, t)

    for t in range(2, tiles):
        onehots(t - 2)
        relay_on(0, t - 2)
        xstart(0, t)
    for k in (8, 9):
        fetch(k).wait()
    yarrived(1)
    lax.fori_loop(0, X // 4, yown, 0, unroll=2)
    xstart(1, 0)
    tcol[me_c] = add_up(row_totals, trow, rows)
    col_totals = gather_sum("col", cols, tcol, s2, r2)
    for k in (6, 7, 10):
        fetch(k).wait()
    for t in range(tiles):
        first_of(t)
        relay_on(1, t)
        if t + 1 < tiles:
            xstart(1, t + 1)
    tot = add_up(col_totals, tcol, cols)
    alpha = jnp.sum(tot[0], keepdims=True) / jnp.sum(tot[1], keepdims=True)

    def last_of(h, t):
        lanes = pl.ds(h * LANES, LANES)
        xarrived(h, t)
        val = xpass(h, t)
        m = cov[:, pl.ds(t * 8, 8), lanes].astype(F32).reshape(X * 8, LANES)
        contrast[:, pl.ds(t * 8, 8), lanes] = contrast_of(val, m, alpha).reshape(X, 8, LANES)
        histogram(h, groups * t // tiles, groups * (t + 1) // tiles)

    def cstep(i, unused):
        val = ypass(0, i)
        x4, lanes = pl.ds(i * 4, 4), pl.ds(0, LANES)
        m = cov[x4, :, lanes].astype(F32).reshape(4 * Y, LANES)
        contrast[x4, :, lanes] = contrast_of(val, m, alpha).reshape(4, Y, LANES)
        return unused

    yarrived(0)
    lax.fori_loop(0, X // 4, cstep, 0, unroll=2)
    histogram(0, 0, groups)
    for t in range(tiles):
        last_of(1, t)

    a = acc[...]
    same = lax.broadcasted_iota(jnp.int32, a.shape, 0) % 8 == lax.broadcasted_iota(jnp.int32, a.shape, 1) % 8
    a = jnp.where(same, a, 0.0).reshape(32, 8, 256).sum(axis=1).T
    terms = []
    for q in range(4):
        for k in range(4):
            at = q * 64 + k * 16
            term = a[at:at + 8] if q == 0 else a[at:at + 8] + a[at + 8:at + 16]
            terms.append(jnp.sum(term, axis=0, keepdims=True))
    spread = jnp.dot(
        jnp.concatenate(terms, axis=0), rep[...],
        precision=lax.Precision.HIGHEST, preferred_element_type=F32,
    )
    own = lax.broadcasted_iota(jnp.int32, spread.shape, 1) // 32 == lax.broadcasted_iota(jnp.int32, spread.shape, 0) % 4
    spread = jnp.where(own, spread, 0.0)
    mine = jnp.concatenate(
        [jnp.sum(spread[4 * q:4 * q + 4], axis=0, keepdims=True) for q in range(4)]
        + [jnp.zeros((4, NPATCH), F32)], axis=0,
    )
    if rows * cols <= DIRECT:
        me = me_r * cols + me_c
        sall[me] = mine
        copies = []
        for k, (kr, kc) in enumerate(shifts(rows, cols)):
            copy = pltpu.make_async_remote_copy(
                src_ref=sall.at[me, pl.ds(0, 4)],
                dst_ref=sall.at[me, pl.ds(0, 4)],
                send_sem=s3.at[k],
                recv_sem=r3.at[k],
                device_id={"row": lax.rem(me_r + kr, rows), "col": lax.rem(me_c + kc, cols)},
                device_id_type=MESH,
            )
            copy.start()
            copies.append(copy)
        for copy in copies:
            copy.wait_recv()
        sums[...] = jnp.sum(sall[:, 0:4], axis=0) * scale
        for copy in copies:
            copy.wait_send()
    else:
        sall[me_r] = mine
        scol[me_c] = add_up(gather_sum("row", rows, sall, s3, r3), sall, rows)
        whole = add_up(gather_sum("col", cols, scol, s4, r4), scol, cols)
        sums[...] = whole[0:4] * scale

    for h in range(2):
        for t in range(tiles):
            xeach(h, t, lambda copy: copy.wait_send())
            relay(h, t, lambda up: xsecond(h, up, t).wait_send())
        for up in (False, True):
            for part in range(W // 8):
                yeach(h, up, part, lambda copy: copy.wait_send())


def local(galaxy, randoms, coverage, patch):
    rows, cols = lax.axis_size("row"), lax.axis_size("col")
    X, Y, Z = galaxy.shape
    W = RADIUS
    tiles = Y // 8
    groups = X // 2 * tiles // GROUP
    direct = (rows * cols if rows * cols <= DIRECT else rows) - 1
    scale = NPATCH / (X * rows * Y * cols * Z)
    tz = split_np(band(Z, Z, 0).T)
    kx = split_np(np.kron(band(X, X + 2 * W, W), np.eye(8, dtype=np.float32)))
    ky = split_np(np.kron(np.eye(4, dtype=np.float32), band(Y, Y + 2 * W, W)))
    rep = (np.arange(NPATCH)[None, :] % 32 == np.arange(32)[:, None]).astype(np.float32)
    consts = [jnp.asarray(v) for v in (*tz, *kx, *ky, rep)]
    args = (galaxy, randoms, coverage, patch, *consts)
    vmem = pl.BlockSpec(memory_space=pltpu.VMEM)
    dma = pltpu.SemaphoreType.DMA
    contrast, sums = pl.pallas_call(
        functools.partial(kernel, rows, cols, scale),
        out_shape=(
            pltpu.VMEM((X, Y, Z), F32),
            pltpu.VMEM((4, NPATCH), F32),
        ),
        in_specs=[pl.BlockSpec(memory_space=pl.ANY)] * 11,
        out_specs=(vmem, vmem),
        scratch_shapes=[pltpu.VMEM(v.shape, v.dtype) for v in args] + [
            pltpu.VMEM((2, 2, X + 2 * W, Y, LANES), F32),
            pltpu.VMEM((2, 2, X, Y + 2 * W, LANES), F32),
            pltpu.VMEM((256, 256), F32),
            pltpu.VMEM((rows, 2, 8, LANES), F32),
            pltpu.VMEM((cols, 2, 8, LANES), F32),
            pltpu.VMEM((direct + 1, 8, NPATCH), F32),
            pltpu.VMEM((cols, 8, NPATCH), F32),
            pltpu.VMEM((2, tiles // 2, 2, W, 8, LANES), F32),
            pltpu.VMEM((2, groups, 64, 2 * LANES * GROUP), BF16),
            pltpu.VMEM((2, groups, 256, 2 * LANES * GROUP), BF16),
            dma((11, X // 8)),
            dma((2, 2, tiles)), dma((2, 2, tiles)), dma((2, 2, W // 8)), dma((2, 2, W // 8)),
            dma((2, tiles // 2)), dma((2, tiles // 2)),
            dma((rows - 1,)), dma((rows - 1,)), dma((cols - 1,)), dma((cols - 1,)),
            dma((direct,)), dma((direct,)), dma((cols - 1,)), dma((cols - 1,)),
        ],
        compiler_params=pltpu.CompilerParams(
            collective_id=0, has_side_effects=True, vmem_limit_bytes=56 * 1024 * 1024
        ),
    )(*args)
    return contrast, sums


def solution(mesh):
    spec = P("row", "col", None)
    return jax.shard_map(
        local, mesh=mesh, in_specs=(spec,) * 4, out_specs=(spec, P()), check_vma=False
    )
```

```python
import functools

import jax
import jax.numpy as jnp
import ml_dtypes
import numpy as np
from jax import lax
from jax.experimental import pallas as pl
from jax.experimental.pallas import tpu as pltpu
from jax.sharding import PartitionSpec as P

RADIUS = 16
NPATCH = 128
LANES = 128
GROUP = 16
DIRECT = 32
F32 = jnp.float32
BF16 = jnp.bfloat16
MESH = pl.DeviceIdType.MESH


def taps_np():
    offs = np.arange(-RADIUS, RADIUS + 1).astype(np.float32)
    sigma = RADIUS / 2.0
    vals = np.exp(-offs * offs / np.float32(2.0 * sigma * sigma)).astype(np.float32)
    return (vals / vals.sum(dtype=np.float32)).astype(np.float32)


def split_np(mat):
    high = mat.astype(ml_dtypes.bfloat16)
    low = (mat - high.astype(np.float32)).astype(ml_dtypes.bfloat16)
    return high, low


def band(outs, ins, shift):
    taps = taps_np()
    mat = np.zeros((outs, ins), np.float32)
    for o in range(outs):
        for j in range(-RADIUS, RADIUS + 1):
            i = o + j + shift
            if 0 <= i < ins:
                mat[o, i] = taps[j + RADIUS]
    return mat


def split(val):
    high = val.astype(BF16)
    low = (val - high.astype(F32)).astype(BF16)
    return high, low


def dot(a, b):
    return jnp.dot(a, b, preferred_element_type=F32)


def gather_sum(axis, size, buf, send, recv):
    me = lax.axis_index(axis)
    copies = []
    for k in range(1, size):
        copy = pltpu.make_async_remote_copy(
            src_ref=buf.at[me],
            dst_ref=buf.at[me],
            send_sem=send.at[k - 1],
            recv_sem=recv.at[k - 1],
            device_id={axis: lax.rem(me + k, size)},
            device_id_type=MESH,
        )
        copy.start()
        copies.append(copy)
    return copies


def add_up(copies, buf, size):
    for copy in copies:
        copy.wait()
    total = buf[0]
    for k in range(1, size):
        total = total + buf[k]
    return total


def shifts(rows, cols):
    pairs = [(r, c) for r in range(rows) for c in range(cols) if (r, c) != (0, 0)]
    return sorted(pairs, key=lambda rc: -(min(rc[0], 1) + min(rc[1], cols - rc[1])))


def kernel(
    rows, cols, scale,
    *refs,
):
    hbm, (contrast, sums), vmem = refs[:11], refs[11:13], refs[13:24]
    (
        xb, yb, acc, trow, tcol, sall, scol, rb, oh, rh, sin,
        sx, rx, sy, ry, srel, rrel, s1, r1, s2, r2, s3, r3, s4, r4,
    ) = refs[24:]
    gal, ran, cov, pat, thi, tlo, kxhi, kxlo, kyhi, kylo, rep = vmem
    X, Y, Z = gal.shape
    W = RADIUS
    tiles = Y // 8
    me_r = lax.axis_index("row")
    me_c = lax.axis_index("col")

    def fetch(k, t=None):
        at = slice(None) if t is None else (slice(None), pl.ds(t * 8, 8))
        return pltpu.make_async_copy(hbm[k].at[at], vmem[k].at[at], sin.at[k, t or 0])

    fetch(0, 0).start()
    fetch(1, 0).start()
    fetch(4).start()
    fetch(5).start()
    for t in range(1, tiles):
        fetch(0, t).start()
        fetch(1, t).start()
    for k in (2, 3, 8, 9, 6, 7, 10):
        fetch(k).start()

    barrier = pltpu.get_barrier_semaphore()
    for k in range(1, rows):
        pl.semaphore_signal(barrier, inc=1, device_id={"row": lax.rem(me_r + k, rows)}, device_id_type=MESH)
    for k in range(1, cols):
        pl.semaphore_signal(barrier, inc=1, device_id={"col": lax.rem(me_c + k, cols)}, device_id_type=MESH)
    fetch(4).wait()
    fetch(5).wait()

    relayed = rows == 4
    detour = tiles // 2 if relayed else 0

    def xsrc(h, up, t):
        return xb.at[h, :, pl.ds(X if up else W, W), pl.ds(t * 8, 8)]

    def xdst(h, up, t):
        return xb.at[h, :, pl.ds(0 if up else X + W, W), pl.ds(t * 8, 8)]

    def xsend(src, dst, ssem, rsem, hop):
        return pltpu.make_async_remote_copy(
            src_ref=src, dst_ref=dst, send_sem=ssem, recv_sem=rsem,
            device_id={"row": lax.rem(me_r + (hop + rows), rows)}, device_id_type=MESH,
        )

    def xcopy(h, up, t):
        u = int(up)
        return xsend(xsrc(h, up, t), xdst(h, up, t), sx.at[h, u, t], rx.at[h, u, t], 1 if up else -1)

    def xfirst(h, up, t):
        return xsend(xsrc(h, up, t), rb.at[h, t], sx.at[h, int(up), t], rrel.at[h, t], 2 if up else -2)

    def xsecond(h, up, t):
        return xsend(rb.at[h, t], xdst(h, up, t), srel.at[h, t], rx.at[h, int(up), t], -1 if up else 1)

    def xeach(h, t, act):
        for up in (False, True):
            has = me_r < rows - 1 if up else me_r > 0
            if t < detour:
                turn = me_r == (1 if up else 2)

                @pl.when(turn)
                def _():
                    act(xfirst(h, up, t))

                has = jnp.logical_and(has, jnp.logical_not(turn))

            @pl.when(has)
            def _():
                act(xcopy(h, up, t))

    def relay(h, t, act):
        if t < detour:
            for up in (False, True):
                @pl.when(me_r == (3 if up else 0))
                def _():
                    act(up)

    def relay_on(h, t):
        def go(up):
            xfirst(h, up, t).wait_recv()
            xsecond(h, up, t).start()

        relay(h, t, go)

    def xarrived(h, t):
        @pl.when(me_r > 0)
        def _():
            xcopy(h, True, t).wait_recv()

        @pl.when(me_r < rows - 1)
        def _():
            xcopy(h, False, t).wait_recv()

    def ycopy(h, up, part):
        own, far = ((Y, 0) if up else (W, Y + W))
        return pltpu.make_async_remote_copy(
            src_ref=yb.at[h, :, :, pl.ds(own + 8 * part, 8)],
            dst_ref=yb.at[h, :, :, pl.ds(far + 8 * part, 8)],
            send_sem=sy.at[h, int(up), part],
            recv_sem=ry.at[h, int(up), part],
            device_id={"col": lax.rem(me_c + (1 if up else cols - 1), cols)},
            device_id_type=MESH,
        )

    def yeach(h, up, part, act):
        @pl.when(me_c < cols - 1 if up else me_c > 0)
        def _():
            act(ycopy(h, up, part))

    def ystart(h, t):
        for up in (False, True):
            part = t - (tiles - W // 8 if up else 0)
            if 0 <= part < W // 8:
                yeach(h, up, part, lambda copy: copy.start())

    def yarrived(h):
        for part in range(W // 8):
            @pl.when(me_c > 0)
            def _():
                ycopy(h, True, part).wait_recv()

            @pl.when(me_c < cols - 1)
            def _():
                ycopy(h, False, part).wait_recv()

    def xstart(h, t):
        xeach(h, t, lambda copy: copy.start())

    for t in range(tiles):
        fetch(0, t).wait()
        fetch(1, t).wait()
        for f, ref in enumerate((gal, ran)):
            high, low = split(ref[:, pl.ds(t * 8, 8)].reshape(X * 8, Z))
            val = dot(high, thi[...]) + dot(high, tlo[...]) + dot(low, thi[...])
            xb[0, f, pl.ds(W, X), pl.ds(t * 8, 8)] = val[:, :LANES].reshape(X, 8, LANES)
            yb[1, f, :, pl.ds(W + t * 8, 8)] = val[:, LANES:].reshape(X, 8, LANES)
        if t == 0:
            pl.semaphore_wait(barrier, rows + cols - 2)
        if t < 2:
            xstart(0, t)
        ystart(1, t)

    for h in range(2):
        @pl.when(me_r == 0)
        def _():
            xb[h, :, 0:W] = jnp.zeros((2, W, Y, LANES), F32)

        @pl.when(me_r == rows - 1)
        def _():
            xb[h, :, X + W:] = jnp.zeros((2, W, Y, LANES), F32)

        @pl.when(me_c == 0)
        def _():
            yb[h, :, :, 0:W] = jnp.zeros((2, X, W, LANES), F32)

        @pl.when(me_c == cols - 1)
        def _():
            yb[h, :, :, Y + W:] = jnp.zeros((2, X, W, LANES), F32)

    for k in (2, 3):
        fetch(k).wait()

    def tstep(i, carry):
        m = cov[i].astype(F32)
        g = (m * gal[i]).reshape(Y // 8, 8, Z).sum(axis=0)
        r = (m * ran[i]).reshape(Y // 8, 8, Z).sum(axis=0)
        return carry[0] + g, carry[1] + r

    zero = jnp.zeros((8, Z), F32)
    tg, tr = lax.fori_loop(0, X, tstep, (zero, zero))
    for f, t in enumerate((tg, tr)):
        trow[me_r, f] = sum(t[:, k * LANES:(k + 1) * LANES] for k in range(Z // LANES))
    row_totals = gather_sum("row", rows, trow, s1, r1)

    acc[...] = jnp.zeros_like(acc)
    groups = X // 2 * tiles // GROUP

    def members(h, n):
        for k in range(GROUP):
            i = n * GROUP + k
            yield (i // tiles, i % tiles) if h == 0 else (i % (X // 2), i // (X // 2))

    def cells(ref, h, n):
        parts = []
        for lx, t in members(h, n):
            at = pl.ds(pl.multiple_of(t * 8, 8), 8), pl.ds(h * LANES, LANES)
            parts += [ref[(2 * lx, *at)], ref[(2 * lx + 1, *at)]]
        return jnp.concatenate(parts, axis=1)

    def onehots(h):
        def step(n, unused):
            p = jnp.where(cells(cov, h, n) > 0, cells(pat, h, n), -1)
            phi, plo = p >> 5, p & 31

            def rows_of(a, b):
                return jnp.concatenate([a, b], axis=0).astype(BF16)

            def one(v, k):
                return jnp.where(v == k, 1.0, 0.0)

            for k in range(4):
                hit = one(phi, k)
                oh[h, n, pl.ds(16 * k, 16)] = rows_of(hit, hit)
            for k in range(16):
                rh[h, n, pl.ds(16 * k, 16)] = rows_of(one(plo, 2 * k), one(plo, 2 * k + 1))
            return unused

        lax.fori_loop(0, groups, step, 0)

    def histogram(h, first, last):
        def step(n, unused):
            c = cells(contrast, h, n)
            hot = oh[h, n]
            terms = [hot]
            power = c
            for q in range(3):
                high, low = split(power)
                both = jnp.concatenate([high.astype(F32), low.astype(F32)], axis=0).astype(BF16)
                terms.append(jnp.concatenate([both] * 4, axis=0) * hot)
                power = power * c
            acc[...] += lax.dot_general(
                rh[h, n], jnp.concatenate(terms, axis=0), (((1,), (1,)), ((), ())),
                preferred_element_type=F32,
            )
            return unused

        lax.fori_loop(first, last, step, 0, unroll=min(2, last - first))

    def ypass(h, i):
        both = jnp.concatenate(
            [yb[h, f, pl.ds(i * 4, 4)].reshape(4 * (Y + 2 * W), LANES) for f in range(2)], axis=1
        )
        high, low = split(both)
        kh = kyhi[...]
        return dot(kh, high) + dot(kylo[...], high) + dot(kh, low)

    def xpass(h, t):
        ys = pl.ds(t * 8, 8)
        both = jnp.concatenate(
            [xb[h, f, :, ys].reshape((X + 2 * W) * 8, LANES) for f in range(2)], axis=1
        )
        high, low = split(both)
        kh = kxhi[...]
        return dot(kh, high) + dot(kxlo[...], high) + dot(kh, low)

    def contrast_of(val, m, alpha):
        nbar = alpha * val[:, LANES:]
        weight = 1.0 / (1.0 + 2.0 * nbar)
        return m * weight * (val[:, :LANES] / nbar - 1.0)

    def yown(i, unused):
        val = ypass(1, i)
        for f in range(2):
            xb[1, f, pl.ds(W + i * 4, 4)] = val[:, f * LANES:(f + 1) * LANES].reshape(4, Y, LANES)
        return unused

    def first_of(t):
        xarrived(0, t)
        val = xpass(0, t)
        for f in range(2):
            yb[0, f, :, pl.ds(W + t * 8, 8)] = val[:, f * LANES:(f + 1) * LANES].reshape(X, 8, LANES)
        ystart(0, t)

    for t in range(2, tiles):
        onehots(t - 2)
        relay_on(0, t - 2)
        xstart(0, t)
    for k in (8, 9):
        fetch(k).wait()
    yarrived(1)
    lax.fori_loop(0, X // 4, yown, 0, unroll=2)
    xstart(1, 0)
    tcol[me_c] = add_up(row_totals, trow, rows)
    col_totals = gather_sum("col", cols, tcol, s2, r2)
    for k in (6, 7, 10):
        fetch(k).wait()
    for t in range(tiles):
        first_of(t)
        relay_on(1, t)
        if t + 1 < tiles:
            xstart(1, t + 1)
    tot = add_up(col_totals, tcol, cols)
    alpha = jnp.sum(tot[0], keepdims=True) / jnp.sum(tot[1], keepdims=True)

    def last_of(h, t):
        lanes = pl.ds(h * LANES, LANES)
        xarrived(h, t)
        val = xpass(h, t)
        m = cov[:, pl.ds(t * 8, 8), lanes].astype(F32).reshape(X * 8, LANES)
        contrast[:, pl.ds(t * 8, 8), lanes] = contrast_of(val, m, alpha).reshape(X, 8, LANES)
        histogram(h, groups * t // tiles, groups * (t + 1) // tiles)

    def cstep(i, unused):
        val = ypass(0, i)
        x4, lanes = pl.ds(i * 4, 4), pl.ds(0, LANES)
        m = cov[x4, :, lanes].astype(F32).reshape(4 * Y, LANES)
        contrast[x4, :, lanes] = contrast_of(val, m, alpha).reshape(4, Y, LANES)
        return unused

    yarrived(0)
    lax.fori_loop(0, X // 4, cstep, 0, unroll=2)
    histogram(0, 0, groups)
    for t in range(tiles):
        last_of(1, t)

    a = acc[...]
    same = lax.broadcasted_iota(jnp.int32, a.shape, 0) % 8 == lax.broadcasted_iota(jnp.int32, a.shape, 1) % 8
    a = jnp.where(same, a, 0.0).reshape(32, 8, 256).sum(axis=1).T
    terms = []
    for q in range(4):
        for k in range(4):
            at = q * 64 + k * 16
            term = a[at:at + 8] if q == 0 else a[at:at + 8] + a[at + 8:at + 16]
            terms.append(jnp.sum(term, axis=0, keepdims=True))
    spread = jnp.dot(
        jnp.concatenate(terms, axis=0), rep[...],
        precision=lax.Precision.HIGHEST, preferred_element_type=F32,
    )
    own = lax.broadcasted_iota(jnp.int32, spread.shape, 1) // 32 == lax.broadcasted_iota(jnp.int32, spread.shape, 0) % 4
    spread = jnp.where(own, spread, 0.0)
    mine = jnp.concatenate(
        [jnp.sum(spread[4 * q:4 * q + 4], axis=0, keepdims=True) for q in range(4)]
        + [jnp.zeros((4, NPATCH), F32)], axis=0,
    )
    if rows * cols <= DIRECT:
        me = me_r * cols + me_c
        sall[me] = mine
        copies = []
        for k, (kr, kc) in enumerate(shifts(rows, cols)):
            copy = pltpu.make_async_remote_copy(
                src_ref=sall.at[me, pl.ds(0, 4)],
                dst_ref=sall.at[me, pl.ds(0, 4)],
                send_sem=s3.at[k],
                recv_sem=r3.at[k],
                device_id={"row": lax.rem(me_r + kr, rows), "col": lax.rem(me_c + kc, cols)},
                device_id_type=MESH,
            )
            copy.start()
            copies.append(copy)
        for copy in copies:
            copy.wait_recv()
        sums[...] = jnp.sum(sall[:, 0:4], axis=0) * scale
        for copy in copies:
            copy.wait_send()
    else:
        sall[me_r] = mine
        scol[me_c] = add_up(gather_sum("row", rows, sall, s3, r3), sall, rows)
        whole = add_up(gather_sum("col", cols, scol, s4, r4), scol, cols)
        sums[...] = whole[0:4] * scale

    for h in range(2):
        for t in range(tiles):
            xeach(h, t, lambda copy: copy.wait_send())
            relay(h, t, lambda up: xsecond(h, up, t).wait_send())
        for up in (False, True):
            for part in range(W // 8):
                yeach(h, up, part, lambda copy: copy.wait_send())


def store(contrast, sums, contrast_out, sums_out, sem):
    step = contrast.shape[0] // 1
    copies = [pltpu.make_async_copy(contrast.at[pl.ds(k * step, step)], contrast_out.at[pl.ds(k * step, step)], sem.at[k]) for k in range(1)]
    copies.append(pltpu.make_async_copy(sums, sums_out, sem.at[1]))
    for copy in copies:
        copy.start()
    for copy in copies:
        copy.wait()


def local(galaxy, randoms, coverage, patch):
    rows, cols = lax.axis_size("row"), lax.axis_size("col")
    X, Y, Z = galaxy.shape
    W = RADIUS
    tiles = Y // 8
    groups = X // 2 * tiles // GROUP
    direct = (rows * cols if rows * cols <= DIRECT else rows) - 1
    scale = NPATCH / (X * rows * Y * cols * Z)
    tz = split_np(band(Z, Z, 0).T)
    kx = split_np(np.kron(band(X, X + 2 * W, W), np.eye(8, dtype=np.float32)))
    ky = split_np(np.kron(np.eye(4, dtype=np.float32), band(Y, Y + 2 * W, W)))
    rep = (np.arange(NPATCH)[None, :] % 32 == np.arange(32)[:, None]).astype(np.float32)
    consts = [jnp.asarray(v) for v in (*tz, *kx, *ky, rep)]
    args = (galaxy, randoms, coverage, patch, *consts)
    vmem = pl.BlockSpec(memory_space=pltpu.VMEM)
    dma = pltpu.SemaphoreType.DMA
    contrast, sums = pl.pallas_call(
        functools.partial(kernel, rows, cols, scale),
        out_shape=(
            pltpu.VMEM((X, Y, Z), F32),
            pltpu.VMEM((4, NPATCH), F32),
        ),
        in_specs=[pl.BlockSpec(memory_space=pl.ANY)] * 11,
        out_specs=(vmem, vmem),
        scratch_shapes=[pltpu.VMEM(v.shape, v.dtype) for v in args] + [
            pltpu.VMEM((2, 2, X + 2 * W, Y, LANES), F32),
            pltpu.VMEM((2, 2, X, Y + 2 * W, LANES), F32),
            pltpu.VMEM((256, 256), F32),
            pltpu.VMEM((rows, 2, 8, LANES), F32),
            pltpu.VMEM((cols, 2, 8, LANES), F32),
            pltpu.VMEM((direct + 1, 8, NPATCH), F32),
            pltpu.VMEM((cols, 8, NPATCH), F32),
            pltpu.VMEM((2, tiles // 2, 2, W, 8, LANES), F32),
            pltpu.VMEM((2, groups, 64, 2 * LANES * GROUP), BF16),
            pltpu.VMEM((2, groups, 256, 2 * LANES * GROUP), BF16),
            dma((11, tiles)),
            dma((2, 2, tiles)), dma((2, 2, tiles)), dma((2, 2, W // 8)), dma((2, 2, W // 8)),
            dma((2, tiles // 2)), dma((2, tiles // 2)),
            dma((rows - 1,)), dma((rows - 1,)), dma((cols - 1,)), dma((cols - 1,)),
            dma((direct,)), dma((direct,)), dma((cols - 1,)), dma((cols - 1,)),
        ],
        compiler_params=pltpu.CompilerParams(
            collective_id=0, has_side_effects=True, vmem_limit_bytes=56 * 1024 * 1024
        ),
    )(*args)
    return pl.pallas_call(
        store,
        out_shape=(
            jax.ShapeDtypeStruct((X, Y, Z), F32),
            jax.ShapeDtypeStruct((4, NPATCH), F32),
        ),
        in_specs=[pl.BlockSpec(memory_space=pl.ANY)] * 2,
        out_specs=(pl.BlockSpec(memory_space=pl.ANY),) * 2,
        scratch_shapes=[dma((1 + 1,))],
    )(*(pltpu.with_memory_space_constraint(v, pltpu.VMEM) for v in (contrast, sums)))


def solution(mesh):
    spec = P("row", "col", None)
    return jax.shard_map(
        local, mesh=mesh, in_specs=(spec,) * 4, out_specs=(spec, P()), check_vma=False
    )
```

```python
import functools

import jax
import jax.numpy as jnp
import ml_dtypes
import numpy as np
from jax import lax
from jax.experimental import pallas as pl
from jax.experimental.pallas import tpu as pltpu
from jax.sharding import PartitionSpec as P

RADIUS = 16
NPATCH = 128
LANES = 128
GROUP = 16
DIRECT = 32
F32 = jnp.float32
BF16 = jnp.bfloat16
MESH = pl.DeviceIdType.MESH


def taps_np():
    offs = np.arange(-RADIUS, RADIUS + 1).astype(np.float32)
    sigma = RADIUS / 2.0
    vals = np.exp(-offs * offs / np.float32(2.0 * sigma * sigma)).astype(np.float32)
    return (vals / vals.sum(dtype=np.float32)).astype(np.float32)


def split_np(mat):
    high = mat.astype(ml_dtypes.bfloat16)
    low = (mat - high.astype(np.float32)).astype(ml_dtypes.bfloat16)
    return high, low


def band(outs, ins, shift):
    taps = taps_np()
    mat = np.zeros((outs, ins), np.float32)
    for o in range(outs):
        for j in range(-RADIUS, RADIUS + 1):
            i = o + j + shift
            if 0 <= i < ins:
                mat[o, i] = taps[j + RADIUS]
    return mat


def split(val):
    high = val.astype(BF16)
    low = (val - high.astype(F32)).astype(BF16)
    return high, low


def dot(a, b):
    return jnp.dot(a, b, preferred_element_type=F32)


def gather_sum(axis, size, buf, send, recv):
    me = lax.axis_index(axis)
    copies = []
    for k in range(1, size):
        copy = pltpu.make_async_remote_copy(
            src_ref=buf.at[me],
            dst_ref=buf.at[me],
            send_sem=send.at[k - 1],
            recv_sem=recv.at[k - 1],
            device_id={axis: lax.rem(me + k, size)},
            device_id_type=MESH,
        )
        copy.start()
        copies.append(copy)
    return copies


def add_up(copies, buf, size):
    for copy in copies:
        copy.wait()
    total = buf[0]
    for k in range(1, size):
        total = total + buf[k]
    return total


def shifts(rows, cols):
    pairs = [(r, c) for r in range(rows) for c in range(cols) if (r, c) != (0, 0)]
    return sorted(pairs, key=lambda rc: -(min(rc[0], 1) + min(rc[1], cols - rc[1])))


def kernel(
    rows, cols, scale,
    *refs,
):
    hbm, (contrast, sums), vmem = refs[:11], refs[11:13], refs[13:24]
    (
        xb, yb, acc, trow, tcol, sall, scol, rb, oh, rh, sin,
        sx, rx, sy, ry, srel, rrel, s1, r1, s2, r2, s3, r3, s4, r4,
    ) = refs[24:]
    gal, ran, cov, pat, thi, tlo, kxhi, kxlo, kyhi, kylo, rep = vmem
    X, Y, Z = gal.shape
    W = RADIUS
    tiles = Y // 8
    me_r = lax.axis_index("row")
    me_c = lax.axis_index("col")

    def fetch(k, t=None):
        at = slice(None) if t is None else (slice(None), pl.ds(t * 8, 8))
        return pltpu.make_async_copy(hbm[k].at[at], vmem[k].at[at], sin.at[k, t or 0])

    fetch(0, 0).start()
    fetch(1, 0).start()
    fetch(4).start()
    fetch(5).start()
    for t in range(1, tiles):
        fetch(0, t).start()
        fetch(1, t).start()
    for k in (2, 3, 8, 9, 6, 7, 10):
        fetch(k).start()

    barrier = pltpu.get_barrier_semaphore()
    for k in range(1, rows):
        pl.semaphore_signal(barrier, inc=1, device_id={"row": lax.rem(me_r + k, rows)}, device_id_type=MESH)
    for k in range(1, cols):
        pl.semaphore_signal(barrier, inc=1, device_id={"col": lax.rem(me_c + k, cols)}, device_id_type=MESH)
    fetch(4).wait()
    fetch(5).wait()

    relayed = rows == 4
    detour = tiles // 2 if relayed else 0

    def xsrc(h, up, t):
        return xb.at[h, :, pl.ds(X if up else W, W), pl.ds(t * 8, 8)]

    def xdst(h, up, t):
        return xb.at[h, :, pl.ds(0 if up else X + W, W), pl.ds(t * 8, 8)]

    def xsend(src, dst, ssem, rsem, hop):
        return pltpu.make_async_remote_copy(
            src_ref=src, dst_ref=dst, send_sem=ssem, recv_sem=rsem,
            device_id={"row": lax.rem(me_r + (hop + rows), rows)}, device_id_type=MESH,
        )

    def xcopy(h, up, t):
        u = int(up)
        return xsend(xsrc(h, up, t), xdst(h, up, t), sx.at[h, u, t], rx.at[h, u, t], 1 if up else -1)

    def xfirst(h, up, t):
        return xsend(xsrc(h, up, t), rb.at[h, t], sx.at[h, int(up), t], rrel.at[h, t], 2 if up else -2)

    def xsecond(h, up, t):
        return xsend(rb.at[h, t], xdst(h, up, t), srel.at[h, t], rx.at[h, int(up), t], -1 if up else 1)

    def xacross(h, t, act):
        for up in (False, True):
            if relayed:
                @pl.when(me_r == (1 if up else 2))
                def _():
                    act((xfirst if t < detour else xcopy)(h, up, t))

    def xalong(h, t, act):
        for up in (False, True):
            has = me_r < rows - 1 if up else me_r > 0
            if relayed:
                has = jnp.logical_and(has, me_r != (1 if up else 2))

            @pl.when(has)
            def _():
                act(xcopy(h, up, t))

    def relay(h, t, act):
        if t < detour:
            for up in (False, True):
                @pl.when(me_r == (3 if up else 0))
                def _():
                    act(up)

    def relay_on(h, t):
        def go(up):
            xfirst(h, up, t).wait_recv()
            xsecond(h, up, t).start()

        relay(h, t, go)

    def xarrived(h, t):
        @pl.when(me_r > 0)
        def _():
            xcopy(h, True, t).wait_recv()

        @pl.when(me_r < rows - 1)
        def _():
            xcopy(h, False, t).wait_recv()

    def ycopy(h, up, part):
        own, far = ((Y, 0) if up else (W, Y + W))
        return pltpu.make_async_remote_copy(
            src_ref=yb.at[h, :, :, pl.ds(own + 8 * part, 8)],
            dst_ref=yb.at[h, :, :, pl.ds(far + 8 * part, 8)],
            send_sem=sy.at[h, int(up), part],
            recv_sem=ry.at[h, int(up), part],
            device_id={"col": lax.rem(me_c + (1 if up else cols - 1), cols)},
            device_id_type=MESH,
        )

    def yeach(h, up, part, act):
        @pl.when(me_c < cols - 1 if up else me_c > 0)
        def _():
            act(ycopy(h, up, part))

    def ystart(h, t):
        for up in (False, True):
            part = t - (tiles - W // 8 if up else 0)
            if 0 <= part < W // 8:
                yeach(h, up, part, lambda copy: copy.start())

    def yarrived(h):
        for part in range(W // 8):
            @pl.when(me_c > 0)
            def _():
                ycopy(h, True, part).wait_recv()

            @pl.when(me_c < cols - 1)
            def _():
                ycopy(h, False, part).wait_recv()

    def xeach(h, t, act):
        xacross(h, t, act)
        xalong(h, t, act)

    def begin(copy):
        copy.start()

    def xstart(h, t):
        xeach(h, t, begin)

    for t in range(tiles):
        fetch(0, t).wait()
        fetch(1, t).wait()
        for f, ref in enumerate((gal, ran)):
            high, low = split(ref[:, pl.ds(t * 8, 8)].reshape(X * 8, Z))
            val = dot(high, thi[...]) + dot(high, tlo[...]) + dot(low, thi[...])
            xb[0, f, pl.ds(W, X), pl.ds(t * 8, 8)] = val[:, :LANES].reshape(X, 8, LANES)
            yb[1, f, :, pl.ds(W + t * 8, 8)] = val[:, LANES:].reshape(X, 8, LANES)
        if t == 0:
            pl.semaphore_wait(barrier, rows + cols - 2)
        if t < 2:
            xstart(0, t)
        ystart(1, t)

    for h in range(2):
        @pl.when(me_r == 0)
        def _():
            xb[h, :, 0:W] = jnp.zeros((2, W, Y, LANES), F32)

        @pl.when(me_r == rows - 1)
        def _():
            xb[h, :, X + W:] = jnp.zeros((2, W, Y, LANES), F32)

        @pl.when(me_c == 0)
        def _():
            yb[h, :, :, 0:W] = jnp.zeros((2, X, W, LANES), F32)

        @pl.when(me_c == cols - 1)
        def _():
            yb[h, :, :, Y + W:] = jnp.zeros((2, X, W, LANES), F32)

    for k in (2, 3):
        fetch(k).wait()

    def tstep(i, carry):
        m = cov[i].astype(F32)
        g = (m * gal[i]).reshape(Y // 8, 8, Z).sum(axis=0)
        r = (m * ran[i]).reshape(Y // 8, 8, Z).sum(axis=0)
        return carry[0] + g, carry[1] + r

    zero = jnp.zeros((8, Z), F32)
    tg, tr = lax.fori_loop(0, X, tstep, (zero, zero))
    for f, t in enumerate((tg, tr)):
        trow[me_r, f] = sum(t[:, k * LANES:(k + 1) * LANES] for k in range(Z // LANES))
    row_totals = gather_sum("row", rows, trow, s1, r1)

    acc[...] = jnp.zeros_like(acc)
    groups = X // 2 * tiles // GROUP

    def members(h, first, count):
        for k in range(count):
            i = first + k
            yield (i // tiles, i % tiles) if h == 0 else (i % (X // 2), i // (X // 2))

    def cells(ref, h, first, count=GROUP):
        parts = []
        for lx, t in members(h, first, count):
            at = pl.ds(pl.multiple_of(t * 8, 8), 8), pl.ds(h * LANES, LANES)
            parts += [ref[(2 * lx, *at)], ref[(2 * lx + 1, *at)]]
        return jnp.concatenate(parts, axis=1)

    def onehots(h):
        def step(n, unused):
            p = jnp.where(cells(cov, h, n * GROUP) > 0, cells(pat, h, n * GROUP), -1)
            phi, plo = p >> 5, p & 31

            def rows_of(a, b):
                return jnp.concatenate([a, b], axis=0).astype(BF16)

            def one(v, k):
                return jnp.where(v == k, 1.0, 0.0)

            for k in range(4):
                hit = one(phi, k)
                oh[h, n, pl.ds(16 * k, 16)] = rows_of(hit, hit)
            for k in range(16):
                rh[h, n, pl.ds(16 * k, 16)] = rows_of(one(plo, 2 * k), one(plo, 2 * k + 1))
            return unused

        lax.fori_loop(0, groups, step, 0)

    def add_group(h, n, part=None):
        if part is None:
            at = slice(None)
            c = cells(contrast, h, n * GROUP)
        else:
            at = pl.ds(pl.multiple_of(part * GROUP * LANES, GROUP * LANES), GROUP * LANES)
            c = cells(contrast, h, n * GROUP + part * (GROUP // 2), GROUP // 2)
        hot = oh[h, n, :, at]
        terms = [hot]
        power = c
        for q in range(3):
            high, low = split(power)
            both = jnp.concatenate([high.astype(F32), low.astype(F32)], axis=0).astype(BF16)
            terms.append(jnp.concatenate([both] * 4, axis=0) * hot)
            power = power * c
        acc[...] += lax.dot_general(
            rh[h, n, :, at], jnp.concatenate(terms, axis=0), (((1,), (1,)), ((), ())),
            preferred_element_type=F32,
        )

    def histogram(h, first, last):
        def step(n, unused):
            add_group(h, n)
            return unused

        lax.fori_loop(first, last, step, 0, unroll=min(2, last - first))

    def ypass(h, i):
        both = jnp.concatenate(
            [yb[h, f, pl.ds(i * 4, 4)].reshape(4 * (Y + 2 * W), LANES) for f in range(2)], axis=1
        )
        high, low = split(both)
        kh = kyhi[...]
        return dot(kh, high) + dot(kylo[...], high) + dot(kh, low)

    def xpass(h, t):
        ys = pl.ds(t * 8, 8)
        both = jnp.concatenate(
            [xb[h, f, :, ys].reshape((X + 2 * W) * 8, LANES) for f in range(2)], axis=1
        )
        high, low = split(both)
        kh = kxhi[...]
        return dot(kh, high) + dot(kxlo[...], high) + dot(kh, low)

    def contrast_of(val, m, alpha):
        nbar = alpha * val[:, LANES:]
        weight = 1.0 / (1.0 + 2.0 * nbar)
        return m * weight * (val[:, :LANES] / nbar - 1.0)

    def yown(i, unused):
        val = ypass(1, i)
        for f in range(2):
            xb[1, f, pl.ds(W + i * 4, 4)] = val[:, f * LANES:(f + 1) * LANES].reshape(4, Y, LANES)
        return unused

    def first_of(t):
        xarrived(0, t)
        val = xpass(0, t)
        for f in range(2):
            yb[0, f, :, pl.ds(W + t * 8, 8)] = val[:, f * LANES:(f + 1) * LANES].reshape(X, 8, LANES)
        ystart(0, t)

    for t in range(2, tiles):
        onehots(t - 2)
        relay_on(0, t - 2)
        xstart(0, t)
    for k in (8, 9):
        fetch(k).wait()
    yarrived(1)
    lax.fori_loop(0, X // 4, yown, 0, unroll=2)
    xstart(1, 0)
    tcol[me_c] = add_up(row_totals, trow, rows)
    col_totals = gather_sum("col", cols, tcol, s2, r2)
    for k in (6, 7, 10):
        fetch(k).wait()
    for t in range(tiles):
        first_of(t)
        relay_on(1, t)
        if t + 1 < tiles:
            if t == 0:
                for k in range(1, tiles):
                    xacross(1, k, begin)
            xalong(1, t + 1, begin)
    tot = add_up(col_totals, tcol, cols)
    alpha = jnp.sum(tot[0], keepdims=True) / jnp.sum(tot[1], keepdims=True)

    def half_of(t, upper):
        ys, lanes = pl.ds(t * 8, 8), pl.ds(LANES, LANES)

        @pl.when(jnp.logical_and(upper == 0, me_r > 0))
        def _():
            xcopy(1, True, t).wait_recv()

        @pl.when(jnp.logical_and(upper == 1, me_r < rows - 1))
        def _():
            xcopy(1, False, t).wait_recv()

        first = upper * W
        both = jnp.concatenate(
            [xb[1, f, pl.ds(first, 3 * W), ys].reshape(3 * W * 8, LANES) for f in range(2)], axis=1
        )
        high, low = split(both)
        kh, kl = kxhi[0:W * 8, 0:3 * W * 8], kxlo[0:W * 8, 0:3 * W * 8]
        val = dot(kh, high) + dot(kl, high) + dot(kh, low)
        m = cov[pl.ds(first, W), ys, lanes].astype(F32).reshape(W * 8, LANES)
        contrast[pl.ds(first, W), ys, lanes] = contrast_of(val, m, alpha).reshape(W, 8, LANES)
        add_group(1, t, upper)

    def last_of(h, t):
        lanes = pl.ds(h * LANES, LANES)
        xarrived(h, t)
        val = xpass(h, t)
        m = cov[:, pl.ds(t * 8, 8), lanes].astype(F32).reshape(X * 8, LANES)
        contrast[:, pl.ds(t * 8, 8), lanes] = contrast_of(val, m, alpha).reshape(X, 8, LANES)
        histogram(h, groups * t // tiles, groups * (t + 1) // tiles)

    def cstep(i, unused):
        val = ypass(0, i)
        x4, lanes = pl.ds(i * 4, 4), pl.ds(0, LANES)
        m = cov[x4, :, lanes].astype(F32).reshape(4 * Y, LANES)
        contrast[x4, :, lanes] = contrast_of(val, m, alpha).reshape(4, Y, LANES)
        return unused

    yarrived(0)
    lax.fori_loop(0, X // 4, cstep, 0, unroll=2)
    histogram(0, 0, groups)
    early = lax.rem(me_r, 2)
    late = 1 - early
    last_of(1, 0)
    last_of(1, 1)
    half_of(2, early)
    half_of(3, early)
    half_of(2, late)
    half_of(3, late)

    a = acc[...]
    same = lax.broadcasted_iota(jnp.int32, a.shape, 0) % 8 == lax.broadcasted_iota(jnp.int32, a.shape, 1) % 8
    a = jnp.where(same, a, 0.0).reshape(32, 8, 256).sum(axis=1).T
    terms = []
    for q in range(4):
        for k in range(4):
            at = q * 64 + k * 16
            term = a[at:at + 8] if q == 0 else a[at:at + 8] + a[at + 8:at + 16]
            terms.append(jnp.sum(term, axis=0, keepdims=True))
    spread = jnp.dot(
        jnp.concatenate(terms, axis=0), rep[...],
        precision=lax.Precision.HIGHEST, preferred_element_type=F32,
    )
    own = lax.broadcasted_iota(jnp.int32, spread.shape, 1) // 32 == lax.broadcasted_iota(jnp.int32, spread.shape, 0) % 4
    spread = jnp.where(own, spread, 0.0)
    mine = jnp.concatenate(
        [jnp.sum(spread[4 * q:4 * q + 4], axis=0, keepdims=True) for q in range(4)]
        + [jnp.zeros((4, NPATCH), F32)], axis=0,
    )
    if rows * cols <= DIRECT:
        me = me_r * cols + me_c
        sall[me] = mine
        copies = []
        for k, (kr, kc) in enumerate(shifts(rows, cols)):
            copy = pltpu.make_async_remote_copy(
                src_ref=sall.at[me, pl.ds(0, 4)],
                dst_ref=sall.at[me, pl.ds(0, 4)],
                send_sem=s3.at[k],
                recv_sem=r3.at[k],
                device_id={"row": lax.rem(me_r + kr, rows), "col": lax.rem(me_c + kc, cols)},
                device_id_type=MESH,
            )
            copy.start()
            copies.append(copy)
        for copy in copies:
            copy.wait_recv()
        sums[...] = jnp.sum(sall[:, 0:4], axis=0) * scale
        for copy in copies:
            copy.wait_send()
    else:
        sall[me_r] = mine
        scol[me_c] = add_up(gather_sum("row", rows, sall, s3, r3), sall, rows)
        whole = add_up(gather_sum("col", cols, scol, s4, r4), scol, cols)
        sums[...] = whole[0:4] * scale

    for h in range(2):
        for t in range(tiles):
            xeach(h, t, lambda copy: copy.wait_send())
            relay(h, t, lambda up: xsecond(h, up, t).wait_send())
        for up in (False, True):
            for part in range(W // 8):
                yeach(h, up, part, lambda copy: copy.wait_send())


def store(contrast, sums, contrast_out, sums_out, sem):
    step = contrast.shape[0] // 1
    copies = [pltpu.make_async_copy(contrast.at[pl.ds(k * step, step)], contrast_out.at[pl.ds(k * step, step)], sem.at[k]) for k in range(1)]
    copies.append(pltpu.make_async_copy(sums, sums_out, sem.at[1]))
    for copy in copies:
        copy.start()
    for copy in copies:
        copy.wait()


def local(galaxy, randoms, coverage, patch):
    rows, cols = lax.axis_size("row"), lax.axis_size("col")
    X, Y, Z = galaxy.shape
    W = RADIUS
    tiles = Y // 8
    groups = X // 2 * tiles // GROUP
    direct = (rows * cols if rows * cols <= DIRECT else rows) - 1
    scale = NPATCH / (X * rows * Y * cols * Z)
    tz = split_np(band(Z, Z, 0).T)
    kx = split_np(np.kron(band(X, X + 2 * W, W), np.eye(8, dtype=np.float32)))
    ky = split_np(np.kron(np.eye(4, dtype=np.float32), band(Y, Y + 2 * W, W)))
    rep = (np.arange(NPATCH)[None, :] % 32 == np.arange(32)[:, None]).astype(np.float32)
    consts = [jnp.asarray(v) for v in (*tz, *kx, *ky, rep)]
    args = (galaxy, randoms, coverage, patch, *consts)
    vmem = pl.BlockSpec(memory_space=pltpu.VMEM)
    dma = pltpu.SemaphoreType.DMA
    contrast, sums = pl.pallas_call(
        functools.partial(kernel, rows, cols, scale),
        out_shape=(
            pltpu.VMEM((X, Y, Z), F32),
            pltpu.VMEM((4, NPATCH), F32),
        ),
        in_specs=[pl.BlockSpec(memory_space=pl.ANY)] * 11,
        out_specs=(vmem, vmem),
        scratch_shapes=[pltpu.VMEM(v.shape, v.dtype) for v in args] + [
            pltpu.VMEM((2, 2, X + 2 * W, Y, LANES), F32),
            pltpu.VMEM((2, 2, X, Y + 2 * W, LANES), F32),
            pltpu.VMEM((256, 256), F32),
            pltpu.VMEM((rows, 2, 8, LANES), F32),
            pltpu.VMEM((cols, 2, 8, LANES), F32),
            pltpu.VMEM((direct + 1, 8, NPATCH), F32),
            pltpu.VMEM((cols, 8, NPATCH), F32),
            pltpu.VMEM((2, tiles // 2, 2, W, 8, LANES), F32),
            pltpu.VMEM((2, groups, 64, 2 * LANES * GROUP), BF16),
            pltpu.VMEM((2, groups, 256, 2 * LANES * GROUP), BF16),
            dma((11, tiles)),
            dma((2, 2, tiles)), dma((2, 2, tiles)), dma((2, 2, W // 8)), dma((2, 2, W // 8)),
            dma((2, tiles // 2)), dma((2, tiles // 2)),
            dma((rows - 1,)), dma((rows - 1,)), dma((cols - 1,)), dma((cols - 1,)),
            dma((direct,)), dma((direct,)), dma((cols - 1,)), dma((cols - 1,)),
        ],
        compiler_params=pltpu.CompilerParams(
            collective_id=0, has_side_effects=True, vmem_limit_bytes=56 * 1024 * 1024
        ),
    )(*args)
    return pl.pallas_call(
        store,
        out_shape=(
            jax.ShapeDtypeStruct((X, Y, Z), F32),
            jax.ShapeDtypeStruct((4, NPATCH), F32),
        ),
        in_specs=[pl.BlockSpec(memory_space=pl.ANY)] * 2,
        out_specs=(pl.BlockSpec(memory_space=pl.ANY),) * 2,
        scratch_shapes=[dma((1 + 1,))],
    )(*(pltpu.with_memory_space_constraint(v, pltpu.VMEM) for v in (contrast, sums)))


def solution(mesh):
    spec = P("row", "col", None)
    return jax.shard_map(
        local, mesh=mesh, in_specs=(spec,) * 4, out_specs=(spec, P()), check_vma=False
    )
```

```python
import functools

import jax
import jax.numpy as jnp
import ml_dtypes
import numpy as np
from jax import lax
from jax.experimental import pallas as pl
from jax.experimental.pallas import tpu as pltpu
from jax.sharding import PartitionSpec as P

RADIUS = 16
NPATCH = 128
LANES = 128
GROUP = 16
DIRECT = 32
F32 = jnp.float32
BF16 = jnp.bfloat16
MESH = pl.DeviceIdType.MESH


def taps_np():
    offs = np.arange(-RADIUS, RADIUS + 1).astype(np.float32)
    sigma = RADIUS / 2.0
    vals = np.exp(-offs * offs / np.float32(2.0 * sigma * sigma)).astype(np.float32)
    return (vals / vals.sum(dtype=np.float32)).astype(np.float32)


def split_np(mat):
    high = mat.astype(ml_dtypes.bfloat16)
    low = (mat - high.astype(np.float32)).astype(ml_dtypes.bfloat16)
    return high, low


def band(outs, ins, shift):
    taps = taps_np()
    mat = np.zeros((outs, ins), np.float32)
    for o in range(outs):
        for j in range(-RADIUS, RADIUS + 1):
            i = o + j + shift
            if 0 <= i < ins:
                mat[o, i] = taps[j + RADIUS]
    return mat


def split(val):
    high = val.astype(BF16)
    low = (val - high.astype(F32)).astype(BF16)
    return high, low


def dot(a, b):
    return jnp.dot(a, b, preferred_element_type=F32)


def gather_sum(axis, size, buf, send, recv):
    me = lax.axis_index(axis)
    copies = []
    for k in range(1, size):
        copy = pltpu.make_async_remote_copy(
            src_ref=buf.at[me],
            dst_ref=buf.at[me],
            send_sem=send.at[k - 1],
            recv_sem=recv.at[k - 1],
            device_id={axis: lax.rem(me + k, size)},
            device_id_type=MESH,
        )
        copy.start()
        copies.append(copy)
    return copies


def add_up(copies, buf, size):
    for copy in copies:
        copy.wait()
    total = buf[0]
    for k in range(1, size):
        total = total + buf[k]
    return total


def shifts(rows, cols):
    pairs = [(r, c) for r in range(rows) for c in range(cols) if (r, c) != (0, 0)]
    return sorted(pairs, key=lambda rc: -(min(rc[0], 1) + min(rc[1], cols - rc[1])))


def kernel(
    rows, cols, scale,
    *refs,
):
    hbm, (contrast, sums), vmem = refs[:11], refs[11:13], refs[13:24]
    (
        xb, yb, acc, trow, tcol, sall, scol, rb, oh, rh, sin,
        sx, rx, sy, ry, srel, rrel, s1, r1, s2, r2, s3, r3, s4, r4,
    ) = refs[24:]
    gal, ran, cov, pat, thi, tlo, kxhi, kxlo, kyhi, kylo, rep = vmem
    X, Y, Z = gal.shape
    W = RADIUS
    tiles = Y // 8
    me_r = lax.axis_index("row")
    me_c = lax.axis_index("col")

    def fetch(k, t=None):
        at = slice(None) if t is None else (slice(None), pl.ds(t * 8, 8))
        return pltpu.make_async_copy(hbm[k].at[at], vmem[k].at[at], sin.at[k, t or 0])

    barrier = pltpu.get_barrier_semaphore()
    for k in range(1, rows):
        pl.semaphore_signal(barrier, inc=1, device_id={"row": lax.rem(me_r + k, rows)}, device_id_type=MESH)
    for k in range(1, cols):
        pl.semaphore_signal(barrier, inc=1, device_id={"col": lax.rem(me_c + k, cols)}, device_id_type=MESH)

    fetch(0, 0).start()
    fetch(1, 0).start()
    fetch(4).start()
    fetch(5).start()
    for t in range(1, tiles):
        fetch(0, t).start()
        fetch(1, t).start()
    for k in (2, 3, 8, 9, 6, 7, 10):
        fetch(k).start()
    fetch(4).wait()
    fetch(5).wait()

    relayed = rows == 4
    detour = tiles // 2 if relayed else 0

    def xsrc(h, up, t):
        return xb.at[h, :, pl.ds(X if up else W, W), pl.ds(t * 8, 8)]

    def xdst(h, up, t):
        return xb.at[h, :, pl.ds(0 if up else X + W, W), pl.ds(t * 8, 8)]

    def xsend(src, dst, ssem, rsem, hop):
        return pltpu.make_async_remote_copy(
            src_ref=src, dst_ref=dst, send_sem=ssem, recv_sem=rsem,
            device_id={"row": lax.rem(me_r + (hop + rows), rows)}, device_id_type=MESH,
        )

    def xcopy(h, up, t):
        u = int(up)
        return xsend(xsrc(h, up, t), xdst(h, up, t), sx.at[h, u, t], rx.at[h, u, t], 1 if up else -1)

    def xfirst(h, up, t):
        return xsend(xsrc(h, up, t), rb.at[h, t], sx.at[h, int(up), t], rrel.at[h, t], 2 if up else -2)

    def xsecond(h, up, t):
        return xsend(rb.at[h, t], xdst(h, up, t), srel.at[h, t], rx.at[h, int(up), t], -1 if up else 1)

    def xacross(h, t, act):
        for up in (False, True):
            if relayed:
                @pl.when(me_r == (1 if up else 2))
                def _():
                    act((xfirst if t < detour else xcopy)(h, up, t))

    def xalong(h, t, act):
        for up in (False, True):
            has = me_r < rows - 1 if up else me_r > 0
            if relayed:
                has = jnp.logical_and(has, me_r != (1 if up else 2))

            @pl.when(has)
            def _():
                act(xcopy(h, up, t))

    def relay(h, t, act):
        if t < detour:
            for up in (False, True):
                @pl.when(me_r == (3 if up else 0))
                def _():
                    act(up)

    def relay_on(h, t):
        def go(up):
            xfirst(h, up, t).wait_recv()
            xsecond(h, up, t).start()

        relay(h, t, go)

    def xarrived(h, t):
        @pl.when(me_r > 0)
        def _():
            xcopy(h, True, t).wait_recv()

        @pl.when(me_r < rows - 1)
        def _():
            xcopy(h, False, t).wait_recv()

    def ycopy(h, up, part):
        own, far = ((Y, 0) if up else (W, Y + W))
        return pltpu.make_async_remote_copy(
            src_ref=yb.at[h, :, :, pl.ds(own + 8 * part, 8)],
            dst_ref=yb.at[h, :, :, pl.ds(far + 8 * part, 8)],
            send_sem=sy.at[h, int(up), part],
            recv_sem=ry.at[h, int(up), part],
            device_id={"col": lax.rem(me_c + (1 if up else cols - 1), cols)},
            device_id_type=MESH,
        )

    def yeach(h, up, part, act):
        @pl.when(me_c < cols - 1 if up else me_c > 0)
        def _():
            act(ycopy(h, up, part))

    def ystart(h, t):
        for up in (False, True):
            part = t - (tiles - W // 8 if up else 0)
            if 0 <= part < W // 8:
                yeach(h, up, part, lambda copy: copy.start())

    def yarrived(h):
        for part in range(W // 8):
            @pl.when(me_c > 0)
            def _():
                ycopy(h, True, part).wait_recv()

            @pl.when(me_c < cols - 1)
            def _():
                ycopy(h, False, part).wait_recv()

    def xeach(h, t, act):
        xacross(h, t, act)
        xalong(h, t, act)

    def begin(copy):
        copy.start()

    def xstart(h, t):
        xeach(h, t, begin)

    for t in range(tiles):
        fetch(0, t).wait()
        fetch(1, t).wait()
        for f, ref in enumerate((gal, ran)):
            high, low = split(ref[:, pl.ds(t * 8, 8)].reshape(X * 8, Z))
            val = dot(high, thi[...]) + dot(high, tlo[...]) + dot(low, thi[...])
            xb[0, f, pl.ds(W, X), pl.ds(t * 8, 8)] = val[:, :LANES].reshape(X, 8, LANES)
            yb[1, f, :, pl.ds(W + t * 8, 8)] = val[:, LANES:].reshape(X, 8, LANES)
        if t == 0:
            pl.semaphore_wait(barrier, rows + cols - 2)
        if t < 2:
            xstart(0, t)
        ystart(1, t)

    for h in range(2):
        @pl.when(me_r == 0)
        def _():
            xb[h, :, 0:W] = jnp.zeros((2, W, Y, LANES), F32)

        @pl.when(me_r == rows - 1)
        def _():
            xb[h, :, X + W:] = jnp.zeros((2, W, Y, LANES), F32)

        @pl.when(me_c == 0)
        def _():
            yb[h, :, :, 0:W] = jnp.zeros((2, X, W, LANES), F32)

        @pl.when(me_c == cols - 1)
        def _():
            yb[h, :, :, Y + W:] = jnp.zeros((2, X, W, LANES), F32)

    for k in (2, 3):
        fetch(k).wait()

    def tstep(i, carry):
        m = cov[i].astype(F32)
        g = (m * gal[i]).reshape(Y // 8, 8, Z).sum(axis=0)
        r = (m * ran[i]).reshape(Y // 8, 8, Z).sum(axis=0)
        return carry[0] + g, carry[1] + r

    zero = jnp.zeros((8, Z), F32)
    tg, tr = lax.fori_loop(0, X, tstep, (zero, zero))
    for f, t in enumerate((tg, tr)):
        trow[me_r, f] = sum(t[:, k * LANES:(k + 1) * LANES] for k in range(Z // LANES))
    row_totals = gather_sum("row", rows, trow, s1, r1)

    acc[...] = jnp.zeros_like(acc)
    groups = X // 2 * tiles // GROUP

    def members(h, first, count):
        for k in range(count):
            i = first + k
            yield (i // tiles, i % tiles) if h == 0 else (i % (X // 2), i // (X // 2))

    def cells(ref, h, first, count=GROUP):
        parts = []
        for lx, t in members(h, first, count):
            at = pl.ds(pl.multiple_of(t * 8, 8), 8), pl.ds(h * LANES, LANES)
            parts += [ref[(2 * lx, *at)], ref[(2 * lx + 1, *at)]]
        return jnp.concatenate(parts, axis=1)

    def onehots(h):
        def step(n, unused):
            p = jnp.where(cells(cov, h, n * GROUP) > 0, cells(pat, h, n * GROUP), -1)
            phi, plo = p >> 5, p & 31

            def rows_of(a, b):
                return jnp.concatenate([a, b], axis=0).astype(BF16)

            def one(v, k):
                return jnp.where(v == k, 1.0, 0.0)

            for k in range(4):
                hit = one(phi, k)
                oh[h, n, pl.ds(16 * k, 16)] = rows_of(hit, hit)
            for k in range(16):
                rh[h, n, pl.ds(16 * k, 16)] = rows_of(one(plo, 2 * k), one(plo, 2 * k + 1))
            return unused

        lax.fori_loop(0, groups, step, 0)

    def add_group(h, n, part=None):
        if part is None:
            at = slice(None)
            c = cells(contrast, h, n * GROUP)
        else:
            at = pl.ds(pl.multiple_of(part * GROUP * LANES, GROUP * LANES), GROUP * LANES)
            c = cells(contrast, h, n * GROUP + part * (GROUP // 2), GROUP // 2)
        hot = oh[h, n, :, at]
        terms = [hot]
        power = c
        for q in range(3):
            high, low = split(power)
            both = jnp.concatenate([high.astype(F32), low.astype(F32)], axis=0).astype(BF16)
            terms.append(jnp.concatenate([both] * 4, axis=0) * hot)
            power = power * c
        acc[...] += lax.dot_general(
            rh[h, n, :, at], jnp.concatenate(terms, axis=0), (((1,), (1,)), ((), ())),
            preferred_element_type=F32,
        )

    def histogram(h, first, last):
        def step(n, unused):
            add_group(h, n)
            return unused

        lax.fori_loop(first, last, step, 0, unroll=min(2, last - first))

    def ypass(h, i):
        both = jnp.concatenate(
            [yb[h, f, pl.ds(i * 4, 4)].reshape(4 * (Y + 2 * W), LANES) for f in range(2)], axis=1
        )
        high, low = split(both)
        kh = kyhi[...]
        return dot(kh, high) + dot(kylo[...], high) + dot(kh, low)

    def xpass(h, t):
        ys = pl.ds(t * 8, 8)
        both = jnp.concatenate(
            [xb[h, f, :, ys].reshape((X + 2 * W) * 8, LANES) for f in range(2)], axis=1
        )
        high, low = split(both)
        kh = kxhi[...]
        return dot(kh, high) + dot(kxlo[...], high) + dot(kh, low)

    def contrast_of(val, m, alpha):
        nbar = alpha * val[:, LANES:]
        return m * ((val[:, :LANES] - nbar) / (nbar * (1.0 + 2.0 * nbar)))

    def yown(i, unused):
        val = ypass(1, i)
        for f in range(2):
            xb[1, f, pl.ds(W + i * 4, 4)] = val[:, f * LANES:(f + 1) * LANES].reshape(4, Y, LANES)
        return unused

    def first_of(t):
        xarrived(0, t)
        val = xpass(0, t)
        for f in range(2):
            yb[0, f, :, pl.ds(W + t * 8, 8)] = val[:, f * LANES:(f + 1) * LANES].reshape(X, 8, LANES)
        ystart(0, t)

    for t in range(2, tiles):
        onehots(t - 2)
        relay_on(0, t - 2)
        xstart(0, t)
    for k in (8, 9):
        fetch(k).wait()
    yarrived(1)
    lax.fori_loop(0, X // 4, yown, 0, unroll=2)
    xstart(1, 0)
    tcol[me_c] = add_up(row_totals, trow, rows)
    col_totals = gather_sum("col", cols, tcol, s2, r2)
    for k in (6, 7, 10):
        fetch(k).wait()
    for t in range(tiles):
        first_of(t)
        relay_on(1, t)
        if t + 1 < tiles:
            if t == 0:
                for k in range(1, tiles):
                    xacross(1, k, begin)
            xalong(1, t + 1, begin)
    tot = add_up(col_totals, tcol, cols)
    alpha = jnp.sum(tot[0], keepdims=True) / jnp.sum(tot[1], keepdims=True)

    def half_of(t, upper):
        ys, lanes = pl.ds(t * 8, 8), pl.ds(LANES, LANES)

        @pl.when(jnp.logical_and(upper == 0, me_r > 0))
        def _():
            xcopy(1, True, t).wait_recv()

        @pl.when(jnp.logical_and(upper == 1, me_r < rows - 1))
        def _():
            xcopy(1, False, t).wait_recv()

        first = upper * W
        both = jnp.concatenate(
            [xb[1, f, pl.ds(first, 3 * W), ys].reshape(3 * W * 8, LANES) for f in range(2)], axis=1
        )
        high, low = split(both)
        kh, kl = kxhi[0:W * 8, 0:3 * W * 8], kxlo[0:W * 8, 0:3 * W * 8]
        val = dot(kh, high) + dot(kl, high) + dot(kh, low)
        m = cov[pl.ds(first, W), ys, lanes].astype(F32).reshape(W * 8, LANES)
        contrast[pl.ds(first, W), ys, lanes] = contrast_of(val, m, alpha).reshape(W, 8, LANES)
        add_group(1, t, upper)

    def last_of(h, t):
        lanes = pl.ds(h * LANES, LANES)
        xarrived(h, t)
        val = xpass(h, t)
        m = cov[:, pl.ds(t * 8, 8), lanes].astype(F32).reshape(X * 8, LANES)
        contrast[:, pl.ds(t * 8, 8), lanes] = contrast_of(val, m, alpha).reshape(X, 8, LANES)
        histogram(h, groups * t // tiles, groups * (t + 1) // tiles)

    def cstep(i, unused):
        val = ypass(0, i)
        x4, lanes = pl.ds(i * 4, 4), pl.ds(0, LANES)
        m = cov[x4, :, lanes].astype(F32).reshape(4 * Y, LANES)
        contrast[x4, :, lanes] = contrast_of(val, m, alpha).reshape(4, Y, LANES)
        return unused

    early = lax.rem(me_r, 2)
    late = 1 - early
    last_of(1, 0)
    yarrived(0)
    lax.fori_loop(0, X // 4, cstep, 0, unroll=2)
    histogram(0, 0, groups)
    last_of(1, 1)
    half_of(2, early)
    half_of(3, early)
    half_of(2, late)
    half_of(3, late)

    a = acc[...]
    same = lax.broadcasted_iota(jnp.int32, a.shape, 0) % 8 == lax.broadcasted_iota(jnp.int32, a.shape, 1) % 8
    a = jnp.where(same, a, 0.0).reshape(32, 8, 256).sum(axis=1).T
    terms = []
    for q in range(4):
        for k in range(4):
            at = q * 64 + k * 16
            term = a[at:at + 8] if q == 0 else a[at:at + 8] + a[at + 8:at + 16]
            terms.append(jnp.sum(term, axis=0, keepdims=True))
    mine = jnp.concatenate(
        [jnp.concatenate([terms[4 * q + k] for q in range(4)] + [jnp.zeros((4, 32), F32)], axis=0) for k in range(4)],
        axis=1,
    )
    if rows * cols <= DIRECT:
        me = me_r * cols + me_c
        sall[me] = mine
        copies = []
        for k, (kr, kc) in enumerate(shifts(rows, cols)):
            copy = pltpu.make_async_remote_copy(
                src_ref=sall.at[me, pl.ds(0, 4)],
                dst_ref=sall.at[me, pl.ds(0, 4)],
                send_sem=s3.at[k],
                recv_sem=r3.at[k],
                device_id={"row": lax.rem(me_r + kr, rows), "col": lax.rem(me_c + kc, cols)},
                device_id_type=MESH,
            )
            copy.start()
            copies.append(copy)
        for copy in copies:
            copy.wait_recv()
        sums[...] = jnp.sum(sall[:, 0:4], axis=0) * scale
        for copy in copies:
            copy.wait_send()
    else:
        sall[me_r] = mine
        scol[me_c] = add_up(gather_sum("row", rows, sall, s3, r3), sall, rows)
        whole = add_up(gather_sum("col", cols, scol, s4, r4), scol, cols)
        sums[...] = whole[0:4] * scale

    for h in range(2):
        for t in range(tiles):
            xeach(h, t, lambda copy: copy.wait_send())
            relay(h, t, lambda up: xsecond(h, up, t).wait_send())
        for up in (False, True):
            for part in range(W // 8):
                yeach(h, up, part, lambda copy: copy.wait_send())


def store(contrast, sums, contrast_out, sums_out, sem):
    step = contrast.shape[0] // 1
    copies = [pltpu.make_async_copy(contrast.at[pl.ds(k * step, step)], contrast_out.at[pl.ds(k * step, step)], sem.at[k]) for k in range(1)]
    copies.append(pltpu.make_async_copy(sums, sums_out, sem.at[1]))
    for copy in copies:
        copy.start()
    for copy in copies:
        copy.wait()


def local(galaxy, randoms, coverage, patch):
    rows, cols = lax.axis_size("row"), lax.axis_size("col")
    X, Y, Z = galaxy.shape
    W = RADIUS
    tiles = Y // 8
    groups = X // 2 * tiles // GROUP
    direct = (rows * cols if rows * cols <= DIRECT else rows) - 1
    scale = NPATCH / (X * rows * Y * cols * Z)
    tz = split_np(band(Z, Z, 0).T)
    kx = split_np(np.kron(band(X, X + 2 * W, W), np.eye(8, dtype=np.float32)))
    ky = split_np(np.kron(np.eye(4, dtype=np.float32), band(Y, Y + 2 * W, W)))
    rep = (np.arange(NPATCH)[None, :] % 32 == np.arange(32)[:, None]).astype(np.float32)
    consts = [jnp.asarray(v) for v in (*tz, *kx, *ky, rep)]
    args = (galaxy, randoms, coverage, patch, *consts)
    vmem = pl.BlockSpec(memory_space=pltpu.VMEM)
    dma = pltpu.SemaphoreType.DMA
    contrast, sums = pl.pallas_call(
        functools.partial(kernel, rows, cols, scale),
        out_shape=(
            pltpu.VMEM((X, Y, Z), F32),
            pltpu.VMEM((4, NPATCH), F32),
        ),
        in_specs=[pl.BlockSpec(memory_space=pl.ANY)] * 11,
        out_specs=(vmem, vmem),
        scratch_shapes=[pltpu.VMEM(v.shape, v.dtype) for v in args] + [
            pltpu.VMEM((2, 2, X + 2 * W, Y, LANES), F32),
            pltpu.VMEM((2, 2, X, Y + 2 * W, LANES), F32),
            pltpu.VMEM((256, 256), F32),
            pltpu.VMEM((rows, 2, 8, LANES), F32),
            pltpu.VMEM((cols, 2, 8, LANES), F32),
            pltpu.VMEM((direct + 1, 8, NPATCH), F32),
            pltpu.VMEM((cols, 8, NPATCH), F32),
            pltpu.VMEM((2, tiles // 2, 2, W, 8, LANES), F32),
            pltpu.VMEM((2, groups, 64, 2 * LANES * GROUP), BF16),
            pltpu.VMEM((2, groups, 256, 2 * LANES * GROUP), BF16),
            dma((11, tiles)),
            dma((2, 2, tiles)), dma((2, 2, tiles)), dma((2, 2, W // 8)), dma((2, 2, W // 8)),
            dma((2, tiles // 2)), dma((2, tiles // 2)),
            dma((rows - 1,)), dma((rows - 1,)), dma((cols - 1,)), dma((cols - 1,)),
            dma((direct,)), dma((direct,)), dma((cols - 1,)), dma((cols - 1,)),
        ],
        compiler_params=pltpu.CompilerParams(
            collective_id=0, has_side_effects=True, vmem_limit_bytes=56 * 1024 * 1024
        ),
    )(*args)
    return pl.pallas_call(
        store,
        out_shape=(
            jax.ShapeDtypeStruct((X, Y, Z), F32),
            jax.ShapeDtypeStruct((4, NPATCH), F32),
        ),
        in_specs=[pl.BlockSpec(memory_space=pl.ANY)] * 2,
        out_specs=(pl.BlockSpec(memory_space=pl.ANY),) * 2,
        scratch_shapes=[dma((1 + 1,))],
    )(*(pltpu.with_memory_space_constraint(v, pltpu.VMEM) for v in (contrast, sums)))


def solution(mesh):
    spec = P("row", "col", None)
    return jax.shard_map(
        local, mesh=mesh, in_specs=(spec,) * 4, out_specs=(spec, P()), check_vma=False
    )
```

```python
import functools

import jax
import jax.numpy as jnp
import ml_dtypes
import numpy as np
from jax import lax
from jax.experimental import pallas as pl
from jax.experimental.pallas import tpu as pltpu
from jax.sharding import PartitionSpec as P

RADIUS = 16
NPATCH = 128
LANES = 128
GROUP = 16
DIRECT = 32
F32 = jnp.float32
BF16 = jnp.bfloat16
MESH = pl.DeviceIdType.MESH


def taps_np():
    offs = np.arange(-RADIUS, RADIUS + 1).astype(np.float32)
    sigma = RADIUS / 2.0
    vals = np.exp(-offs * offs / np.float32(2.0 * sigma * sigma)).astype(np.float32)
    return (vals / vals.sum(dtype=np.float32)).astype(np.float32)


def split_np(mat):
    high = mat.astype(ml_dtypes.bfloat16)
    low = (mat - high.astype(np.float32)).astype(ml_dtypes.bfloat16)
    return high, low


def band(outs, ins, shift):
    taps = taps_np()
    mat = np.zeros((outs, ins), np.float32)
    for o in range(outs):
        for j in range(-RADIUS, RADIUS + 1):
            i = o + j + shift
            if 0 <= i < ins:
                mat[o, i] = taps[j + RADIUS]
    return mat


def split(val):
    high = val.astype(BF16)
    low = (val - high.astype(F32)).astype(BF16)
    return high, low


def dot(a, b):
    return jnp.dot(a, b, preferred_element_type=F32)


def gather_sum(axis, size, buf, send, recv):
    me = lax.axis_index(axis)
    copies = []
    for k in range(1, size):
        copy = pltpu.make_async_remote_copy(
            src_ref=buf.at[me],
            dst_ref=buf.at[me],
            send_sem=send.at[k - 1],
            recv_sem=recv.at[k - 1],
            device_id={axis: lax.rem(me + k, size)},
            device_id_type=MESH,
        )
        copy.start()
        copies.append(copy)
    return copies


def add_up(copies, buf, size):
    for copy in copies:
        copy.wait()
    total = buf[0]
    for k in range(1, size):
        total = total + buf[k]
    return total


def shifts(rows, cols):
    pairs = [(r, c) for r in range(rows) for c in range(cols) if (r, c) != (0, 0)]
    return sorted(pairs, key=lambda rc: -(min(rc[0], 1) + min(rc[1], cols - rc[1])))


def kernel(
    rows, cols, scale,
    *refs,
):
    hbm, (contrast, sums), vmem = refs[:11], refs[11:13], refs[13:24]
    (
        xb, yb, acc, trow, tcol, sall, scol, rb, oh, rh, sin,
        sx, rx, sy, ry, srel, rrel, s1, r1, s2, r2, s3, r3, s4, r4,
    ) = refs[24:]
    gal, ran, cov, pat, thi, tlo, kxhi, kxlo, kyhi, kylo, rep = vmem
    X, Y, Z = gal.shape
    W = RADIUS
    tiles = Y // 8
    me_r = lax.axis_index("row")
    me_c = lax.axis_index("col")

    def fetch(k, t=None):
        at = slice(None) if t is None else (slice(None), pl.ds(t * 8, 8))
        return pltpu.make_async_copy(hbm[k].at[at], vmem[k].at[at], sin.at[k, t or 0])

    barrier = pltpu.get_barrier_semaphore()
    for k in range(1, rows):
        pl.semaphore_signal(barrier, inc=1, device_id={"row": lax.rem(me_r + k, rows)}, device_id_type=MESH)
    for k in range(1, cols):
        pl.semaphore_signal(barrier, inc=1, device_id={"col": lax.rem(me_c + k, cols)}, device_id_type=MESH)

    fetch(0, 0).start()
    fetch(1, 0).start()
    fetch(4).start()
    fetch(5).start()
    for t in range(1, tiles):
        fetch(0, t).start()
        fetch(1, t).start()
    for k in (2, 3, 8, 9, 6, 7, 10):
        fetch(k).start()
    fetch(4).wait()
    fetch(5).wait()

    relayed = rows == 4
    detour = tiles // 2 if relayed else 0

    def xsrc(h, up, t):
        return xb.at[h, :, pl.ds(X if up else W, W), pl.ds(t * 8, 8)]

    def xdst(h, up, t):
        return xb.at[h, :, pl.ds(0 if up else X + W, W), pl.ds(t * 8, 8)]

    def xsend(src, dst, ssem, rsem, hop):
        return pltpu.make_async_remote_copy(
            src_ref=src, dst_ref=dst, send_sem=ssem, recv_sem=rsem,
            device_id={"row": lax.rem(me_r + (hop + rows), rows)}, device_id_type=MESH,
        )

    def xcopy(h, up, t):
        u = int(up)
        return xsend(xsrc(h, up, t), xdst(h, up, t), sx.at[h, u, t], rx.at[h, u, t], 1 if up else -1)

    def xfirst(h, up, t):
        return xsend(xsrc(h, up, t), rb.at[h, t], sx.at[h, int(up), t], rrel.at[h, t], 2 if up else -2)

    def xsecond(h, up, t):
        return xsend(rb.at[h, t], xdst(h, up, t), srel.at[h, t], rx.at[h, int(up), t], -1 if up else 1)

    def xacross(h, t, act):
        for up in (False, True):
            if relayed:
                @pl.when(me_r == (1 if up else 2))
                def _():
                    act((xfirst if t < detour else xcopy)(h, up, t))

    def xalong(h, t, act):
        for up in (False, True):
            has = me_r < rows - 1 if up else me_r > 0
            if relayed:
                has = jnp.logical_and(has, me_r != (1 if up else 2))

            @pl.when(has)
            def _():
                act(xcopy(h, up, t))

    def relay(h, t, act):
        if t < detour:
            for up in (False, True):
                @pl.when(me_r == (3 if up else 0))
                def _():
                    act(up)

    def relay_on(h, t):
        def go(up):
            xfirst(h, up, t).wait_recv()
            xsecond(h, up, t).start()

        relay(h, t, go)

    def xarrived(h, t):
        @pl.when(me_r > 0)
        def _():
            xcopy(h, True, t).wait_recv()

        @pl.when(me_r < rows - 1)
        def _():
            xcopy(h, False, t).wait_recv()

    def ycopy(h, up, part):
        own, far = ((Y, 0) if up else (W, Y + W))
        return pltpu.make_async_remote_copy(
            src_ref=yb.at[h, :, :, pl.ds(own + 8 * part, 8)],
            dst_ref=yb.at[h, :, :, pl.ds(far + 8 * part, 8)],
            send_sem=sy.at[h, int(up), part],
            recv_sem=ry.at[h, int(up), part],
            device_id={"col": lax.rem(me_c + (1 if up else cols - 1), cols)},
            device_id_type=MESH,
        )

    def yeach(h, up, part, act):
        @pl.when(me_c < cols - 1 if up else me_c > 0)
        def _():
            act(ycopy(h, up, part))

    def ystart(h, t):
        for up in (False, True):
            part = t - (tiles - W // 8 if up else 0)
            if 0 <= part < W // 8:
                yeach(h, up, part, lambda copy: copy.start())

    def yarrived(h):
        for part in range(W // 8):
            @pl.when(me_c > 0)
            def _():
                ycopy(h, True, part).wait_recv()

            @pl.when(me_c < cols - 1)
            def _():
                ycopy(h, False, part).wait_recv()

    def xeach(h, t, act):
        xacross(h, t, act)
        xalong(h, t, act)

    def begin(copy):
        copy.start()

    def xstart(h, t):
        xeach(h, t, begin)

    for t in range(tiles):
        fetch(0, t).wait()
        fetch(1, t).wait()
        for f, ref in enumerate((gal, ran)):
            high, low = split(ref[:, pl.ds(t * 8, 8)].reshape(X * 8, Z))
            val = dot(high, thi[...]) + dot(high, tlo[...]) + dot(low, thi[...])
            xb[0, f, pl.ds(W, X), pl.ds(t * 8, 8)] = val[:, :LANES].reshape(X, 8, LANES)
            yb[1, f, :, pl.ds(W + t * 8, 8)] = val[:, LANES:].reshape(X, 8, LANES)
        if t == 0:
            pl.semaphore_wait(barrier, rows + cols - 2)
        if t < 2:
            xstart(0, t)
        ystart(1, t)

    for h in range(2):
        @pl.when(me_r == 0)
        def _():
            xb[h, :, 0:W] = jnp.zeros((2, W, Y, LANES), F32)

        @pl.when(me_r == rows - 1)
        def _():
            xb[h, :, X + W:] = jnp.zeros((2, W, Y, LANES), F32)

        @pl.when(me_c == 0)
        def _():
            yb[h, :, :, 0:W] = jnp.zeros((2, X, W, LANES), F32)

        @pl.when(me_c == cols - 1)
        def _():
            yb[h, :, :, Y + W:] = jnp.zeros((2, X, W, LANES), F32)

    for k in (2, 3):
        fetch(k).wait()

    def tstep(i, carry):
        m = cov[i].astype(F32)
        g = (m * gal[i]).reshape(Y // 8, 8, Z).sum(axis=0)
        r = (m * ran[i]).reshape(Y // 8, 8, Z).sum(axis=0)
        return carry[0] + g, carry[1] + r

    zero = jnp.zeros((8, Z), F32)
    tg, tr = lax.fori_loop(0, X, tstep, (zero, zero))
    for f, t in enumerate((tg, tr)):
        trow[me_r, f] = sum(t[:, k * LANES:(k + 1) * LANES] for k in range(Z // LANES))
    row_totals = gather_sum("row", rows, trow, s1, r1)

    acc[...] = jnp.zeros_like(acc)
    groups = X // 2 * tiles // GROUP

    def members(h, first, count):
        for k in range(count):
            i = first + k
            yield (i // tiles, i % tiles) if h == 0 else (i % (X // 2), i // (X // 2))

    def cells(ref, h, first, count=GROUP):
        parts = []
        for lx, t in members(h, first, count):
            at = pl.ds(pl.multiple_of(t * 8, 8), 8), pl.ds(h * LANES, LANES)
            parts += [ref[(2 * lx, *at)], ref[(2 * lx + 1, *at)]]
        return jnp.concatenate(parts, axis=1)

    def onehots(h):
        def step(n, unused):
            p = jnp.where(cells(cov, h, n * GROUP) > 0, cells(pat, h, n * GROUP), -1)
            phi, plo = p >> 5, p & 31

            def rows_of(a, b):
                return jnp.concatenate([a, b], axis=0).astype(BF16)

            def one(v, k):
                return jnp.where(v == k, 1.0, 0.0)

            for k in range(4):
                hit = one(phi, k)
                oh[h, n, pl.ds(16 * k, 16)] = rows_of(hit, hit)
            for k in range(16):
                rh[h, n, pl.ds(16 * k, 16)] = rows_of(one(plo, 2 * k), one(plo, 2 * k + 1))
            return unused

        lax.fori_loop(0, groups, step, 0)

    def add_group(h, n, part=None):
        if part is None:
            at = slice(None)
            c = cells(contrast, h, n * GROUP)
        else:
            at = pl.ds(pl.multiple_of(part * GROUP * LANES, GROUP * LANES), GROUP * LANES)
            c = cells(contrast, h, n * GROUP + part * (GROUP // 2), GROUP // 2)
        hot = oh[h, n, :, at]
        terms = [hot]
        power = c
        for q in range(3):
            high, low = split(power)
            both = jnp.concatenate([high.astype(F32), low.astype(F32)], axis=0).astype(BF16)
            terms.append(jnp.concatenate([both] * 4, axis=0) * hot)
            power = power * c
        acc[...] += lax.dot_general(
            rh[h, n, :, at], jnp.concatenate(terms, axis=0), (((1,), (1,)), ((), ())),
            preferred_element_type=F32,
        )

    def histogram(h, first, last):
        def step(n, unused):
            add_group(h, n)
            return unused

        lax.fori_loop(first, last, step, 0, unroll=min(2, last - first))

    def ypass(h, i):
        both = jnp.concatenate(
            [yb[h, f, pl.ds(i * 4, 4)].reshape(4 * (Y + 2 * W), LANES) for f in range(2)], axis=1
        )
        high, low = split(both)
        kh = kyhi[...]
        return dot(kh, high) + dot(kylo[...], high) + dot(kh, low)

    def xpass(h, t):
        ys = pl.ds(t * 8, 8)
        both = jnp.concatenate(
            [xb[h, f, :, ys].reshape((X + 2 * W) * 8, LANES) for f in range(2)], axis=1
        )
        high, low = split(both)
        kh = kxhi[...]
        return dot(kh, high) + dot(kxlo[...], high) + dot(kh, low)

    def contrast_of(val, m, alpha):
        nbar = alpha * val[:, LANES:]
        return m * ((val[:, :LANES] - nbar) / (nbar * (1.0 + 2.0 * nbar)))

    def yown(i, unused):
        val = ypass(1, i)
        for f in range(2):
            xb[1, f, pl.ds(W + i * 4, 4)] = val[:, f * LANES:(f + 1) * LANES].reshape(4, Y, LANES)
        return unused

    def first_of(t):
        xarrived(0, t)
        val = xpass(0, t)
        for f in range(2):
            yb[0, f, :, pl.ds(W + t * 8, 8)] = val[:, f * LANES:(f + 1) * LANES].reshape(X, 8, LANES)
        ystart(0, t)

    for t in range(2, tiles):
        onehots(t - 2)
        relay_on(0, t - 2)
        xstart(0, t)
    for k in (8, 9):
        fetch(k).wait()
    yarrived(1)
    lax.fori_loop(0, X // 4, yown, 0, unroll=2)
    xstart(1, 0)
    tcol[me_c] = add_up(row_totals, trow, rows)
    col_totals = gather_sum("col", cols, tcol, s2, r2)
    for k in (6, 7, 10):
        fetch(k).wait()
    for t in range(tiles):
        first_of(t)
        relay_on(1, t)
        if t + 1 < tiles:
            if t == 0:
                for k in range(1, tiles):
                    xacross(1, k, begin)
            xalong(1, t + 1, begin)
    tot = add_up(col_totals, tcol, cols)
    alpha = jnp.sum(tot[0], keepdims=True) / jnp.sum(tot[1], keepdims=True)

    def half_of(t, upper):
        ys, lanes = pl.ds(t * 8, 8), pl.ds(LANES, LANES)

        @pl.when(jnp.logical_and(upper == 0, me_r > 0))
        def _():
            xcopy(1, True, t).wait_recv()

        @pl.when(jnp.logical_and(upper == 1, me_r < rows - 1))
        def _():
            xcopy(1, False, t).wait_recv()

        first = upper * W
        both = jnp.concatenate(
            [xb[1, f, pl.ds(first, 3 * W), ys].reshape(3 * W * 8, LANES) for f in range(2)], axis=1
        )
        high, low = split(both)
        kh, kl = kxhi[0:W * 8, 0:3 * W * 8], kxlo[0:W * 8, 0:3 * W * 8]
        val = dot(kh, high) + dot(kl, high) + dot(kh, low)
        m = cov[pl.ds(first, W), ys, lanes].astype(F32).reshape(W * 8, LANES)
        contrast[pl.ds(first, W), ys, lanes] = contrast_of(val, m, alpha).reshape(W, 8, LANES)
        add_group(1, t, upper)

    def last_of(h, t):
        lanes = pl.ds(h * LANES, LANES)
        xarrived(h, t)
        val = xpass(h, t)
        m = cov[:, pl.ds(t * 8, 8), lanes].astype(F32).reshape(X * 8, LANES)
        contrast[:, pl.ds(t * 8, 8), lanes] = contrast_of(val, m, alpha).reshape(X, 8, LANES)
        histogram(h, groups * t // tiles, groups * (t + 1) // tiles)

    def cstep(i, unused):
        val = ypass(0, i)
        x4, lanes = pl.ds(i * 4, 4), pl.ds(0, LANES)
        m = cov[x4, :, lanes].astype(F32).reshape(4 * Y, LANES)
        contrast[x4, :, lanes] = contrast_of(val, m, alpha).reshape(4, Y, LANES)
        return unused

    early = lax.rem(me_r, 2)
    late = 1 - early
    last_of(1, 0)
    yarrived(0)
    lax.fori_loop(0, X // 4, cstep, 0, unroll=2)
    histogram(0, 0, groups)
    last_of(1, 1)
    half_of(2, early)
    half_of(3, early)
    half_of(2, late)
    half_of(3, late)

    a = acc[...]
    same = lax.broadcasted_iota(jnp.int32, a.shape, 0) % 8 == lax.broadcasted_iota(jnp.int32, a.shape, 1) % 8
    a = jnp.where(same, a, 0.0).reshape(32, 8, 256).sum(axis=1).T
    terms = []
    for q in range(4):
        for k in range(4):
            at = q * 64 + k * 16
            term = a[at:at + 8] if q == 0 else a[at:at + 8] + a[at + 8:at + 16]
            terms.append(jnp.sum(term, axis=0, keepdims=True))
    mine = jnp.concatenate(
        [jnp.concatenate([terms[4 * q + k] for q in range(4)] + [jnp.zeros((4, 32), F32)], axis=0) for k in range(4)],
        axis=1,
    )
    def drain():
        for h in range(2):
            for t in range(tiles):
                xeach(h, t, lambda copy: copy.wait_send())
                relay(h, t, lambda up: xsecond(h, up, t).wait_send())
            for up in (False, True):
                for part in range(W // 8):
                    yeach(h, up, part, lambda copy: copy.wait_send())

    if rows * cols <= DIRECT:
        me = me_r * cols + me_c
        sall[me] = mine
        copies = []
        for k, (kr, kc) in enumerate(shifts(rows, cols)):
            copy = pltpu.make_async_remote_copy(
                src_ref=sall.at[me, pl.ds(0, 4)],
                dst_ref=sall.at[me, pl.ds(0, 4)],
                send_sem=s3.at[k],
                recv_sem=r3.at[k],
                device_id={"row": lax.rem(me_r + kr, rows), "col": lax.rem(me_c + kc, cols)},
                device_id_type=MESH,
            )
            copy.start()
            copies.append(copy)
        drain()
        for copy in copies:
            copy.wait_send()
        for copy in copies:
            copy.wait_recv()
        sums[...] = jnp.sum(sall[:, 0:4], axis=0) * scale
    else:
        drain()
        sall[me_r] = mine
        scol[me_c] = add_up(gather_sum("row", rows, sall, s3, r3), sall, rows)
        whole = add_up(gather_sum("col", cols, scol, s4, r4), scol, cols)
        sums[...] = whole[0:4] * scale


def store(contrast, sums, contrast_out, sums_out, sem):
    step = contrast.shape[0] // 1
    copies = [pltpu.make_async_copy(contrast.at[pl.ds(k * step, step)], contrast_out.at[pl.ds(k * step, step)], sem.at[k]) for k in range(1)]
    copies.append(pltpu.make_async_copy(sums, sums_out, sem.at[1]))
    for copy in copies:
        copy.start()
    for copy in copies:
        copy.wait()


def local(galaxy, randoms, coverage, patch):
    rows, cols = lax.axis_size("row"), lax.axis_size("col")
    X, Y, Z = galaxy.shape
    W = RADIUS
    tiles = Y // 8
    groups = X // 2 * tiles // GROUP
    direct = (rows * cols if rows * cols <= DIRECT else rows) - 1
    scale = NPATCH / (X * rows * Y * cols * Z)
    tz = split_np(band(Z, Z, 0).T)
    kx = split_np(np.kron(band(X, X + 2 * W, W), np.eye(8, dtype=np.float32)))
    ky = split_np(np.kron(np.eye(4, dtype=np.float32), band(Y, Y + 2 * W, W)))
    rep = (np.arange(NPATCH)[None, :] % 32 == np.arange(32)[:, None]).astype(np.float32)
    consts = [jnp.asarray(v) for v in (*tz, *kx, *ky, rep)]
    args = (galaxy, randoms, coverage, patch, *consts)
    vmem = pl.BlockSpec(memory_space=pltpu.VMEM)
    dma = pltpu.SemaphoreType.DMA
    contrast, sums = pl.pallas_call(
        functools.partial(kernel, rows, cols, scale),
        out_shape=(
            pltpu.VMEM((X, Y, Z), F32),
            pltpu.VMEM((4, NPATCH), F32),
        ),
        in_specs=[pl.BlockSpec(memory_space=pl.ANY)] * 11,
        out_specs=(vmem, vmem),
        scratch_shapes=[pltpu.VMEM(v.shape, v.dtype) for v in args] + [
            pltpu.VMEM((2, 2, X + 2 * W, Y, LANES), F32),
            pltpu.VMEM((2, 2, X, Y + 2 * W, LANES), F32),
            pltpu.VMEM((256, 256), F32),
            pltpu.VMEM((rows, 2, 8, LANES), F32),
            pltpu.VMEM((cols, 2, 8, LANES), F32),
            pltpu.VMEM((direct + 1, 8, NPATCH), F32),
            pltpu.VMEM((cols, 8, NPATCH), F32),
            pltpu.VMEM((2, tiles // 2, 2, W, 8, LANES), F32),
            pltpu.VMEM((2, groups, 64, 2 * LANES * GROUP), BF16),
            pltpu.VMEM((2, groups, 256, 2 * LANES * GROUP), BF16),
            dma((11, tiles)),
            dma((2, 2, tiles)), dma((2, 2, tiles)), dma((2, 2, W // 8)), dma((2, 2, W // 8)),
            dma((2, tiles // 2)), dma((2, tiles // 2)),
            dma((rows - 1,)), dma((rows - 1,)), dma((cols - 1,)), dma((cols - 1,)),
            dma((direct,)), dma((direct,)), dma((cols - 1,)), dma((cols - 1,)),
        ],
        compiler_params=pltpu.CompilerParams(
            collective_id=0, has_side_effects=True, vmem_limit_bytes=56 * 1024 * 1024
        ),
    )(*args)
    return pl.pallas_call(
        store,
        out_shape=(
            jax.ShapeDtypeStruct((X, Y, Z), F32),
            jax.ShapeDtypeStruct((4, NPATCH), F32),
        ),
        in_specs=[pl.BlockSpec(memory_space=pl.ANY)] * 2,
        out_specs=(pl.BlockSpec(memory_space=pl.ANY),) * 2,
        scratch_shapes=[dma((1 + 1,))],
    )(*(pltpu.with_memory_space_constraint(v, pltpu.VMEM) for v in (contrast, sums)))


def solution(mesh):
    spec = P("row", "col", None)
    return jax.shard_map(
        local, mesh=mesh, in_specs=(spec,) * 4, out_specs=(spec, P()), check_vma=False
    )
```

```python
import functools

import jax
import jax.numpy as jnp
import ml_dtypes
import numpy as np
from jax import lax
from jax.experimental import pallas as pl
from jax.experimental.pallas import tpu as pltpu
from jax.sharding import PartitionSpec as P

RADIUS = 16
NPATCH = 128
LANES = 128
GROUP = 16
DIRECT = 32
F32 = jnp.float32
BF16 = jnp.bfloat16
MESH = pl.DeviceIdType.MESH


def taps_np():
    offs = np.arange(-RADIUS, RADIUS + 1).astype(np.float32)
    sigma = RADIUS / 2.0
    vals = np.exp(-offs * offs / np.float32(2.0 * sigma * sigma)).astype(np.float32)
    return (vals / vals.sum(dtype=np.float32)).astype(np.float32)


def split_np(mat):
    high = mat.astype(ml_dtypes.bfloat16)
    low = (mat - high.astype(np.float32)).astype(ml_dtypes.bfloat16)
    return high, low


def band(outs, ins, shift):
    taps = taps_np()
    mat = np.zeros((outs, ins), np.float32)
    for o in range(outs):
        for j in range(-RADIUS, RADIUS + 1):
            i = o + j + shift
            if 0 <= i < ins:
                mat[o, i] = taps[j + RADIUS]
    return mat


def split(val):
    high = val.astype(BF16)
    low = (val - high.astype(F32)).astype(BF16)
    return high, low


def dot(a, b):
    return jnp.dot(a, b, preferred_element_type=F32)


def gather_sum(axis, size, buf, send, recv):
    me = lax.axis_index(axis)
    copies = []
    for k in range(1, size):
        copy = pltpu.make_async_remote_copy(
            src_ref=buf.at[me],
            dst_ref=buf.at[me],
            send_sem=send.at[k - 1],
            recv_sem=recv.at[k - 1],
            device_id={axis: lax.rem(me + k, size)},
            device_id_type=MESH,
        )
        copy.start()
        copies.append(copy)
    return copies


def add_up(copies, buf, size):
    for copy in copies:
        copy.wait()
    total = buf[0]
    for k in range(1, size):
        total = total + buf[k]
    return total


def shifts(rows, cols):
    pairs = [(r, c) for r in range(rows) for c in range(cols) if (r, c) != (0, 0)]
    return sorted(pairs, key=lambda rc: -(min(rc[0], 1) + min(rc[1], cols - rc[1])))


def kernel(
    rows, cols, scale,
    *refs,
):
    hbm, (contrast, sums), vmem = refs[:11], refs[11:13], refs[13:24]
    (
        xb, yb, acc, trow, tcol, sall, scol, rb, oh, rh, sin,
        sx, rx, sy, ry, srel, rrel, s1, r1, s2, r2, s3, r3, s4, r4,
    ) = refs[24:]
    gal, ran, cov, pat, thi, tlo, kxhi, kxlo, kyhi, kylo, rep = vmem
    X, Y, Z = gal.shape
    W = RADIUS
    tiles = Y // 8
    me_r = lax.axis_index("row")
    me_c = lax.axis_index("col")

    def fetch(k, t=None):
        at = slice(None) if t is None else (slice(None), pl.ds(t * 8, 8))
        return pltpu.make_async_copy(hbm[k].at[at], vmem[k].at[at], sin.at[k, t or 0])

    fetch(0, 0).start()
    fetch(1, 0).start()
    fetch(4).start()
    fetch(5).start()
    for t in range(1, tiles):
        fetch(0, t).start()
        fetch(1, t).start()
    for k in (2, 3, 8, 9, 6, 7, 10):
        fetch(k).start()

    barrier = pltpu.get_barrier_semaphore()
    for k in range(1, rows):
        pl.semaphore_signal(barrier, inc=1, device_id={"row": lax.rem(me_r + k, rows)}, device_id_type=MESH)
    for k in range(1, cols):
        pl.semaphore_signal(barrier, inc=1, device_id={"col": lax.rem(me_c + k, cols)}, device_id_type=MESH)
    fetch(4).wait()
    fetch(5).wait()

    relayed = rows == 4
    detour = tiles // 2 if relayed else 0

    def xsrc(h, up, t):
        return xb.at[h, :, pl.ds(X if up else W, W), pl.ds(t * 8, 8)]

    def xdst(h, up, t):
        return xb.at[h, :, pl.ds(0 if up else X + W, W), pl.ds(t * 8, 8)]

    def xsend(src, dst, ssem, rsem, hop):
        return pltpu.make_async_remote_copy(
            src_ref=src, dst_ref=dst, send_sem=ssem, recv_sem=rsem,
            device_id={"row": lax.rem(me_r + (hop + rows), rows)}, device_id_type=MESH,
        )

    def xcopy(h, up, t):
        u = int(up)
        return xsend(xsrc(h, up, t), xdst(h, up, t), sx.at[h, u, t], rx.at[h, u, t], 1 if up else -1)

    def xfirst(h, up, t):
        return xsend(xsrc(h, up, t), rb.at[h, t], sx.at[h, int(up), t], rrel.at[h, t], 2 if up else -2)

    def xsecond(h, up, t):
        return xsend(rb.at[h, t], xdst(h, up, t), srel.at[h, t], rx.at[h, int(up), t], -1 if up else 1)

    def xacross(h, t, act):
        for up in (False, True):
            if relayed:
                @pl.when(me_r == (1 if up else 2))
                def _():
                    act((xfirst if t < detour else xcopy)(h, up, t))

    def xalong(h, t, act):
        for up in (False, True):
            has = me_r < rows - 1 if up else me_r > 0
            if relayed:
                has = jnp.logical_and(has, me_r != (1 if up else 2))

            @pl.when(has)
            def _():
                act(xcopy(h, up, t))

    def relay(h, t, act):
        if t < detour:
            for up in (False, True):
                @pl.when(me_r == (3 if up else 0))
                def _():
                    act(up)

    def relay_on(h, t):
        def go(up):
            xfirst(h, up, t).wait_recv()
            xsecond(h, up, t).start()

        relay(h, t, go)

    def xarrived(h, t):
        @pl.when(me_r > 0)
        def _():
            xcopy(h, True, t).wait_recv()

        @pl.when(me_r < rows - 1)
        def _():
            xcopy(h, False, t).wait_recv()

    def ycopy(h, up, part):
        own, far = ((Y, 0) if up else (W, Y + W))
        return pltpu.make_async_remote_copy(
            src_ref=yb.at[h, :, :, pl.ds(own + 8 * part, 8)],
            dst_ref=yb.at[h, :, :, pl.ds(far + 8 * part, 8)],
            send_sem=sy.at[h, int(up), part],
            recv_sem=ry.at[h, int(up), part],
            device_id={"col": lax.rem(me_c + (1 if up else cols - 1), cols)},
            device_id_type=MESH,
        )

    def yeach(h, up, part, act):
        @pl.when(me_c < cols - 1 if up else me_c > 0)
        def _():
            act(ycopy(h, up, part))

    def ystart(h, t):
        for up in (False, True):
            part = t - (tiles - W // 8 if up else 0)
            if 0 <= part < W // 8:
                yeach(h, up, part, lambda copy: copy.start())

    def yarrived(h):
        for part in range(W // 8):
            @pl.when(me_c > 0)
            def _():
                ycopy(h, True, part).wait_recv()

            @pl.when(me_c < cols - 1)
            def _():
                ycopy(h, False, part).wait_recv()

    def xeach(h, t, act):
        xacross(h, t, act)
        xalong(h, t, act)

    def begin(copy):
        copy.start()

    def xstart(h, t):
        xeach(h, t, begin)

    for t in range(tiles):
        fetch(0, t).wait()
        fetch(1, t).wait()
        for f, ref in enumerate((gal, ran)):
            high, low = split(ref[:, pl.ds(t * 8, 8)].reshape(X * 8, Z))
            val = dot(high, thi[...]) + dot(high, tlo[...]) + dot(low, thi[...])
            xb[0, f, pl.ds(W, X), pl.ds(t * 8, 8)] = val[:, :LANES].reshape(X, 8, LANES)
            yb[1, f, :, pl.ds(W + t * 8, 8)] = val[:, LANES:].reshape(X, 8, LANES)
        if t == 0:
            pl.semaphore_wait(barrier, rows + cols - 2)
        if t < 2:
            xstart(0, t)
        ystart(1, t)

    for h in range(2):
        @pl.when(me_r == 0)
        def _():
            xb[h, :, 0:W] = jnp.zeros((2, W, Y, LANES), F32)

        @pl.when(me_r == rows - 1)
        def _():
            xb[h, :, X + W:] = jnp.zeros((2, W, Y, LANES), F32)

        @pl.when(me_c == 0)
        def _():
            yb[h, :, :, 0:W] = jnp.zeros((2, X, W, LANES), F32)

        @pl.when(me_c == cols - 1)
        def _():
            yb[h, :, :, Y + W:] = jnp.zeros((2, X, W, LANES), F32)

    for t in range(2, tiles):
        xacross(0, t, begin)
    for k in (2, 3):
        fetch(k).wait()

    def tstep(i, carry):
        m = cov[i].astype(F32)
        g = (m * gal[i]).reshape(Y // 8, 8, Z).sum(axis=0)
        r = (m * ran[i]).reshape(Y // 8, 8, Z).sum(axis=0)
        return carry[0] + g, carry[1] + r

    zero = jnp.zeros((8, Z), F32)
    tg, tr = lax.fori_loop(0, X, tstep, (zero, zero))
    for f, t in enumerate((tg, tr)):
        trow[me_r, f] = sum(t[:, k * LANES:(k + 1) * LANES] for k in range(Z // LANES))
    row_totals = gather_sum("row", rows, trow, s1, r1)

    acc[...] = jnp.zeros_like(acc)
    groups = X // 2 * tiles // GROUP

    def members(h, first, count):
        for k in range(count):
            i = first + k
            yield (i // tiles, i % tiles) if h == 0 else (i % (X // 2), i // (X // 2))

    def cells(ref, h, first, count=GROUP):
        parts = []
        for lx, t in members(h, first, count):
            at = pl.ds(pl.multiple_of(t * 8, 8), 8), pl.ds(h * LANES, LANES)
            parts += [ref[(2 * lx, *at)], ref[(2 * lx + 1, *at)]]
        return jnp.concatenate(parts, axis=1)

    def onehots(h):
        def step(n, unused):
            p = jnp.where(cells(cov, h, n * GROUP) > 0, cells(pat, h, n * GROUP), -1)
            phi, plo = p >> 5, p & 31

            def rows_of(a, b):
                return jnp.concatenate([a, b], axis=0).astype(BF16)

            def one(v, k):
                return jnp.where(v == k, 1.0, 0.0)

            for k in range(4):
                hit = one(phi, k)
                oh[h, n, pl.ds(16 * k, 16)] = rows_of(hit, hit)
            for k in range(16):
                rh[h, n, pl.ds(16 * k, 16)] = rows_of(one(plo, 2 * k), one(plo, 2 * k + 1))
            return unused

        lax.fori_loop(0, groups, step, 0)

    def add_group(h, n, part=None):
        if part is None:
            at = slice(None)
            c = cells(contrast, h, n * GROUP)
        else:
            at = pl.ds(pl.multiple_of(part * GROUP * LANES, GROUP * LANES), GROUP * LANES)
            c = cells(contrast, h, n * GROUP + part * (GROUP // 2), GROUP // 2)
        hot = oh[h, n, :, at]
        terms = [hot]
        power = c
        for q in range(3):
            high, low = split(power)
            both = jnp.concatenate([high.astype(F32), low.astype(F32)], axis=0).astype(BF16)
            terms.append(jnp.concatenate([both] * 4, axis=0) * hot)
            power = power * c
        acc[...] += lax.dot_general(
            rh[h, n, :, at], jnp.concatenate(terms, axis=0), (((1,), (1,)), ((), ())),
            preferred_element_type=F32,
        )

    def histogram(h, first, last):
        def step(n, unused):
            add_group(h, n)
            return unused

        lax.fori_loop(first, last, step, 0, unroll=min(2, last - first))

    def ypass(h, i):
        both = jnp.concatenate(
            [yb[h, f, pl.ds(i * 4, 4)].reshape(4 * (Y + 2 * W), LANES) for f in range(2)], axis=1
        )
        high, low = split(both)
        kh = kyhi[...]
        return dot(kh, high) + dot(kylo[...], high) + dot(kh, low)

    def xpass(h, t):
        ys = pl.ds(t * 8, 8)
        both = jnp.concatenate(
            [xb[h, f, :, ys].reshape((X + 2 * W) * 8, LANES) for f in range(2)], axis=1
        )
        high, low = split(both)
        kh = kxhi[...]
        return dot(kh, high) + dot(kxlo[...], high) + dot(kh, low)

    def contrast_of(val, m, alpha):
        nbar = alpha * val[:, LANES:]
        weight = 1.0 / (1.0 + 2.0 * nbar)
        return m * weight * (val[:, :LANES] / nbar - 1.0)

    def yown(i, unused):
        val = ypass(1, i)
        for f in range(2):
            xb[1, f, pl.ds(W + i * 4, 4)] = val[:, f * LANES:(f + 1) * LANES].reshape(4, Y, LANES)
        return unused

    def first_of(t):
        xarrived(0, t)
        val = xpass(0, t)
        for f in range(2):
            yb[0, f, :, pl.ds(W + t * 8, 8)] = val[:, f * LANES:(f + 1) * LANES].reshape(X, 8, LANES)
        ystart(0, t)

    for t in range(2, tiles):
        onehots(t - 2)
        relay_on(0, t - 2)
        xalong(0, t, begin)
    for k in (8, 9):
        fetch(k).wait()
    yarrived(1)
    lax.fori_loop(0, X // 4, yown, 0, unroll=2)
    xstart(1, 0)
    tcol[me_c] = add_up(row_totals, trow, rows)
    col_totals = gather_sum("col", cols, tcol, s2, r2)
    for k in (6, 7, 10):
        fetch(k).wait()
    for t in range(tiles):
        first_of(t)
        relay_on(1, t)
        if t + 1 < tiles:
            if t == 0:
                for k in range(1, tiles):
                    xacross(1, k, begin)
            xalong(1, t + 1, begin)
    tot = add_up(col_totals, tcol, cols)
    alpha = jnp.sum(tot[0], keepdims=True) / jnp.sum(tot[1], keepdims=True)

    def half_of(t, upper):
        ys, lanes = pl.ds(t * 8, 8), pl.ds(LANES, LANES)

        @pl.when(jnp.logical_and(upper == 0, me_r > 0))
        def _():
            xcopy(1, True, t).wait_recv()

        @pl.when(jnp.logical_and(upper == 1, me_r < rows - 1))
        def _():
            xcopy(1, False, t).wait_recv()

        first = upper * W
        both = jnp.concatenate(
            [xb[1, f, pl.ds(first, 3 * W), ys].reshape(3 * W * 8, LANES) for f in range(2)], axis=1
        )
        high, low = split(both)
        kh, kl = kxhi[0:W * 8, 0:3 * W * 8], kxlo[0:W * 8, 0:3 * W * 8]
        val = dot(kh, high) + dot(kl, high) + dot(kh, low)
        m = cov[pl.ds(first, W), ys, lanes].astype(F32).reshape(W * 8, LANES)
        contrast[pl.ds(first, W), ys, lanes] = contrast_of(val, m, alpha).reshape(W, 8, LANES)
        add_group(1, t, upper)

    def last_of(h, t):
        lanes = pl.ds(h * LANES, LANES)
        xarrived(h, t)
        val = xpass(h, t)
        m = cov[:, pl.ds(t * 8, 8), lanes].astype(F32).reshape(X * 8, LANES)
        contrast[:, pl.ds(t * 8, 8), lanes] = contrast_of(val, m, alpha).reshape(X, 8, LANES)
        histogram(h, groups * t // tiles, groups * (t + 1) // tiles)

    def cstep(i, unused):
        val = ypass(0, i)
        x4, lanes = pl.ds(i * 4, 4), pl.ds(0, LANES)
        m = cov[x4, :, lanes].astype(F32).reshape(4 * Y, LANES)
        contrast[x4, :, lanes] = contrast_of(val, m, alpha).reshape(4, Y, LANES)
        return unused

    yarrived(0)
    lax.fori_loop(0, X // 4, cstep, 0, unroll=2)
    histogram(0, 0, groups)
    early = lax.rem(me_r, 2)
    late = 1 - early
    last_of(1, 0)
    last_of(1, 1)
    half_of(2, early)
    half_of(3, early)
    half_of(2, late)
    half_of(3, late)

    a = acc[...]
    same = lax.broadcasted_iota(jnp.int32, a.shape, 0) % 8 == lax.broadcasted_iota(jnp.int32, a.shape, 1) % 8
    a = jnp.where(same, a, 0.0).reshape(32, 8, 256).sum(axis=1).T
    terms = []
    for q in range(4):
        for k in range(4):
            at = q * 64 + k * 16
            term = a[at:at + 8] if q == 0 else a[at:at + 8] + a[at + 8:at + 16]
            terms.append(jnp.sum(term, axis=0, keepdims=True))
    spread = jnp.dot(
        jnp.concatenate(terms, axis=0), rep[...],
        precision=lax.Precision.HIGHEST, preferred_element_type=F32,
    )
    own = lax.broadcasted_iota(jnp.int32, spread.shape, 1) // 32 == lax.broadcasted_iota(jnp.int32, spread.shape, 0) % 4
    spread = jnp.where(own, spread, 0.0)
    mine = jnp.concatenate(
        [jnp.sum(spread[4 * q:4 * q + 4], axis=0, keepdims=True) for q in range(4)]
        + [jnp.zeros((4, NPATCH), F32)], axis=0,
    )
    if rows * cols <= DIRECT:
        me = me_r * cols + me_c
        sall[me] = mine
        copies = []
        for k, (kr, kc) in enumerate(shifts(rows, cols)):
            copy = pltpu.make_async_remote_copy(
                src_ref=sall.at[me, pl.ds(0, 4)],
                dst_ref=sall.at[me, pl.ds(0, 4)],
                send_sem=s3.at[k],
                recv_sem=r3.at[k],
                device_id={"row": lax.rem(me_r + kr, rows), "col": lax.rem(me_c + kc, cols)},
                device_id_type=MESH,
            )
            copy.start()
            copies.append(copy)
        for copy in copies:
            copy.wait_recv()
        sums[...] = jnp.sum(sall[:, 0:4], axis=0) * scale
        for copy in copies:
            copy.wait_send()
    else:
        sall[me_r] = mine
        scol[me_c] = add_up(gather_sum("row", rows, sall, s3, r3), sall, rows)
        whole = add_up(gather_sum("col", cols, scol, s4, r4), scol, cols)
        sums[...] = whole[0:4] * scale

    for h in range(2):
        for t in range(tiles):
            xeach(h, t, lambda copy: copy.wait_send())
            relay(h, t, lambda up: xsecond(h, up, t).wait_send())
        for up in (False, True):
            for part in range(W // 8):
                yeach(h, up, part, lambda copy: copy.wait_send())


def store(contrast, sums, contrast_out, sums_out, sem):
    step = contrast.shape[0] // 1
    copies = [pltpu.make_async_copy(contrast.at[pl.ds(k * step, step)], contrast_out.at[pl.ds(k * step, step)], sem.at[k]) for k in range(1)]
    copies.append(pltpu.make_async_copy(sums, sums_out, sem.at[1]))
    for copy in copies:
        copy.start()
    for copy in copies:
        copy.wait()


def local(galaxy, randoms, coverage, patch):
    rows, cols = lax.axis_size("row"), lax.axis_size("col")
    X, Y, Z = galaxy.shape
    W = RADIUS
    tiles = Y // 8
    groups = X // 2 * tiles // GROUP
    direct = (rows * cols if rows * cols <= DIRECT else rows) - 1
    scale = NPATCH / (X * rows * Y * cols * Z)
    tz = split_np(band(Z, Z, 0).T)
    kx = split_np(np.kron(band(X, X + 2 * W, W), np.eye(8, dtype=np.float32)))
    ky = split_np(np.kron(np.eye(4, dtype=np.float32), band(Y, Y + 2 * W, W)))
    rep = (np.arange(NPATCH)[None, :] % 32 == np.arange(32)[:, None]).astype(np.float32)
    consts = [jnp.asarray(v) for v in (*tz, *kx, *ky, rep)]
    args = (galaxy, randoms, coverage, patch, *consts)
    vmem = pl.BlockSpec(memory_space=pltpu.VMEM)
    dma = pltpu.SemaphoreType.DMA
    contrast, sums = pl.pallas_call(
        functools.partial(kernel, rows, cols, scale),
        out_shape=(
            pltpu.VMEM((X, Y, Z), F32),
            pltpu.VMEM((4, NPATCH), F32),
        ),
        in_specs=[pl.BlockSpec(memory_space=pl.ANY)] * 11,
        out_specs=(vmem, vmem),
        scratch_shapes=[pltpu.VMEM(v.shape, v.dtype) for v in args] + [
            pltpu.VMEM((2, 2, X + 2 * W, Y, LANES), F32),
            pltpu.VMEM((2, 2, X, Y + 2 * W, LANES), F32),
            pltpu.VMEM((256, 256), F32),
            pltpu.VMEM((rows, 2, 8, LANES), F32),
            pltpu.VMEM((cols, 2, 8, LANES), F32),
            pltpu.VMEM((direct + 1, 8, NPATCH), F32),
            pltpu.VMEM((cols, 8, NPATCH), F32),
            pltpu.VMEM((2, tiles // 2, 2, W, 8, LANES), F32),
            pltpu.VMEM((2, groups, 64, 2 * LANES * GROUP), BF16),
            pltpu.VMEM((2, groups, 256, 2 * LANES * GROUP), BF16),
            dma((11, tiles)),
            dma((2, 2, tiles)), dma((2, 2, tiles)), dma((2, 2, W // 8)), dma((2, 2, W // 8)),
            dma((2, tiles // 2)), dma((2, tiles // 2)),
            dma((rows - 1,)), dma((rows - 1,)), dma((cols - 1,)), dma((cols - 1,)),
            dma((direct,)), dma((direct,)), dma((cols - 1,)), dma((cols - 1,)),
        ],
        compiler_params=pltpu.CompilerParams(
            collective_id=0, has_side_effects=True, vmem_limit_bytes=56 * 1024 * 1024
        ),
    )(*args)
    return pl.pallas_call(
        store,
        out_shape=(
            jax.ShapeDtypeStruct((X, Y, Z), F32),
            jax.ShapeDtypeStruct((4, NPATCH), F32),
        ),
        in_specs=[pl.BlockSpec(memory_space=pl.ANY)] * 2,
        out_specs=(pl.BlockSpec(memory_space=pl.ANY),) * 2,
        scratch_shapes=[dma((1 + 1,))],
    )(*(pltpu.with_memory_space_constraint(v, pltpu.VMEM) for v in (contrast, sums)))


def solution(mesh):
    spec = P("row", "col", None)
    return jax.shard_map(
        local, mesh=mesh, in_specs=(spec,) * 4, out_specs=(spec, P()), check_vma=False
    )
```

```python
import functools

import jax
import jax.numpy as jnp
import ml_dtypes
import numpy as np
from jax import lax
from jax.experimental import pallas as pl
from jax.experimental.pallas import tpu as pltpu
from jax.sharding import PartitionSpec as P

RADIUS = 16
NPATCH = 128
LANES = 128
GROUP = 16
DIRECT = 32
F32 = jnp.float32
BF16 = jnp.bfloat16
MESH = pl.DeviceIdType.MESH


def taps_np():
    offs = np.arange(-RADIUS, RADIUS + 1).astype(np.float32)
    sigma = RADIUS / 2.0
    vals = np.exp(-offs * offs / np.float32(2.0 * sigma * sigma)).astype(np.float32)
    return (vals / vals.sum(dtype=np.float32)).astype(np.float32)


def split_np(mat):
    high = mat.astype(ml_dtypes.bfloat16)
    low = (mat - high.astype(np.float32)).astype(ml_dtypes.bfloat16)
    return high, low


def band(outs, ins, shift):
    taps = taps_np()
    mat = np.zeros((outs, ins), np.float32)
    for o in range(outs):
        for j in range(-RADIUS, RADIUS + 1):
            i = o + j + shift
            if 0 <= i < ins:
                mat[o, i] = taps[j + RADIUS]
    return mat


def split(val):
    high = val.astype(BF16)
    low = (val - high.astype(F32)).astype(BF16)
    return high, low


def dot(a, b):
    return jnp.dot(a, b, preferred_element_type=F32)


def gather_sum(axis, size, buf, send, recv):
    me = lax.axis_index(axis)
    copies = []
    for k in range(1, size):
        copy = pltpu.make_async_remote_copy(
            src_ref=buf.at[me],
            dst_ref=buf.at[me],
            send_sem=send.at[k - 1],
            recv_sem=recv.at[k - 1],
            device_id={axis: lax.rem(me + k, size)},
            device_id_type=MESH,
        )
        copy.start()
        copies.append(copy)
    return copies


def add_up(copies, buf, size):
    for copy in copies:
        copy.wait()
    total = buf[0]
    for k in range(1, size):
        total = total + buf[k]
    return total


def shifts(rows, cols):
    pairs = [(r, c) for r in range(rows) for c in range(cols) if (r, c) != (0, 0)]
    return sorted(pairs, key=lambda rc: -(min(rc[0], 1) + min(rc[1], cols - rc[1])))


def kernel(
    rows, cols, scale,
    *refs,
):
    hbm, (contrast, sums), vmem = refs[:11], refs[11:13], refs[13:24]
    (
        xb, yb, acc, trow, tcol, sall, scol, rb, oh, rh, sin,
        sx, rx, sy, ry, srel, rrel, s1, r1, s2, r2, s3, r3, s4, r4,
    ) = refs[24:]
    gal, ran, cov, pat, thi, tlo, kxhi, kxlo, kyhi, kylo, rep = vmem
    X, Y, Z = gal.shape
    W = RADIUS
    tiles = Y // 8
    me_r = lax.axis_index("row")
    me_c = lax.axis_index("col")

    def fetch(k, t=None):
        at = slice(None) if t is None else (slice(None), pl.ds(t * 8, 8))
        return pltpu.make_async_copy(hbm[k].at[at], vmem[k].at[at], sin.at[k, t or 0])

    barrier = pltpu.get_barrier_semaphore()
    for k in range(1, rows):
        pl.semaphore_signal(barrier, inc=1, device_id={"row": lax.rem(me_r + k, rows)}, device_id_type=MESH)
    for k in range(1, cols):
        pl.semaphore_signal(barrier, inc=1, device_id={"col": lax.rem(me_c + k, cols)}, device_id_type=MESH)

    fetch(0, 0).start()
    fetch(1, 0).start()
    fetch(4).start()
    fetch(5).start()
    for t in range(1, tiles):
        fetch(0, t).start()
        fetch(1, t).start()
    for k in (2, 3, 8, 9, 6, 7, 10):
        fetch(k).start()
    fetch(4).wait()
    fetch(5).wait()

    relayed = rows == 4
    detour = tiles // 2 if relayed else 0

    def xsrc(h, up, t):
        return xb.at[h, :, pl.ds(X if up else W, W), pl.ds(t * 8, 8)]

    def xdst(h, up, t):
        return xb.at[h, :, pl.ds(0 if up else X + W, W), pl.ds(t * 8, 8)]

    def xsend(src, dst, ssem, rsem, hop):
        return pltpu.make_async_remote_copy(
            src_ref=src, dst_ref=dst, send_sem=ssem, recv_sem=rsem,
            device_id={"row": lax.rem(me_r + (hop + rows), rows)}, device_id_type=MESH,
        )

    def xcopy(h, up, t):
        u = int(up)
        return xsend(xsrc(h, up, t), xdst(h, up, t), sx.at[h, u, t], rx.at[h, u, t], 1 if up else -1)

    def xfirst(h, up, t):
        return xsend(xsrc(h, up, t), rb.at[h, t], sx.at[h, int(up), t], rrel.at[h, t], 2 if up else -2)

    def xsecond(h, up, t):
        return xsend(rb.at[h, t], xdst(h, up, t), srel.at[h, t], rx.at[h, int(up), t], -1 if up else 1)

    def xacross(h, t, act):
        for up in (False, True):
            if relayed:
                @pl.when(me_r == (1 if up else 2))
                def _():
                    act((xfirst if t < detour else xcopy)(h, up, t))

    def xalong(h, t, act):
        for up in (False, True):
            has = me_r < rows - 1 if up else me_r > 0
            if relayed:
                has = jnp.logical_and(has, me_r != (1 if up else 2))

            @pl.when(has)
            def _():
                act(xcopy(h, up, t))

    def relay(h, t, act):
        if t < detour:
            for up in (False, True):
                @pl.when(me_r == (3 if up else 0))
                def _():
                    act(up)

    def relay_on(h, t):
        def go(up):
            xfirst(h, up, t).wait_recv()
            xsecond(h, up, t).start()

        relay(h, t, go)

    def xarrived(h, t):
        @pl.when(me_r > 0)
        def _():
            xcopy(h, True, t).wait_recv()

        @pl.when(me_r < rows - 1)
        def _():
            xcopy(h, False, t).wait_recv()

    def ycopy(h, up, part):
        own, far = ((Y, 0) if up else (W, Y + W))
        return pltpu.make_async_remote_copy(
            src_ref=yb.at[h, :, :, pl.ds(own + 8 * part, 8)],
            dst_ref=yb.at[h, :, :, pl.ds(far + 8 * part, 8)],
            send_sem=sy.at[h, int(up), part],
            recv_sem=ry.at[h, int(up), part],
            device_id={"col": lax.rem(me_c + (1 if up else cols - 1), cols)},
            device_id_type=MESH,
        )

    def yeach(h, up, part, act):
        @pl.when(me_c < cols - 1 if up else me_c > 0)
        def _():
            act(ycopy(h, up, part))

    def ystart(h, t):
        for up in (False, True):
            part = t - (tiles - W // 8 if up else 0)
            if 0 <= part < W // 8:
                yeach(h, up, part, lambda copy: copy.start())

    def yarrived(h):
        for part in range(W // 8):
            @pl.when(me_c > 0)
            def _():
                ycopy(h, True, part).wait_recv()

            @pl.when(me_c < cols - 1)
            def _():
                ycopy(h, False, part).wait_recv()

    def xeach(h, t, act):
        xacross(h, t, act)
        xalong(h, t, act)

    def begin(copy):
        copy.start()

    def xstart(h, t):
        xeach(h, t, begin)

    def zpass(t, h):
        lanes = pl.ds(h * LANES, LANES)
        for f, ref in enumerate((gal, ran)):
            high, low = split(ref[:, pl.ds(t * 8, 8)].reshape(X * 8, Z))
            th = thi[:, lanes]
            val = (dot(high, th) + dot(high, tlo[:, lanes]) + dot(low, th)).reshape(X, 8, LANES)
            if h == 0:
                xb[0, f, pl.ds(W, X), pl.ds(t * 8, 8)] = val
            else:
                yb[1, f, :, pl.ds(W + t * 8, 8)] = val

    for t in range(2):
        fetch(0, t).wait()
        fetch(1, t).wait()
        zpass(t, 0)
        if t == 0:
            pl.semaphore_wait(barrier, rows + cols - 2)
        xstart(0, t)
    for t in range(tiles):
        if t > 1:
            fetch(0, t).wait()
            fetch(1, t).wait()
        zpass(t, 1)
        ystart(1, t)
    for t in range(2, tiles):
        zpass(t, 0)

    for h in range(2):
        @pl.when(me_r == 0)
        def _():
            xb[h, :, 0:W] = jnp.zeros((2, W, Y, LANES), F32)

        @pl.when(me_r == rows - 1)
        def _():
            xb[h, :, X + W:] = jnp.zeros((2, W, Y, LANES), F32)

        @pl.when(me_c == 0)
        def _():
            yb[h, :, :, 0:W] = jnp.zeros((2, X, W, LANES), F32)

        @pl.when(me_c == cols - 1)
        def _():
            yb[h, :, :, Y + W:] = jnp.zeros((2, X, W, LANES), F32)

    for k in (2, 3):
        fetch(k).wait()

    def tstep(i, carry):
        m = cov[i].astype(F32)
        g = (m * gal[i]).reshape(Y // 8, 8, Z).sum(axis=0)
        r = (m * ran[i]).reshape(Y // 8, 8, Z).sum(axis=0)
        return carry[0] + g, carry[1] + r

    zero = jnp.zeros((8, Z), F32)
    tg, tr = lax.fori_loop(0, X, tstep, (zero, zero))
    for f, t in enumerate((tg, tr)):
        trow[me_r, f] = sum(t[:, k * LANES:(k + 1) * LANES] for k in range(Z // LANES))
    row_totals = gather_sum("row", rows, trow, s1, r1)

    acc[...] = jnp.zeros_like(acc)
    groups = X // 2 * tiles // GROUP

    def members(h, first, count):
        for k in range(count):
            i = first + k
            yield (i // tiles, i % tiles) if h == 0 else (i % (X // 2), i // (X // 2))

    def cells(ref, h, first, count=GROUP):
        parts = []
        for lx, t in members(h, first, count):
            at = pl.ds(pl.multiple_of(t * 8, 8), 8), pl.ds(h * LANES, LANES)
            parts += [ref[(2 * lx, *at)], ref[(2 * lx + 1, *at)]]
        return jnp.concatenate(parts, axis=1)

    def onehots(h):
        def step(n, unused):
            p = jnp.where(cells(cov, h, n * GROUP) > 0, cells(pat, h, n * GROUP), -1)
            phi, plo = p >> 5, p & 31

            def rows_of(a, b):
                return jnp.concatenate([a, b], axis=0).astype(BF16)

            def one(v, k):
                return jnp.where(v == k, 1.0, 0.0)

            for k in range(4):
                hit = one(phi, k)
                oh[h, n, pl.ds(16 * k, 16)] = rows_of(hit, hit)
            for k in range(16):
                rh[h, n, pl.ds(16 * k, 16)] = rows_of(one(plo, 2 * k), one(plo, 2 * k + 1))
            return unused

        lax.fori_loop(0, groups, step, 0)

    def add_group(h, n, part=None):
        if part is None:
            at = slice(None)
            c = cells(contrast, h, n * GROUP)
        else:
            at = pl.ds(pl.multiple_of(part * GROUP * LANES, GROUP * LANES), GROUP * LANES)
            c = cells(contrast, h, n * GROUP + part * (GROUP // 2), GROUP // 2)
        hot = oh[h, n, :, at]
        terms = [hot]
        power = c
        for q in range(3):
            high, low = split(power)
            both = jnp.concatenate([high.astype(F32), low.astype(F32)], axis=0).astype(BF16)
            terms.append(jnp.concatenate([both] * 4, axis=0) * hot)
            power = power * c
        acc[...] += lax.dot_general(
            rh[h, n, :, at], jnp.concatenate(terms, axis=0), (((1,), (1,)), ((), ())),
            preferred_element_type=F32,
        )

    def histogram(h, first, last):
        def step(n, unused):
            add_group(h, n)
            return unused

        lax.fori_loop(first, last, step, 0, unroll=min(2, last - first))

    def ypass(h, i):
        both = jnp.concatenate(
            [yb[h, f, pl.ds(i * 4, 4)].reshape(4 * (Y + 2 * W), LANES) for f in range(2)], axis=1
        )
        high, low = split(both)
        kh = kyhi[...]
        return dot(kh, high) + dot(kylo[...], high) + dot(kh, low)

    def xpass(h, t):
        ys = pl.ds(t * 8, 8)
        both = jnp.concatenate(
            [xb[h, f, :, ys].reshape((X + 2 * W) * 8, LANES) for f in range(2)], axis=1
        )
        high, low = split(both)
        kh = kxhi[...]
        return dot(kh, high) + dot(kxlo[...], high) + dot(kh, low)

    def contrast_of(val, m, alpha):
        nbar = alpha * val[:, LANES:]
        return m * ((val[:, :LANES] - nbar) / (nbar * (1.0 + 2.0 * nbar)))

    def yown(i, unused):
        val = ypass(1, i)
        for f in range(2):
            xb[1, f, pl.ds(W + i * 4, 4)] = val[:, f * LANES:(f + 1) * LANES].reshape(4, Y, LANES)
        return unused

    def first_of(t):
        xarrived(0, t)
        val = xpass(0, t)
        for f in range(2):
            yb[0, f, :, pl.ds(W + t * 8, 8)] = val[:, f * LANES:(f + 1) * LANES].reshape(X, 8, LANES)
        ystart(0, t)

    for t in range(2, tiles):
        onehots(t - 2)
        relay_on(0, t - 2)
        xstart(0, t)
    for k in (8, 9):
        fetch(k).wait()
    yarrived(1)
    lax.fori_loop(0, X // 4, yown, 0, unroll=2)
    xstart(1, 0)
    tcol[me_c] = add_up(row_totals, trow, rows)
    col_totals = gather_sum("col", cols, tcol, s2, r2)
    for k in (6, 7, 10):
        fetch(k).wait()
    for t in range(tiles):
        first_of(t)
        relay_on(1, t)
        if t + 1 < tiles:
            if t == 0:
                for k in range(1, tiles):
                    xacross(1, k, begin)
            xalong(1, t + 1, begin)
    tot = add_up(col_totals, tcol, cols)
    alpha = jnp.sum(tot[0], keepdims=True) / jnp.sum(tot[1], keepdims=True)

    def half_of(t, upper):
        ys, lanes = pl.ds(t * 8, 8), pl.ds(LANES, LANES)

        @pl.when(jnp.logical_and(upper == 0, me_r > 0))
        def _():
            xcopy(1, True, t).wait_recv()

        @pl.when(jnp.logical_and(upper == 1, me_r < rows - 1))
        def _():
            xcopy(1, False, t).wait_recv()

        first = upper * W
        both = jnp.concatenate(
            [xb[1, f, pl.ds(first, 3 * W), ys].reshape(3 * W * 8, LANES) for f in range(2)], axis=1
        )
        high, low = split(both)
        kh, kl = kxhi[0:W * 8, 0:3 * W * 8], kxlo[0:W * 8, 0:3 * W * 8]
        val = dot(kh, high) + dot(kl, high) + dot(kh, low)
        m = cov[pl.ds(first, W), ys, lanes].astype(F32).reshape(W * 8, LANES)
        contrast[pl.ds(first, W), ys, lanes] = contrast_of(val, m, alpha).reshape(W, 8, LANES)
        add_group(1, t, upper)

    def last_of(h, t):
        lanes = pl.ds(h * LANES, LANES)
        xarrived(h, t)
        val = xpass(h, t)
        m = cov[:, pl.ds(t * 8, 8), lanes].astype(F32).reshape(X * 8, LANES)
        contrast[:, pl.ds(t * 8, 8), lanes] = contrast_of(val, m, alpha).reshape(X, 8, LANES)
        histogram(h, groups * t // tiles, groups * (t + 1) // tiles)

    def cstep(i, unused):
        val = ypass(0, i)
        x4, lanes = pl.ds(i * 4, 4), pl.ds(0, LANES)
        m = cov[x4, :, lanes].astype(F32).reshape(4 * Y, LANES)
        contrast[x4, :, lanes] = contrast_of(val, m, alpha).reshape(4, Y, LANES)
        return unused

    early = lax.rem(me_r, 2)
    late = 1 - early
    last_of(1, 0)
    yarrived(0)
    lax.fori_loop(0, X // 4, cstep, 0, unroll=2)
    histogram(0, 0, groups)
    last_of(1, 1)
    half_of(2, early)
    half_of(3, early)
    half_of(2, late)
    half_of(3, late)

    a = acc[...]
    same = lax.broadcasted_iota(jnp.int32, a.shape, 0) % 8 == lax.broadcasted_iota(jnp.int32, a.shape, 1) % 8
    a = jnp.where(same, a, 0.0).reshape(32, 8, 256).sum(axis=1).T
    terms = []
    for q in range(4):
        for k in range(4):
            at = q * 64 + k * 16
            term = a[at:at + 8] if q == 0 else a[at:at + 8] + a[at + 8:at + 16]
            terms.append(jnp.sum(term, axis=0, keepdims=True))
    mine = jnp.concatenate(
        [jnp.concatenate([terms[4 * q + k] for q in range(4)] + [jnp.zeros((4, 32), F32)], axis=0) for k in range(4)],
        axis=1,
    )
    def drain():
        for h in range(2):
            for t in range(tiles):
                xeach(h, t, lambda copy: copy.wait_send())
                relay(h, t, lambda up: xsecond(h, up, t).wait_send())
            for up in (False, True):
                for part in range(W // 8):
                    yeach(h, up, part, lambda copy: copy.wait_send())

    if rows * cols <= DIRECT:
        me = me_r * cols + me_c
        sall[me] = mine
        copies = []
        for k, (kr, kc) in enumerate(shifts(rows, cols)):
            copy = pltpu.make_async_remote_copy(
                src_ref=sall.at[me, pl.ds(0, 4)],
                dst_ref=sall.at[me, pl.ds(0, 4)],
                send_sem=s3.at[k],
                recv_sem=r3.at[k],
                device_id={"row": lax.rem(me_r + kr, rows), "col": lax.rem(me_c + kc, cols)},
                device_id_type=MESH,
            )
            copy.start()
            copies.append(copy)
        drain()
        for copy in copies:
            copy.wait_send()
        for copy in copies:
            copy.wait_recv()
        sums[...] = jnp.sum(sall[:, 0:4], axis=0) * scale
    else:
        drain()
        sall[me_r] = mine
        scol[me_c] = add_up(gather_sum("row", rows, sall, s3, r3), sall, rows)
        whole = add_up(gather_sum("col", cols, scol, s4, r4), scol, cols)
        sums[...] = whole[0:4] * scale


def store(contrast, sums, contrast_out, sums_out, sem):
    step = contrast.shape[0] // 1
    copies = [pltpu.make_async_copy(contrast.at[pl.ds(k * step, step)], contrast_out.at[pl.ds(k * step, step)], sem.at[k]) for k in range(1)]
    copies.append(pltpu.make_async_copy(sums, sums_out, sem.at[1]))
    for copy in copies:
        copy.start()
    for copy in copies:
        copy.wait()


def local(galaxy, randoms, coverage, patch):
    rows, cols = lax.axis_size("row"), lax.axis_size("col")
    X, Y, Z = galaxy.shape
    W = RADIUS
    tiles = Y // 8
    groups = X // 2 * tiles // GROUP
    direct = (rows * cols if rows * cols <= DIRECT else rows) - 1
    scale = NPATCH / (X * rows * Y * cols * Z)
    tz = split_np(band(Z, Z, 0).T)
    kx = split_np(np.kron(band(X, X + 2 * W, W), np.eye(8, dtype=np.float32)))
    ky = split_np(np.kron(np.eye(4, dtype=np.float32), band(Y, Y + 2 * W, W)))
    rep = (np.arange(NPATCH)[None, :] % 32 == np.arange(32)[:, None]).astype(np.float32)
    consts = [jnp.asarray(v) for v in (*tz, *kx, *ky, rep)]
    args = (galaxy, randoms, coverage, patch, *consts)
    vmem = pl.BlockSpec(memory_space=pltpu.VMEM)
    dma = pltpu.SemaphoreType.DMA
    contrast, sums = pl.pallas_call(
        functools.partial(kernel, rows, cols, scale),
        out_shape=(
            pltpu.VMEM((X, Y, Z), F32),
            pltpu.VMEM((4, NPATCH), F32),
        ),
        in_specs=[pl.BlockSpec(memory_space=pl.ANY)] * 11,
        out_specs=(vmem, vmem),
        scratch_shapes=[pltpu.VMEM(v.shape, v.dtype) for v in args] + [
            pltpu.VMEM((2, 2, X + 2 * W, Y, LANES), F32),
            pltpu.VMEM((2, 2, X, Y + 2 * W, LANES), F32),
            pltpu.VMEM((256, 256), F32),
            pltpu.VMEM((rows, 2, 8, LANES), F32),
            pltpu.VMEM((cols, 2, 8, LANES), F32),
            pltpu.VMEM((direct + 1, 8, NPATCH), F32),
            pltpu.VMEM((cols, 8, NPATCH), F32),
            pltpu.VMEM((2, tiles // 2, 2, W, 8, LANES), F32),
            pltpu.VMEM((2, groups, 64, 2 * LANES * GROUP), BF16),
            pltpu.VMEM((2, groups, 256, 2 * LANES * GROUP), BF16),
            dma((11, tiles)),
            dma((2, 2, tiles)), dma((2, 2, tiles)), dma((2, 2, W // 8)), dma((2, 2, W // 8)),
            dma((2, tiles // 2)), dma((2, tiles // 2)),
            dma((rows - 1,)), dma((rows - 1,)), dma((cols - 1,)), dma((cols - 1,)),
            dma((direct,)), dma((direct,)), dma((cols - 1,)), dma((cols - 1,)),
        ],
        compiler_params=pltpu.CompilerParams(
            collective_id=0, has_side_effects=True, vmem_limit_bytes=56 * 1024 * 1024
        ),
    )(*args)
    return pl.pallas_call(
        store,
        out_shape=(
            jax.ShapeDtypeStruct((X, Y, Z), F32),
            jax.ShapeDtypeStruct((4, NPATCH), F32),
        ),
        in_specs=[pl.BlockSpec(memory_space=pl.ANY)] * 2,
        out_specs=(pl.BlockSpec(memory_space=pl.ANY),) * 2,
        scratch_shapes=[dma((1 + 1,))],
    )(*(pltpu.with_memory_space_constraint(v, pltpu.VMEM) for v in (contrast, sums)))


def solution(mesh):
    spec = P("row", "col", None)
    return jax.shard_map(
        local, mesh=mesh, in_specs=(spec,) * 4, out_specs=(spec, P()), check_vma=False
    )
```

```python
import functools

import jax
import jax.numpy as jnp
import ml_dtypes
import numpy as np
from jax import lax
from jax.experimental import pallas as pl
from jax.experimental.pallas import tpu as pltpu
from jax.sharding import PartitionSpec as P

RADIUS = 16
NPATCH = 128
LANES = 128
GROUP = 16
DIRECT = 32
F32 = jnp.float32
BF16 = jnp.bfloat16
MESH = pl.DeviceIdType.MESH


def taps_np():
    offs = np.arange(-RADIUS, RADIUS + 1).astype(np.float32)
    sigma = RADIUS / 2.0
    vals = np.exp(-offs * offs / np.float32(2.0 * sigma * sigma)).astype(np.float32)
    return (vals / vals.sum(dtype=np.float32)).astype(np.float32)


def split_np(mat):
    high = mat.astype(ml_dtypes.bfloat16)
    low = (mat - high.astype(np.float32)).astype(ml_dtypes.bfloat16)
    return high, low


def band(outs, ins, shift):
    taps = taps_np()
    mat = np.zeros((outs, ins), np.float32)
    for o in range(outs):
        for j in range(-RADIUS, RADIUS + 1):
            i = o + j + shift
            if 0 <= i < ins:
                mat[o, i] = taps[j + RADIUS]
    return mat


def split(val):
    high = val.astype(BF16)
    low = (val - high.astype(F32)).astype(BF16)
    return high, low


def dot(a, b):
    return jnp.dot(a, b, preferred_element_type=F32)


def gather_sum(axis, size, buf, send, recv):
    me = lax.axis_index(axis)
    copies = []
    for k in range(1, size):
        copy = pltpu.make_async_remote_copy(
            src_ref=buf.at[me],
            dst_ref=buf.at[me],
            send_sem=send.at[k - 1],
            recv_sem=recv.at[k - 1],
            device_id={axis: lax.rem(me + k, size)},
            device_id_type=MESH,
        )
        copy.start()
        copies.append(copy)
    return copies


def add_up(copies, buf, size):
    for copy in copies:
        copy.wait()
    total = buf[0]
    for k in range(1, size):
        total = total + buf[k]
    return total


def shifts(rows, cols):
    pairs = [(r, c) for r in range(rows) for c in range(cols) if (r, c) != (0, 0)]
    return sorted(pairs, key=lambda rc: -(min(rc[0], 1) + min(rc[1], cols - rc[1])))


def kernel(
    rows, cols, scale,
    *refs,
):
    hbm, (contrast, sums), vmem = refs[:11], refs[11:13], refs[13:24]
    (
        xb, yb, acc, trow, tcol, sall, scol, rb, oh, rh, sin,
        sx, rx, sy, ry, srel, rrel, s1, r1, s2, r2, s3, r3, s4, r4,
    ) = refs[24:]
    gal, ran, cov, pat, thi, tlo, kxhi, kxlo, kyhi, kylo, rep = vmem
    X, Y, Z = gal.shape
    W = RADIUS
    tiles = Y // 8
    me_r = lax.axis_index("row")
    me_c = lax.axis_index("col")

    def fetch(k, t=None):
        at = slice(None) if t is None else (slice(None), pl.ds(t * 8, 8))
        return pltpu.make_async_copy(hbm[k].at[at], vmem[k].at[at], sin.at[k, t or 0])

    barrier = pltpu.get_barrier_semaphore()
    for k in range(1, rows):
        pl.semaphore_signal(barrier, inc=1, device_id={"row": lax.rem(me_r + k, rows)}, device_id_type=MESH)
    for k in range(1, cols):
        pl.semaphore_signal(barrier, inc=1, device_id={"col": lax.rem(me_c + k, cols)}, device_id_type=MESH)

    fetch(0, 0).start()
    fetch(1, 0).start()
    fetch(4).start()
    fetch(5).start()
    for t in range(1, tiles):
        fetch(0, t).start()
        fetch(1, t).start()
    for k in (2, 3, 8, 9, 6, 7, 10):
        fetch(k).start()
    fetch(4).wait()
    fetch(5).wait()

    relayed = rows == 4
    detour = tiles // 2 if relayed else 0

    def xsrc(h, up, t):
        return xb.at[h, :, pl.ds(X if up else W, W), pl.ds(t * 8, 8)]

    def xdst(h, up, t):
        return xb.at[h, :, pl.ds(0 if up else X + W, W), pl.ds(t * 8, 8)]

    def xsend(src, dst, ssem, rsem, hop):
        return pltpu.make_async_remote_copy(
            src_ref=src, dst_ref=dst, send_sem=ssem, recv_sem=rsem,
            device_id={"row": lax.rem(me_r + (hop + rows), rows)}, device_id_type=MESH,
        )

    def xcopy(h, up, t):
        u = int(up)
        return xsend(xsrc(h, up, t), xdst(h, up, t), sx.at[h, u, t], rx.at[h, u, t], 1 if up else -1)

    def xfirst(h, up, t):
        return xsend(xsrc(h, up, t), rb.at[h, t], sx.at[h, int(up), t], rrel.at[h, t], 2 if up else -2)

    def xsecond(h, up, t):
        return xsend(rb.at[h, t], xdst(h, up, t), srel.at[h, t], rx.at[h, int(up), t], -1 if up else 1)

    def xacross(h, t, act):
        for up in (False, True):
            if relayed:
                @pl.when(me_r == (1 if up else 2))
                def _():
                    act((xfirst if t < detour else xcopy)(h, up, t))

    def xalong(h, t, act):
        for up in (False, True):
            has = me_r < rows - 1 if up else me_r > 0
            if relayed:
                has = jnp.logical_and(has, me_r != (1 if up else 2))

            @pl.when(has)
            def _():
                act(xcopy(h, up, t))

    def relay(h, t, act):
        if t < detour:
            for up in (False, True):
                @pl.when(me_r == (3 if up else 0))
                def _():
                    act(up)

    def relay_on(h, t):
        def go(up):
            xfirst(h, up, t).wait_recv()
            xsecond(h, up, t).start()

        relay(h, t, go)

    def xarrived(h, t):
        @pl.when(me_r > 0)
        def _():
            xcopy(h, True, t).wait_recv()

        @pl.when(me_r < rows - 1)
        def _():
            xcopy(h, False, t).wait_recv()

    def ycopy(h, up, part):
        own, far = ((Y, 0) if up else (W, Y + W))
        return pltpu.make_async_remote_copy(
            src_ref=yb.at[h, :, :, pl.ds(own + 8 * part, 8)],
            dst_ref=yb.at[h, :, :, pl.ds(far + 8 * part, 8)],
            send_sem=sy.at[h, int(up), part],
            recv_sem=ry.at[h, int(up), part],
            device_id={"col": lax.rem(me_c + (1 if up else cols - 1), cols)},
            device_id_type=MESH,
        )

    def yeach(h, up, part, act):
        @pl.when(me_c < cols - 1 if up else me_c > 0)
        def _():
            act(ycopy(h, up, part))

    def ystart(h, t):
        for up in (False, True):
            part = t - (tiles - W // 8 if up else 0)
            if 0 <= part < W // 8:
                yeach(h, up, part, lambda copy: copy.start())

    def yarrived(h):
        for part in range(W // 8):
            @pl.when(me_c > 0)
            def _():
                ycopy(h, True, part).wait_recv()

            @pl.when(me_c < cols - 1)
            def _():
                ycopy(h, False, part).wait_recv()

    def xeach(h, t, act):
        xacross(h, t, act)
        xalong(h, t, act)

    def begin(copy):
        copy.start()

    def xstart(h, t):
        xeach(h, t, begin)

    def zpass(t, h):
        lanes = pl.ds(h * LANES, LANES)
        for f, ref in enumerate((gal, ran)):
            high, low = split(ref[:, pl.ds(t * 8, 8)].reshape(X * 8, Z))
            th = thi[:, lanes]
            val = (dot(high, th) + dot(high, tlo[:, lanes]) + dot(low, th)).reshape(X, 8, LANES)
            if h == 0:
                xb[0, f, pl.ds(W, X), pl.ds(t * 8, 8)] = val
            else:
                yb[1, f, :, pl.ds(W + t * 8, 8)] = val

    for t in range(2):
        fetch(0, t).wait()
        fetch(1, t).wait()
        zpass(t, 0)
        if t == 0:
            pl.semaphore_wait(barrier, rows + cols - 2)
        xstart(0, t)
    for t in range(tiles):
        if t > 1:
            fetch(0, t).wait()
            fetch(1, t).wait()
        zpass(t, 1)
        ystart(1, t)
    for t in range(2, tiles):
        zpass(t, 0)

    for h in range(2):
        @pl.when(me_r == 0)
        def _():
            xb[h, :, 0:W] = jnp.zeros((2, W, Y, LANES), F32)

        @pl.when(me_r == rows - 1)
        def _():
            xb[h, :, X + W:] = jnp.zeros((2, W, Y, LANES), F32)

        @pl.when(me_c == 0)
        def _():
            yb[h, :, :, 0:W] = jnp.zeros((2, X, W, LANES), F32)

        @pl.when(me_c == cols - 1)
        def _():
            yb[h, :, :, Y + W:] = jnp.zeros((2, X, W, LANES), F32)

    for t in range(2, tiles):
        xacross(0, t, begin)
    for k in (2, 3):
        fetch(k).wait()

    def tstep(i, carry):
        m = cov[i].astype(F32)
        g = (m * gal[i]).reshape(Y // 8, 8, Z).sum(axis=0)
        r = (m * ran[i]).reshape(Y // 8, 8, Z).sum(axis=0)
        return carry[0] + g, carry[1] + r

    zero = jnp.zeros((8, Z), F32)
    tg, tr = lax.fori_loop(0, X, tstep, (zero, zero))
    for f, t in enumerate((tg, tr)):
        trow[me_r, f] = sum(t[:, k * LANES:(k + 1) * LANES] for k in range(Z // LANES))
    row_totals = gather_sum("row", rows, trow, s1, r1)

    acc[...] = jnp.zeros_like(acc)
    groups = X // 2 * tiles // GROUP

    def members(h, first, count):
        for k in range(count):
            i = first + k
            yield (i // tiles, i % tiles) if h == 0 else (i % (X // 2), i // (X // 2))

    def cells(ref, h, first, count=GROUP):
        parts = []
        for lx, t in members(h, first, count):
            at = pl.ds(pl.multiple_of(t * 8, 8), 8), pl.ds(h * LANES, LANES)
            parts += [ref[(2 * lx, *at)], ref[(2 * lx + 1, *at)]]
        return jnp.concatenate(parts, axis=1)

    def onehots(h):
        def step(n, unused):
            p = jnp.where(cells(cov, h, n * GROUP) > 0, cells(pat, h, n * GROUP), -1)
            phi, plo = p >> 5, p & 31

            def rows_of(a, b):
                return jnp.concatenate([a, b], axis=0).astype(BF16)

            def one(v, k):
                return jnp.where(v == k, 1.0, 0.0)

            for k in range(4):
                hit = one(phi, k)
                oh[h, n, pl.ds(16 * k, 16)] = rows_of(hit, hit)
            for k in range(16):
                rh[h, n, pl.ds(16 * k, 16)] = rows_of(one(plo, 2 * k), one(plo, 2 * k + 1))
            return unused

        lax.fori_loop(0, groups, step, 0)

    def add_group(h, n, part=None):
        if part is None:
            at = slice(None)
            c = cells(contrast, h, n * GROUP)
        else:
            at = pl.ds(pl.multiple_of(part * GROUP * LANES, GROUP * LANES), GROUP * LANES)
            c = cells(contrast, h, n * GROUP + part * (GROUP // 2), GROUP // 2)
        hot = oh[h, n, :, at]
        terms = [hot]
        power = c
        for q in range(3):
            high, low = split(power)
            both = jnp.concatenate([high.astype(F32), low.astype(F32)], axis=0).astype(BF16)
            terms.append(jnp.concatenate([both] * 4, axis=0) * hot)
            power = power * c
        acc[...] += lax.dot_general(
            rh[h, n, :, at], jnp.concatenate(terms, axis=0), (((1,), (1,)), ((), ())),
            preferred_element_type=F32,
        )

    def histogram(h, first, last):
        def step(n, unused):
            add_group(h, n)
            return unused

        lax.fori_loop(first, last, step, 0, unroll=min(2, last - first))

    def ypass(h, i):
        both = jnp.concatenate(
            [yb[h, f, pl.ds(i * 4, 4)].reshape(4 * (Y + 2 * W), LANES) for f in range(2)], axis=1
        )
        high, low = split(both)
        kh = kyhi[...]
        return dot(kh, high) + dot(kylo[...], high) + dot(kh, low)

    def xpass(h, t):
        ys = pl.ds(t * 8, 8)
        both = jnp.concatenate(
            [xb[h, f, :, ys].reshape((X + 2 * W) * 8, LANES) for f in range(2)], axis=1
        )
        high, low = split(both)
        kh = kxhi[...]
        return dot(kh, high) + dot(kxlo[...], high) + dot(kh, low)

    def contrast_of(val, m, alpha):
        nbar = alpha * val[:, LANES:]
        return m * ((val[:, :LANES] - nbar) / (nbar * (1.0 + 2.0 * nbar)))

    def yown(i, unused):
        val = ypass(1, i)
        for f in range(2):
            xb[1, f, pl.ds(W + i * 4, 4)] = val[:, f * LANES:(f + 1) * LANES].reshape(4, Y, LANES)
        return unused

    def first_of(t):
        xarrived(0, t)
        val = xpass(0, t)
        for f in range(2):
            yb[0, f, :, pl.ds(W + t * 8, 8)] = val[:, f * LANES:(f + 1) * LANES].reshape(X, 8, LANES)
        ystart(0, t)

    for t in range(2, tiles):
        onehots(t - 2)
        relay_on(0, t - 2)
        xalong(0, t, begin)
    for k in (8, 9):
        fetch(k).wait()
    yarrived(1)
    lax.fori_loop(0, X // 4, yown, 0, unroll=2)
    xstart(1, 0)
    tcol[me_c] = add_up(row_totals, trow, rows)
    col_totals = gather_sum("col", cols, tcol, s2, r2)
    for k in (6, 7, 10):
        fetch(k).wait()
    for t in range(tiles):
        first_of(t)
        relay_on(1, t)
        if t + 1 < tiles:
            if t == 0:
                for k in range(1, tiles):
                    xacross(1, k, begin)
            xalong(1, t + 1, begin)
    tot = add_up(col_totals, tcol, cols)
    alpha = jnp.sum(tot[0], keepdims=True) / jnp.sum(tot[1], keepdims=True)

    def half_of(t, upper):
        ys, lanes = pl.ds(t * 8, 8), pl.ds(LANES, LANES)

        @pl.when(jnp.logical_and(upper == 0, me_r > 0))
        def _():
            xcopy(1, True, t).wait_recv()

        @pl.when(jnp.logical_and(upper == 1, me_r < rows - 1))
        def _():
            xcopy(1, False, t).wait_recv()

        first = upper * W
        both = jnp.concatenate(
            [xb[1, f, pl.ds(first, 3 * W), ys].reshape(3 * W * 8, LANES) for f in range(2)], axis=1
        )
        high, low = split(both)
        kh, kl = kxhi[0:W * 8, 0:3 * W * 8], kxlo[0:W * 8, 0:3 * W * 8]
        val = dot(kh, high) + dot(kl, high) + dot(kh, low)
        m = cov[pl.ds(first, W), ys, lanes].astype(F32).reshape(W * 8, LANES)
        contrast[pl.ds(first, W), ys, lanes] = contrast_of(val, m, alpha).reshape(W, 8, LANES)
        add_group(1, t, upper)

    def last_of(h, t):
        lanes = pl.ds(h * LANES, LANES)
        xarrived(h, t)
        val = xpass(h, t)
        m = cov[:, pl.ds(t * 8, 8), lanes].astype(F32).reshape(X * 8, LANES)
        contrast[:, pl.ds(t * 8, 8), lanes] = contrast_of(val, m, alpha).reshape(X, 8, LANES)
        histogram(h, groups * t // tiles, groups * (t + 1) // tiles)

    def cstep(i, unused):
        val = ypass(0, i)
        x4, lanes = pl.ds(i * 4, 4), pl.ds(0, LANES)
        m = cov[x4, :, lanes].astype(F32).reshape(4 * Y, LANES)
        contrast[x4, :, lanes] = contrast_of(val, m, alpha).reshape(4, Y, LANES)
        return unused

    early = lax.rem(me_r, 2)
    late = 1 - early
    last_of(1, 0)
    yarrived(0)
    lax.fori_loop(0, X // 4, cstep, 0, unroll=2)
    histogram(0, 0, groups)
    last_of(1, 1)
    half_of(2, early)
    half_of(3, early)
    half_of(2, late)
    half_of(3, late)

    a = acc[...]
    same = lax.broadcasted_iota(jnp.int32, a.shape, 0) % 8 == lax.broadcasted_iota(jnp.int32, a.shape, 1) % 8
    a = jnp.where(same, a, 0.0).reshape(32, 8, 256).sum(axis=1).T
    terms = []
    for q in range(4):
        for k in range(4):
            at = q * 64 + k * 16
            term = a[at:at + 8] if q == 0 else a[at:at + 8] + a[at + 8:at + 16]
            terms.append(jnp.sum(term, axis=0, keepdims=True))
    mine = jnp.concatenate(
        [jnp.concatenate([terms[4 * q + k] for q in range(4)] + [jnp.zeros((4, 32), F32)], axis=0) for k in range(4)],
        axis=1,
    )
    def drain():
        for h in range(2):
            for t in range(tiles):
                xeach(h, t, lambda copy: copy.wait_send())
                relay(h, t, lambda up: xsecond(h, up, t).wait_send())
            for up in (False, True):
                for part in range(W // 8):
                    yeach(h, up, part, lambda copy: copy.wait_send())

    if rows * cols <= DIRECT:
        me = me_r * cols + me_c
        sall[me] = mine
        copies = []
        for k, (kr, kc) in enumerate(shifts(rows, cols)):
            copy = pltpu.make_async_remote_copy(
                src_ref=sall.at[me, pl.ds(0, 4)],
                dst_ref=sall.at[me, pl.ds(0, 4)],
                send_sem=s3.at[k],
                recv_sem=r3.at[k],
                device_id={"row": lax.rem(me_r + kr, rows), "col": lax.rem(me_c + kc, cols)},
                device_id_type=MESH,
            )
            copy.start()
            copies.append(copy)
        drain()
        for copy in copies:
            copy.wait_send()
        for copy in copies:
            copy.wait_recv()
        sums[...] = jnp.sum(sall[:, 0:4], axis=0) * scale
    else:
        drain()
        sall[me_r] = mine
        scol[me_c] = add_up(gather_sum("row", rows, sall, s3, r3), sall, rows)
        whole = add_up(gather_sum("col", cols, scol, s4, r4), scol, cols)
        sums[...] = whole[0:4] * scale


def store(contrast, sums, contrast_out, sums_out, sem):
    step = contrast.shape[0] // 1
    copies = [pltpu.make_async_copy(contrast.at[pl.ds(k * step, step)], contrast_out.at[pl.ds(k * step, step)], sem.at[k]) for k in range(1)]
    copies.append(pltpu.make_async_copy(sums, sums_out, sem.at[1]))
    for copy in copies:
        copy.start()
    for copy in copies:
        copy.wait()


def local(galaxy, randoms, coverage, patch):
    rows, cols = lax.axis_size("row"), lax.axis_size("col")
    X, Y, Z = galaxy.shape
    W = RADIUS
    tiles = Y // 8
    groups = X // 2 * tiles // GROUP
    direct = (rows * cols if rows * cols <= DIRECT else rows) - 1
    scale = NPATCH / (X * rows * Y * cols * Z)
    tz = split_np(band(Z, Z, 0).T)
    kx = split_np(np.kron(band(X, X + 2 * W, W), np.eye(8, dtype=np.float32)))
    ky = split_np(np.kron(np.eye(4, dtype=np.float32), band(Y, Y + 2 * W, W)))
    rep = (np.arange(NPATCH)[None, :] % 32 == np.arange(32)[:, None]).astype(np.float32)
    consts = [jnp.asarray(v) for v in (*tz, *kx, *ky, rep)]
    args = (galaxy, randoms, coverage, patch, *consts)
    vmem = pl.BlockSpec(memory_space=pltpu.VMEM)
    dma = pltpu.SemaphoreType.DMA
    contrast, sums = pl.pallas_call(
        functools.partial(kernel, rows, cols, scale),
        out_shape=(
            pltpu.VMEM((X, Y, Z), F32),
            pltpu.VMEM((4, NPATCH), F32),
        ),
        in_specs=[pl.BlockSpec(memory_space=pl.ANY)] * 11,
        out_specs=(vmem, vmem),
        scratch_shapes=[pltpu.VMEM(v.shape, v.dtype) for v in args] + [
            pltpu.VMEM((2, 2, X + 2 * W, Y, LANES), F32),
            pltpu.VMEM((2, 2, X, Y + 2 * W, LANES), F32),
            pltpu.VMEM((256, 256), F32),
            pltpu.VMEM((rows, 2, 8, LANES), F32),
            pltpu.VMEM((cols, 2, 8, LANES), F32),
            pltpu.VMEM((direct + 1, 8, NPATCH), F32),
            pltpu.VMEM((cols, 8, NPATCH), F32),
            pltpu.VMEM((2, tiles // 2, 2, W, 8, LANES), F32),
            pltpu.VMEM((2, groups, 64, 2 * LANES * GROUP), BF16),
            pltpu.VMEM((2, groups, 256, 2 * LANES * GROUP), BF16),
            dma((11, tiles)),
            dma((2, 2, tiles)), dma((2, 2, tiles)), dma((2, 2, W // 8)), dma((2, 2, W // 8)),
            dma((2, tiles // 2)), dma((2, tiles // 2)),
            dma((rows - 1,)), dma((rows - 1,)), dma((cols - 1,)), dma((cols - 1,)),
            dma((direct,)), dma((direct,)), dma((cols - 1,)), dma((cols - 1,)),
        ],
        compiler_params=pltpu.CompilerParams(
            collective_id=0, has_side_effects=True, vmem_limit_bytes=56 * 1024 * 1024
        ),
    )(*args)
    return pl.pallas_call(
        store,
        out_shape=(
            jax.ShapeDtypeStruct((X, Y, Z), F32),
            jax.ShapeDtypeStruct((4, NPATCH), F32),
        ),
        in_specs=[pl.BlockSpec(memory_space=pl.ANY)] * 2,
        out_specs=(pl.BlockSpec(memory_space=pl.ANY),) * 2,
        scratch_shapes=[dma((1 + 1,))],
    )(*(pltpu.with_memory_space_constraint(v, pltpu.VMEM) for v in (contrast, sums)))


def solution(mesh):
    spec = P("row", "col", None)
    return jax.shard_map(
        local, mesh=mesh, in_specs=(spec,) * 4, out_specs=(spec, P()), check_vma=False
    )
```
